32 devices in a mesh: dp: 4 (over y, x), seq: 8 (over z, core).
Axes of the slice: x: 2, y: 2, z: 4, core: 2. Of those that a mesh axis runs over, the one named last changes fastest.
Arguments:
- inputs: bfloat16 [8, 1024, 768], P('dp', 'seq'), may hold values from -6 to 6
- memory: bfloat16 [8, 1024, 768], P('dp', 'seq'), may hold values from -6 to 6
- cotangent: bfloat16 [8, 1024, 768], P('dp', 'seq'), may hold values from -6 to 6
- segment_ids: int32 [8, 1024], P('dp', 'seq'), may hold values from 0 to 3, never falling along the last dimension, each value on 1 to 512 neighbouring positions
- row_live: int32 [8], P('dp'), may hold values 0 or 1
- buckets: int32 [1024], replicated, may hold values from 0 to 31, as said below
- gain_self: bfloat16 [768], P('dp'), may hold values from 0.5 to 1.5
- w_qkv: bfloat16 [768, 2304], P('dp'), may hold values from -0.21875 to 0.21875
- w_attn_out: bfloat16 [768, 768], P('dp'), may hold values from -2 to 2
- rel_bias: bfloat16 [32, 12], P('dp'), may hold values from -4 to 4
- gain_cross: bfloat16 [768], P('dp'), may hold values from 0.5 to 1.5
- c_query: bfloat16 [768, 768], P('dp'), may hold values from -0.21875 to 0.21875
- c_keyval: bfloat16 [768, 1536], P('dp'), may hold values from -0.21875 to 0.21875
- c_out: bfloat16 [768, 768], P('dp'), may hold values from -2 to 2
- gain_ff: bfloat16 [768], P('dp'), may hold values from 0.5 to 1.5
- w_gate_up: bfloat16 [768, 4096], P('dp'), may hold values from -0.21875 to 0.21875
- w_down: bfloat16 [2048, 768], P('dp'), may hold values from -0.125 to 0.125
Outputs:
- output: bfloat16 [8, 1024, 768], P('dp', 'seq')
- grad_inputs: bfloat16 [8, 1024, 768], P('dp', 'seq')
- grad_memory: bfloat16 [8, 1024, 768], P('dp', 'seq')
- grad_gain_self: float32 [768], P('dp')
- grad_w_qkv: float32 [768, 2304], P('dp')
- grad_w_attn_out: float32 [768, 768], P('dp')
- grad_rel_bias: float32 [32, 12], P('dp')
- grad_gain_cross: float32 [768], P('dp')
- grad_c_query: float32 [768, 768], P('dp')
- grad_c_keyval: float32 [768, 1536], P('dp')
- grad_c_out: float32 [768, 768], P('dp')
- grad_gain_ff: float32 [768], P('dp')
- grad_w_gate_up: float32 [768, 4096], P('dp')
- grad_w_down: float32 [2048, 768], P('dp')
The draws below stay inside these ranges and needn't reach their ends.
Inputs may be any that keep to these rules, and one draw needn't show every extreme that they name: `segment_ids`: along each row the segment ids never fall; every row holds all 4 segments. buckets[d] never falls as the distance d grows, is 0 at d = 0 and reaches 31.
All inputs are finite; a program needn't handle non-finite values. No bound on the sum of `row_live` on one device may be relied on, other than what follows from the above.
Results may differ from the reference program's by a relative error of at most 0.029.
Values may be sent and summed in bfloat16 or wider, within the bound.
A program may use at most 192 MiB of HBM per device.

```python
import math
import jax
import jax.numpy as jnp
import numpy as np
from jax import lax

D = 768
HEADS = 12
HEAD_DIM = 64
FF = 2048
BUCKETS = 32
LEN = 1024
MEM = 1024
ROWS = 8


def draw_buckets(key, part):
    order = jax.random.permutation(key, LEN - 1) + 1
    edges = order[:BUCKETS - 1].astype(jnp.int32)
    distance = jnp.arange(LEN, dtype=jnp.int32)
    return jnp.sum((edges[None, :] <= distance[:, None]).astype(jnp.int32), axis=1).astype(jnp.int32)


def place_ends(values, own_key, low, largest):
    longest = values.shape.index(max(values.shape))
    spots = []
    for shift in (0, 1):
        where = [jax.random.randint(jax.random.fold_in(own_key, axis), (), 0, length) for axis, length in enumerate(values.shape)]
        where[longest] = (where[longest] + shift) % values.shape[longest]
        spots.append(tuple(where))
    return values.at[spots[0]].set(low).at[spots[1]].set(largest)


def steps_of(key, dims, cuts, smallest, top_value):
    def one(axis_at, shards_of):
        draws = jax.random.uniform(jax.random.fold_in(jax.random.fold_in(key, 6), axis_at), (shards_of,), jnp.float32, smallest / len(cuts), top_value / len(cuts))
        return jnp.repeat(jnp.exp(draws), dims[axis_at] // shards_of).reshape((-1,) + (1,) * (len(dims) - axis_at - 1))

    factor_of = one(*cuts[0])
    for cut in cuts[1:]:
        factor_of = factor_of * one(*cut)
    return factor_of


def profile(number_of, total, reach, skew):
    loads = [(1 << 20) // math.isqrt(grade ** skew) + 1 for grade in range(2, number_of + 1)]
    rest, holding = total - reach - (number_of - 1), [1] * (number_of - 1)
    while rest > 0:
        free = [i for i in range(number_of - 1) if holding[i] < reach]
        pool, left = sum([loads[i] for i in free]), rest
        for i in free:
            extra = min(reach - holding[i], max(1, left * loads[i] // pool), rest)
            holding[i] = holding[i] + extra
            rest = rest - extra
    return np.array([reach] + holding)


def ragged_sizes(own_key, amount, total, reach, skew):
    if amount == 2:
        one = jax.random.randint(own_key, (), max(1, total - reach), min(reach, total - 1) + 1)
        return jnp.stack([one, total - one])
    sizes = jnp.asarray(profile(amount, total, reach, skew), jnp.int32)
    pairs = (amount - 1) // 2
    donor, receiver = sizes[1:1 + 2 * pairs:2], sizes[2:2 + 2 * pairs:2]
    slack = jnp.minimum(donor - 1, reach - receiver)
    moved = jax.random.randint(jax.random.fold_in(own_key, 1), (pairs,), 0, 1 << 20) % (slack + 1)
    sizes = sizes.at[1:1 + 2 * pairs:2].set(donor - moved).at[2:2 + 2 * pairs:2].set(receiver + moved)
    return sizes[jax.random.permutation(jax.random.fold_in(own_key, 2), amount)]


def normal_values(key, extent, spread, most, split=(), kind=jnp.bfloat16):
    array = spread * jax.random.normal(key, extent, jnp.float32)
    if split:
        array = array * steps_of(key, extent, split, -0.22, 0.18)
    return jnp.clip(array, -most, most).astype(kind)


def setup_inputs(seed: int = 0) -> dict:
    splits = jax.random.split(jax.random.key(seed), 18)
    inputs = normal_values(splits[0], (ROWS, LEN, D), 1.0, 6.0, ((0, 4), (1, 8)))
    memory = normal_values(splits[1], (ROWS, MEM, D), 1.0, 6.0, ((0, 4), (1, 8)))
    cotangent = normal_values(splits[2], (ROWS, LEN, D), 1.0, 6.0, ((0, 4), (1, 8)))
    segment_ids = jax.vmap(lambda own: jnp.searchsorted(jnp.cumsum(ragged_sizes(own, 4, LEN, LEN // 2, 0)), jnp.arange(LEN), side="right"))(jax.random.split(splits[3], ROWS)).reshape((ROWS, LEN)).astype(jnp.int32)
    row_live = place_ends((jax.random.randint(splits[4], (ROWS,), 0, 8) < 7).astype(jnp.int32), jax.random.fold_in(splits[4], 1), 0, 1)
    buckets = draw_buckets(jax.random.fold_in(splits[17], 71), 0)
    gain_self = jnp.clip(1.0 + 0.1 * jax.random.normal(splits[6], (D,), jnp.float32), 0.5, 1.5).astype(jnp.bfloat16)
    w_qkv = normal_values(splits[7], (D, 3 * D), D ** -0.5, 0.21875, ((0, 4),))
    w_attn_out = normal_values(splits[8], (D, D), 8 ** -0.5, 2.0, ((0, 4),))
    rel_bias = normal_values(splits[9], (BUCKETS, HEADS), 1.0, 4.0, ((0, 4),))
    gain_cross = jnp.clip(1.0 + 0.1 * jax.random.normal(splits[10], (D,), jnp.float32), 0.5, 1.5).astype(jnp.bfloat16)
    c_query = normal_values(splits[11], (D, D), D ** -0.5, 0.21875, ((0, 4),))
    c_keyval = normal_values(splits[12], (D, 2 * D), D ** -0.5, 0.21875, ((0, 4),))
    c_out = normal_values(splits[13], (D, D), 8 ** -0.5, 2.0, ((0, 4),))
    gain_ff = jnp.clip(1.0 + 0.1 * jax.random.normal(splits[14], (D,), jnp.float32), 0.5, 1.5).astype(jnp.bfloat16)
    w_gate_up = normal_values(splits[15], (D, 2 * FF), D ** -0.5, 0.21875, ((0, 4),))
    w_down = normal_values(splits[16], (FF, D), FF ** -0.5, 0.125, ((0, 4),))
    return {"inputs": inputs, "memory": memory, "cotangent": cotangent, "segment_ids": segment_ids, "row_live": row_live, "buckets": buckets, "gain_self": gain_self, "w_qkv": w_qkv, "w_attn_out": w_attn_out, "rel_bias": rel_bias, "gain_cross": gain_cross, "c_query": c_query, "c_keyval": c_keyval, "c_out": c_out, "gain_ff": gain_ff, "w_gate_up": w_gate_up, "w_down": w_down}


epsilon = 1e-06
masked_score = -1000000000.0
highest = lax.Precision.HIGHEST

@jax.custom_vjp
def low(v):
    return lax.optimization_barrier(v.astype(jnp.bfloat16)).astype(jnp.float32)

@jax.custom_vjp
def low_back(v):
    return v

def low_keep(v):
    return (low(v), None)

def low_pass(kept, grad):
    return (grad,)

def back_keep(v):
    return (v, None)

def back_low(kept, grad):
    return (low(grad),)
low.defvjp(low_keep, low_pass)
low_back.defvjp(back_keep, back_low)

def rms_norm(values, gain):
    return values * lax.rsqrt(lax.optimization_barrier(jnp.mean(values * values, axis=-1, keepdims=True)) + epsilon) * gain

def product(left, right, form):
    return jnp.einsum(form, left, right, precision=highest, preferred_element_type=jnp.float32)

def self_attention(query_heads, key_heads, value_heads, seg_row, by_dist):
    block = min(512, LEN)
    count = LEN // block
    scale = HEAD_DIM ** (-0.5)
    key_pos = jnp.arange(LEN, dtype=jnp.int32)

    def one_block(items):
        query_block, seg_block, start = items
        query_pos = start + jnp.arange(block, dtype=jnp.int32)
        offsets = query_pos[:, None] - key_pos[None, :]
        bias = jnp.transpose(jnp.take(by_dist, jnp.clip(offsets, 0, LEN - 1), axis=0), (2, 0, 1))
        scores = low_back(product(query_block, key_heads, 'qhd,khd->hqk') * scale + bias)
        allowed = (offsets >= 0) & (seg_block[:, None] == seg_row[None, :])
        scores = jnp.where(allowed[None], scores, masked_score)
        probs = low(jax.nn.softmax(scores, axis=-1))
        return product(probs, value_heads, 'hqk,khd->qhd')
    starts = jnp.arange(count, dtype=jnp.int32) * block
    result = lax.map(jax.checkpoint(one_block), (query_heads.reshape(count, block, HEADS, HEAD_DIM), seg_row.reshape(count, block), starts))
    return result.reshape(LEN, D)

def cross_attention(query_heads, key_heads, value_heads):
    block = min(512, LEN)
    count = LEN // block
    scale = HEAD_DIM ** (-0.5)

    def one_block(query_block):
        scores = low_back(product(query_block, key_heads, 'qhd,khd->hqk') * scale)
        probs = low(jax.nn.softmax(scores, axis=-1))
        return product(probs, value_heads, 'hqk,khd->qhd')
    result = lax.map(jax.checkpoint(one_block), query_heads.reshape(count, block, HEADS, HEAD_DIM))
    return result.reshape(LEN, D)

def layer(params, dense, memory_row, seg_row, live, buckets):
    g_self, wqkv, wout, rel, g_cross, cquery, ckv, cout, g_ff, wgu, wdown = params
    hidden_one = low(rms_norm(dense, g_self))
    qkv = low(low_back(product(hidden_one, wqkv, 'cd,de->ce')))
    onehot_table = (buckets[:, None] == jnp.arange(BUCKETS, dtype=jnp.int32)[None, :]).astype(jnp.float32)
    by_dist = product(onehot_table, rel, 'lb,bh->lh')
    mixed = self_attention(qkv[:, :D].reshape(LEN, HEADS, HEAD_DIM), qkv[:, D:2 * D].reshape(LEN, HEADS, HEAD_DIM), qkv[:, 2 * D:].reshape(LEN, HEADS, HEAD_DIM), seg_row, by_dist)
    attn_low = low(low_back(mixed))
    after_self = dense + live * low_back(product(attn_low, wout, 'cd,de->ce'))
    hidden_two = low(rms_norm(after_self, g_cross))
    cross_q = low(low_back(product(hidden_two, cquery, 'cd,de->ce')))
    memory_kv = low(low_back(product(memory_row, ckv, 'md,de->me')))
    crossed = cross_attention(cross_q.reshape(LEN, HEADS, HEAD_DIM), memory_kv[:, :D].reshape(MEM, HEADS, HEAD_DIM), memory_kv[:, D:].reshape(MEM, HEADS, HEAD_DIM))
    cross_low = low(low_back(crossed))
    after_cross = after_self + live * low_back(product(cross_low, cout, 'cd,de->ce'))
    hidden_three = low(rms_norm(after_cross, g_ff))
    gate_up = low_back(product(hidden_three, wgu, 'cd,df->cf'))
    mixed_ff = low(jax.nn.gelu(gate_up[:, :FF], approximate=True) * gate_up[:, FF:])
    return after_cross + live * low_back(product(mixed_ff, wdown, 'cf,fd->cd'))

def reference(inputs, memory, cotangent, segment_ids, row_live, buckets, gain_self, w_qkv, w_attn_out, rel_bias, gain_cross, c_query, c_keyval, c_out, gain_ff, w_gate_up, w_down):
    params = (gain_self.astype(jnp.float32), w_qkv.astype(jnp.float32), w_attn_out.astype(jnp.float32), rel_bias.astype(jnp.float32), gain_cross.astype(jnp.float32), c_query.astype(jnp.float32), c_keyval.astype(jnp.float32), c_out.astype(jnp.float32), gain_ff.astype(jnp.float32), w_gate_up.astype(jnp.float32), w_down.astype(jnp.float32))

    def one_row(totals, items):
        row_in, row_mem, row_cot, seg_row, live_row = items
        live = live_row.astype(jnp.float32)

        def forward(prm, dense, mem_row):
            return layer(prm, dense, mem_row, seg_row, live, buckets)
        result, pull = jax.vjp(forward, params, row_in.astype(jnp.float32), row_mem.astype(jnp.float32))
        grad_params, grad_in, grad_mem = pull(row_cot.astype(jnp.float32))
        totals = jax.tree.map(lambda left, right: left + right, totals, grad_params)
        return (totals, (result.astype(jnp.bfloat16), grad_in.astype(jnp.bfloat16), grad_mem.astype(jnp.bfloat16)))
    zeros_init = jax.tree.map(jnp.zeros_like, params)
    totals, (outputs, grad_inputs, grad_memory) = lax.scan(one_row, zeros_init, (inputs, memory, cotangent, segment_ids, row_live))
    return (outputs, grad_inputs, grad_memory, totals[0], totals[1], totals[2], totals[3], totals[4], totals[5], totals[6], totals[7], totals[8], totals[9], totals[10])
```

```python
import jax
import jax.numpy as jnp
from jax import lax
from jax.sharding import PartitionSpec as P

D = 768
HEADS = 12
HEAD_DIM = 64
FF = 2048
BUCKETS = 32
LEN = 1024
MEM = 1024


epsilon = 1e-06
masked_score = -1000000000.0
highest = lax.Precision.HIGHEST


def rms_norm(values, gain):
    return values * lax.rsqrt(jnp.mean(values * values, axis=-1, keepdims=True) + epsilon) * gain


def matmul(left, right, form):
    return jnp.einsum(form, left, right, preferred_element_type=jnp.float32)


def softmax_parts(scores):
    top = jnp.max(scores, axis=-1, keepdims=True)
    expo = jnp.exp(scores - top)
    total = jnp.sum(expo, axis=-1, keepdims=True)
    return (expo / total, (top + jnp.log(total))[..., 0])


def score_grads(scores, lse_row, value_row, grad_row):
    probs = jnp.exp(scores - lse_row[..., None])
    grad_probs = matmul(grad_row, value_row, "qhd,khd->hqk")
    centre = jnp.sum(grad_probs * probs, axis=-1, keepdims=True)
    grad_scores = (probs * (grad_probs - centre)).astype(jnp.bfloat16)
    return (probs, grad_scores, centre[..., 0])


def one_hot_of(buckets):
    return (buckets[:, None] == jnp.arange(BUCKETS, dtype=jnp.int32)).astype(jnp.float32)


def skewed(by_dist, start, rows):
    table = jnp.concatenate([jnp.zeros((LEN - 1, HEADS), by_dist.dtype), by_dist], axis=0)
    window = lax.dynamic_slice_in_dim(table, start, rows + LEN - 1, axis=0)
    line = jnp.pad(window[::-1].T, ((0, 0), (0, 1)))
    width = rows + LEN
    flat = jnp.broadcast_to(line[:, None, :], (HEADS, rows, width)).reshape(HEADS, rows * width)
    return flat[:, : rows * (width - 1)].reshape(HEADS, rows, width - 1)[:, :, rows - 1 :]


def unskewed(block, start, rows):
    width = rows + LEN
    wide = jnp.pad(block, ((0, 0), (0, 0), (rows - 1, 0))).reshape(HEADS, rows * (width - 1))
    line = jnp.sum(jnp.pad(wide, ((0, 0), (0, rows))).reshape(HEADS, rows, width), axis=1)
    window = line[:, : width - 1][:, ::-1].T
    table = jnp.zeros((2 * LEN - 1, HEADS), block.dtype)
    return lax.dynamic_update_slice_in_dim(table, window, start, axis=0)[LEN - 1 :]


def per_device(
    inputs,
    memory,
    cotangent,
    segment_ids,
    row_live,
    buckets,
    gain_self,
    w_qkv,
    w_attn_out,
    rel_bias,
    gain_cross,
    c_query,
    c_keyval,
    c_out,
    gain_ff,
    w_gate_up,
    w_down,
):
    (
        g_self,
        qkv_full,
        out_full,
        bias_full,
        g_cross,
        cq_full,
        ckv_full,
        cout_full,
        g_ffn,
        gu_full,
        down_full,
    ) = (
        lax.all_gather(gain_self, "dp", axis=0, tiled=True),
        lax.all_gather(w_qkv, "dp", axis=0, tiled=True),
        lax.all_gather(w_attn_out, "dp", axis=0, tiled=True),
        lax.all_gather(rel_bias, "dp", axis=0, tiled=True),
        lax.all_gather(gain_cross, "dp", axis=0, tiled=True),
        lax.all_gather(c_query, "dp", axis=0, tiled=True),
        lax.all_gather(c_keyval, "dp", axis=0, tiled=True),
        lax.all_gather(c_out, "dp", axis=0, tiled=True),
        lax.all_gather(gain_ff, "dp", axis=0, tiled=True),
        lax.all_gather(w_gate_up, "dp", axis=0, tiled=True),
        lax.all_gather(w_down, "dp", axis=0, tiled=True),
    )
    num_rows, local_len, _ = inputs.shape
    seq_index = lax.axis_index("seq")
    scale = HEAD_DIM ** (-0.5)
    dense = inputs.astype(jnp.float32)
    live_rows = row_live.astype(jnp.float32)[:, None, None]
    normed_one = rms_norm(dense, g_self.astype(jnp.float32))
    hidden_one = normed_one.astype(jnp.bfloat16)
    qkv_local = matmul(hidden_one, qkv_full, "rcd,de->rce").astype(jnp.bfloat16)
    queries = qkv_local[..., :D]
    key_value = qkv_local[..., D:]
    seg_local = segment_ids.astype(jnp.bfloat16)
    key_all, seg_all = (
        lax.all_gather(key_value, "seq", axis=1, tiled=True),
        lax.all_gather(seg_local, "seq", axis=1, tiled=True),
    )
    positions = seq_index * local_len + jnp.arange(local_len, dtype=jnp.int32)
    offsets = positions[:, None] - jnp.arange(LEN, dtype=jnp.int32)[None, :]
    causal = offsets >= 0
    bucket_hot = one_hot_of(buckets)
    by_dist = jnp.einsum(
        "lb,bh->lh",
        bucket_hot,
        bias_full.astype(jnp.float32),
        precision=highest,
        preferred_element_type=jnp.float32,
    )
    bias_block = skewed(by_dist, seq_index * local_len, local_len)

    def self_scores(queries_h, key_row, seg_row, segk_row):
        raw = matmul(queries_h, key_row, "qhd,khd->hqk") * scale + bias_block
        allowed = causal & (seg_row[:, None] == segk_row[None, :])
        return jnp.where(allowed[None], raw, masked_score)

    def self_forward(items):
        query_row, kv_row, seg_row, segk_row = items
        key_row = kv_row[:, :D].reshape(LEN, HEADS, HEAD_DIM)
        value_row = kv_row[:, D:].reshape(LEN, HEADS, HEAD_DIM)
        scores = self_scores(
            query_row.reshape(local_len, HEADS, HEAD_DIM), key_row, seg_row, segk_row
        )
        probs, lse_row = softmax_parts(scores)
        mixed = matmul(probs.astype(jnp.bfloat16), value_row, "hqk,khd->qhd")
        return (mixed.reshape(local_len, D), lse_row)

    attn_self, lse_self = lax.map(self_forward, (queries, key_all, seg_local, seg_all))
    attn_low = attn_self.astype(jnp.bfloat16)
    branch_one = matmul(attn_low, out_full, "rcd,de->rce")
    after_self = dense + live_rows * branch_one
    normed_two = rms_norm(after_self, g_cross.astype(jnp.float32))
    hidden_two = normed_two.astype(jnp.bfloat16)
    cross_q = matmul(hidden_two, cq_full, "rcd,de->rce").astype(jnp.bfloat16)
    memory_kv = matmul(memory, ckv_full, "rmd,de->rme").astype(jnp.bfloat16)
    memory_all = lax.all_gather(memory_kv, "seq", axis=1, tiled=True)

    def cross_forward(items):
        query_row, kv_row = items
        key_row = kv_row[:, :D].reshape(MEM, HEADS, HEAD_DIM)
        value_row = kv_row[:, D:].reshape(MEM, HEADS, HEAD_DIM)
        scores = (
            matmul(query_row.reshape(local_len, HEADS, HEAD_DIM), key_row, "qhd,khd->hqk") * scale
        )
        probs, lse_row = softmax_parts(scores)
        mixed = matmul(probs.astype(jnp.bfloat16), value_row, "hqk,khd->qhd")
        return (mixed.reshape(local_len, D), lse_row)

    attn_cross, lse_cross = lax.map(cross_forward, (cross_q, memory_all))
    cross_low = attn_cross.astype(jnp.bfloat16)
    branch_two = matmul(cross_low, cout_full, "rcd,de->rce")
    after_cross = after_self + live_rows * branch_two
    normed_three = rms_norm(after_cross, g_ffn.astype(jnp.float32))
    hidden_three = normed_three.astype(jnp.bfloat16)
    gate_up = matmul(hidden_three, gu_full, "rcd,df->rcf")
    gate = gate_up[..., :FF]
    upward = gate_up[..., FF:]
    mixed_ff = (jax.nn.gelu(gate, approximate=True) * upward).astype(jnp.bfloat16)
    branch_three = matmul(mixed_ff, down_full, "rcf,fd->rcd")
    output = (after_cross + live_rows * branch_three).astype(jnp.bfloat16)
    (
        g_self,
        qkv_full,
        out_full,
        bias_full,
        g_cross,
        cq_full,
        ckv_full,
        cout_full,
        g_ffn,
        gu_full,
        down_full,
    ) = (
        lax.all_gather(gain_self, "dp", axis=0, tiled=True),
        lax.all_gather(w_qkv, "dp", axis=0, tiled=True),
        lax.all_gather(w_attn_out, "dp", axis=0, tiled=True),
        lax.all_gather(rel_bias, "dp", axis=0, tiled=True),
        lax.all_gather(gain_cross, "dp", axis=0, tiled=True),
        lax.all_gather(c_query, "dp", axis=0, tiled=True),
        lax.all_gather(c_keyval, "dp", axis=0, tiled=True),
        lax.all_gather(c_out, "dp", axis=0, tiled=True),
        lax.all_gather(gain_ff, "dp", axis=0, tiled=True),
        lax.all_gather(w_gate_up, "dp", axis=0, tiled=True),
        lax.all_gather(w_down, "dp", axis=0, tiled=True),
    )
    grad_out = cotangent.astype(jnp.float32)
    down_in = (live_rows * grad_out).astype(jnp.bfloat16)
    grad_down = matmul(mixed_ff, down_in, "rcf,rcd->fd")
    grad_mixed = matmul(down_in, down_full, "rcd,fd->rcf")
    _, gelu_pull = jax.vjp(
        lambda gate_in, up_in: jax.nn.gelu(gate_in, approximate=True) * up_in, gate, upward
    )
    grad_gate, grad_upward = gelu_pull(grad_mixed)
    grad_gu_low = jnp.concatenate([grad_gate, grad_upward], axis=-1).astype(jnp.bfloat16)
    grad_gate_up = matmul(hidden_three, grad_gu_low, "rcd,rcf->df")
    grad_normed_three = matmul(grad_gu_low, gu_full, "rcf,df->rcd")
    _, pull_three = jax.vjp(rms_norm, after_cross, g_ffn.astype(jnp.float32))
    part_three, grad_gain_ff = pull_three(grad_normed_three)
    grad_after_cross = grad_out + part_three
    cross_in = (live_rows * grad_after_cross).astype(jnp.bfloat16)
    grad_cout = matmul(cross_low, cross_in, "rcd,rce->de")
    grad_cross_attn = matmul(cross_in, cout_full, "rce,de->rcd").astype(jnp.bfloat16)

    def cross_backward(items):
        query_row, kv_row, lse_row, grad_row = items
        queries_h = query_row.reshape(local_len, HEADS, HEAD_DIM)
        grad_h = grad_row.reshape(local_len, HEADS, HEAD_DIM)
        key_row = kv_row[:, :D].reshape(MEM, HEADS, HEAD_DIM)
        value_row = kv_row[:, D:].reshape(MEM, HEADS, HEAD_DIM)
        scores = matmul(queries_h, key_row, "qhd,khd->hqk") * scale
        probs, grad_scores, centre = score_grads(scores, lse_row, value_row, grad_h)
        grad_query = matmul(grad_scores, key_row, "hqk,khd->qhd") * scale
        grad_key = matmul(grad_scores, queries_h, "hqk,qhd->khd") * scale
        grad_value = matmul(probs.astype(jnp.bfloat16), grad_h, "hqk,qhd->khd")
        kv_grads = jnp.concatenate([grad_key.reshape(MEM, D), grad_value.reshape(MEM, D)], axis=-1)
        return (grad_query.reshape(local_len, D), kv_grads, centre)

    grad_cq_rows, grad_memkv_full, _ = lax.map(
        cross_backward, (cross_q, memory_all, lse_cross, grad_cross_attn)
    )
    grad_memkv = lax.psum_scatter(
        grad_memkv_full.astype(jnp.bfloat16), "seq", scatter_dimension=1, tiled=True
    )
    grad_ckv = matmul(memory, grad_memkv, "rmd,rme->de")
    grad_memory = matmul(grad_memkv, ckv_full, "rme,de->rmd").astype(jnp.bfloat16)
    grad_cq_low = grad_cq_rows.astype(jnp.bfloat16)
    grad_cquery = matmul(hidden_two, grad_cq_low, "rcd,rce->de")
    grad_normed_two = matmul(grad_cq_low, cq_full, "rce,de->rcd")
    _, pull_two = jax.vjp(rms_norm, after_self, g_cross.astype(jnp.float32))
    part_two, grad_gain_cross = pull_two(grad_normed_two)
    grad_after_self = grad_after_cross + part_two
    self_in = (live_rows * grad_after_self).astype(jnp.bfloat16)
    grad_wout = matmul(attn_low, self_in, "rcd,rce->de")
    grad_self_attn = matmul(self_in, out_full, "rce,de->rcd").astype(jnp.bfloat16)

    def self_backward(carry, items):
        query_row, kv_row, seg_row, segk_row, lse_row, grad_row = items
        queries_h = query_row.reshape(local_len, HEADS, HEAD_DIM)
        grad_h = grad_row.reshape(local_len, HEADS, HEAD_DIM)
        key_row = kv_row[:, :D].reshape(LEN, HEADS, HEAD_DIM)
        value_row = kv_row[:, D:].reshape(LEN, HEADS, HEAD_DIM)
        scores = self_scores(queries_h, key_row, seg_row, segk_row)
        probs, grad_scores, centre = score_grads(scores, lse_row, value_row, grad_h)
        grad_query = matmul(grad_scores, key_row, "hqk,khd->qhd") * scale
        grad_key = matmul(grad_scores, queries_h, "hqk,qhd->khd") * scale
        grad_value = matmul(probs.astype(jnp.bfloat16), grad_h, "hqk,qhd->khd")
        kv_grads = jnp.concatenate([grad_key.reshape(LEN, D), grad_value.reshape(LEN, D)], axis=-1)
        return (
            carry + grad_scores.astype(jnp.float32),
            (grad_query.reshape(local_len, D), kv_grads, centre),
        )

    zero_block = jnp.zeros((HEADS, local_len, LEN), jnp.float32)
    score_total, (grad_q_rows, grad_kv_full, _) = lax.scan(
        self_backward, zero_block, (queries, key_all, seg_local, seg_all, lse_self, grad_self_attn)
    )
    grad_kv = lax.psum_scatter(
        grad_kv_full.astype(jnp.bfloat16), "seq", scatter_dimension=1, tiled=True
    )
    grad_bias = jnp.einsum(
        "lh,lb->bh",
        unskewed(score_total, seq_index * local_len, local_len),
        bucket_hot,
        precision=highest,
        preferred_element_type=jnp.float32,
    )
    grad_qkv_low = jnp.concatenate([grad_q_rows.astype(jnp.bfloat16), grad_kv], axis=-1)
    grad_wqkv = matmul(hidden_one, grad_qkv_low, "rcd,rce->de")
    grad_normed_one = matmul(grad_qkv_low, qkv_full, "rce,de->rcd")
    _, pull_one = jax.vjp(rms_norm, dense, g_self.astype(jnp.float32))
    part_one, grad_gain_self = pull_one(grad_normed_one)
    grad_inputs = (grad_after_self + part_one).astype(jnp.bfloat16)
    (
        own_gself,
        own_qkv,
        own_wout,
        own_bias,
        own_gcross,
        own_cquery,
        own_ckv,
        own_cout,
        own_gff,
        own_gateup,
        own_down,
    ) = (
        lax.psum_scatter(
            grad_gain_self.astype(jnp.bfloat16), "dp", scatter_dimension=0, tiled=True
        ).astype(jnp.float32),
        lax.psum_scatter(
            grad_wqkv.astype(jnp.bfloat16), "dp", scatter_dimension=0, tiled=True
        ).astype(jnp.float32),
        lax.psum_scatter(
            grad_wout.astype(jnp.bfloat16), "dp", scatter_dimension=0, tiled=True
        ).astype(jnp.float32),
        lax.psum_scatter(
            grad_bias.astype(jnp.bfloat16), "dp", scatter_dimension=0, tiled=True
        ).astype(jnp.float32),
        lax.psum_scatter(
            grad_gain_cross.astype(jnp.bfloat16), "dp", scatter_dimension=0, tiled=True
        ).astype(jnp.float32),
        lax.psum_scatter(
            grad_cquery.astype(jnp.bfloat16), "dp", scatter_dimension=0, tiled=True
        ).astype(jnp.float32),
        lax.psum_scatter(
            grad_ckv.astype(jnp.bfloat16), "dp", scatter_dimension=0, tiled=True
        ).astype(jnp.float32),
        lax.psum_scatter(
            grad_cout.astype(jnp.bfloat16), "dp", scatter_dimension=0, tiled=True
        ).astype(jnp.float32),
        lax.psum_scatter(
            grad_gain_ff.astype(jnp.bfloat16), "dp", scatter_dimension=0, tiled=True
        ).astype(jnp.float32),
        lax.psum_scatter(
            grad_gate_up.astype(jnp.bfloat16), "dp", scatter_dimension=0, tiled=True
        ).astype(jnp.float32),
        lax.psum_scatter(
            grad_down.astype(jnp.bfloat16), "dp", scatter_dimension=0, tiled=True
        ).astype(jnp.float32),
    )
    summed = (
        lax.psum(own_gself.astype(jnp.bfloat16), "seq").astype(jnp.float32),
        lax.psum(own_qkv.astype(jnp.bfloat16), "seq").astype(jnp.float32),
        lax.psum(own_wout.astype(jnp.bfloat16), "seq").astype(jnp.float32),
        lax.psum(own_bias.astype(jnp.bfloat16), "seq").astype(jnp.float32),
        lax.psum(own_gcross.astype(jnp.bfloat16), "seq").astype(jnp.float32),
        lax.psum(own_cquery.astype(jnp.bfloat16), "seq").astype(jnp.float32),
        lax.psum(own_ckv.astype(jnp.bfloat16), "seq").astype(jnp.float32),
        lax.psum(own_cout.astype(jnp.bfloat16), "seq").astype(jnp.float32),
        lax.psum(own_gff.astype(jnp.bfloat16), "seq").astype(jnp.float32),
        lax.psum(own_gateup.astype(jnp.bfloat16), "seq").astype(jnp.float32),
        lax.psum(own_down.astype(jnp.bfloat16), "seq").astype(jnp.float32),
    )
    return (
        output,
        grad_inputs,
        grad_memory,
        summed[0],
        summed[1],
        summed[2],
        summed[3],
        summed[4],
        summed[5],
        summed[6],
        summed[7],
        summed[8],
        summed[9],
        summed[10],
    )


def solution(mesh):
    in_specs = (
        P("dp", "seq", None),
        P("dp", "seq", None),
        P("dp", "seq", None),
        P("dp", "seq"),
        P("dp"),
        P(),
        P("dp"),
        P("dp", None),
        P("dp", None),
        P("dp", None),
        P("dp"),
        P("dp", None),
        P("dp", None),
        P("dp", None),
        P("dp"),
        P("dp", None),
        P("dp", None),
    )
    out_specs = (
        P("dp", "seq", None),
        P("dp", "seq", None),
        P("dp", "seq", None),
        P("dp"),
        P("dp", None),
        P("dp", None),
        P("dp", None),
        P("dp"),
        P("dp", None),
        P("dp", None),
        P("dp", None),
        P("dp"),
        P("dp", None),
        P("dp", None),
    )
    return jax.shard_map(
        per_device, mesh=mesh, in_specs=in_specs, out_specs=out_specs, check_vma=False
    )
```

```python
import jax
import jax.numpy as jnp
from jax import lax
from jax.experimental import pallas as pl
from jax.experimental.pallas import tpu as pltpu
from jax.sharding import PartitionSpec as P

D = 768
HEADS = 12
HEAD_DIM = 64
FF = 2048
BUCKETS = 32
LEN = 1024
MEM = 1024


epsilon = 1e-06
masked_score = -1000000000.0
highest = lax.Precision.HIGHEST


def rms_norm(values, gain):
    return values * lax.rsqrt(jnp.mean(values * values, axis=-1, keepdims=True) + epsilon) * gain


def matmul(left, right, form):
    return jnp.einsum(form, left, right, preferred_element_type=jnp.float32)


def softmax_parts(scores):
    top = jnp.max(scores, axis=-1, keepdims=True)
    expo = jnp.exp(scores - top)
    total = jnp.sum(expo, axis=-1, keepdims=True)
    return (expo / total, (top + jnp.log(total))[..., 0])


def score_grads(scores, lse_row, value_row, grad_row):
    probs = jnp.exp(scores - lse_row[..., None])
    grad_probs = matmul(grad_row, value_row, "qhd,khd->hqk")
    centre = jnp.sum(grad_probs * probs, axis=-1, keepdims=True)
    grad_scores = (probs * (grad_probs - centre)).astype(jnp.bfloat16)
    return (probs, grad_scores, centre[..., 0])


def one_hot_of(buckets):
    return (buckets[:, None] == jnp.arange(BUCKETS, dtype=jnp.int32)).astype(jnp.float32)


def skewed(by_dist, start, rows):
    table = jnp.concatenate([jnp.zeros((LEN - 1, HEADS), by_dist.dtype), by_dist], axis=0)
    window = lax.dynamic_slice_in_dim(table, start, rows + LEN - 1, axis=0)
    line = jnp.pad(window[::-1].T, ((0, 0), (0, 1)))
    width = rows + LEN
    flat = jnp.broadcast_to(line[:, None, :], (HEADS, rows, width)).reshape(HEADS, rows * width)
    return flat[:, : rows * (width - 1)].reshape(HEADS, rows, width - 1)[:, :, rows - 1 :]


def unskewed(block, start, rows):
    width = rows + LEN
    wide = jnp.pad(block, ((0, 0), (0, 0), (rows - 1, 0))).reshape(HEADS, rows * (width - 1))
    line = jnp.sum(jnp.pad(wide, ((0, 0), (0, rows))).reshape(HEADS, rows, width), axis=1)
    window = line[:, : width - 1][:, ::-1].T
    table = jnp.zeros((2 * LEN - 1, HEADS), block.dtype)
    return lax.dynamic_update_slice_in_dim(table, window, start, axis=0)[LEN - 1 :]


def per_device(
    inputs,
    memory,
    cotangent,
    segment_ids,
    row_live,
    buckets,
    gain_self,
    w_qkv,
    w_attn_out,
    rel_bias,
    gain_cross,
    c_query,
    c_keyval,
    c_out,
    gain_ff,
    w_gate_up,
    w_down,
):
    (
        g_self,
        qkv_full,
        out_full,
        bias_full,
        g_cross,
        cq_full,
        ckv_full,
        cout_full,
        g_ffn,
        gu_full,
        down_full,
    ) = (
        lax.all_gather(gain_self, "dp", axis=0, tiled=True),
        lax.all_gather(w_qkv, "dp", axis=0, tiled=True),
        lax.all_gather(w_attn_out, "dp", axis=0, tiled=True),
        lax.all_gather(rel_bias, "dp", axis=0, tiled=True),
        lax.all_gather(gain_cross, "dp", axis=0, tiled=True),
        lax.all_gather(c_query, "dp", axis=0, tiled=True),
        lax.all_gather(c_keyval, "dp", axis=0, tiled=True),
        lax.all_gather(c_out, "dp", axis=0, tiled=True),
        lax.all_gather(gain_ff, "dp", axis=0, tiled=True),
        lax.all_gather(w_gate_up, "dp", axis=0, tiled=True),
        lax.all_gather(w_down, "dp", axis=0, tiled=True),
    )
    num_rows, local_len, _ = inputs.shape
    seq_index = lax.axis_index("seq")
    scale = HEAD_DIM ** (-0.5)
    dense = inputs.astype(jnp.float32)
    live_rows = row_live.astype(jnp.float32)[:, None, None]
    normed_one = rms_norm(dense, g_self.astype(jnp.float32))
    hidden_one = normed_one.astype(jnp.bfloat16)
    qkv_local = matmul(hidden_one, qkv_full, "rcd,de->rce").astype(jnp.bfloat16)
    queries = qkv_local[..., :D]
    key_value = qkv_local[..., D:]
    seg_local = segment_ids.astype(jnp.bfloat16)
    key_all, seg_all = (
        lax.all_gather(key_value, "seq", axis=1, tiled=True),
        lax.all_gather(seg_local, "seq", axis=1, tiled=True),
    )
    positions = seq_index * local_len + jnp.arange(local_len, dtype=jnp.int32)
    offsets = positions[:, None] - jnp.arange(LEN, dtype=jnp.int32)[None, :]
    causal = offsets >= 0
    bucket_hot = one_hot_of(buckets)
    by_dist = jnp.einsum(
        "lb,bh->lh",
        bucket_hot,
        bias_full.astype(jnp.float32),
        precision=highest,
        preferred_element_type=jnp.float32,
    )
    bias_block = skewed(by_dist, seq_index * local_len, local_len)

    def self_scores(queries_h, key_row, seg_row, segk_row):
        raw = matmul(queries_h, key_row, "qhd,khd->hqk") * scale + bias_block
        allowed = causal & (seg_row[:, None] == segk_row[None, :])
        return jnp.where(allowed[None], raw, masked_score)

    def self_forward(items):
        query_row, kv_row, seg_row, segk_row = items
        key_row = kv_row[:, :D].reshape(LEN, HEADS, HEAD_DIM)
        value_row = kv_row[:, D:].reshape(LEN, HEADS, HEAD_DIM)
        scores = self_scores(
            query_row.reshape(local_len, HEADS, HEAD_DIM), key_row, seg_row, segk_row
        )
        probs, lse_row = softmax_parts(scores)
        mixed = matmul(probs.astype(jnp.bfloat16), value_row, "hqk,khd->qhd")
        return (mixed.reshape(local_len, D), lse_row)

    attn_self, lse_self = lax.map(self_forward, (queries, key_all, seg_local, seg_all))
    attn_low = attn_self.astype(jnp.bfloat16)
    branch_one = matmul(attn_low, out_full, "rcd,de->rce")
    after_self = dense + live_rows * branch_one
    normed_two = rms_norm(after_self, g_cross.astype(jnp.float32))
    hidden_two = normed_two.astype(jnp.bfloat16)
    cross_q = matmul(hidden_two, cq_full, "rcd,de->rce").astype(jnp.bfloat16)
    memory_kv = matmul(memory, ckv_full, "rmd,de->rme").astype(jnp.bfloat16)
    memory_all = lax.all_gather(memory_kv, "seq", axis=1, tiled=True)

    def cross_forward(items):
        query_row, kv_row = items
        key_row = kv_row[:, :D].reshape(MEM, HEADS, HEAD_DIM)
        value_row = kv_row[:, D:].reshape(MEM, HEADS, HEAD_DIM)
        scores = (
            matmul(query_row.reshape(local_len, HEADS, HEAD_DIM), key_row, "qhd,khd->hqk") * scale
        )
        probs, lse_row = softmax_parts(scores)
        mixed = matmul(probs.astype(jnp.bfloat16), value_row, "hqk,khd->qhd")
        return (mixed.reshape(local_len, D), lse_row)

    attn_cross, lse_cross = lax.map(cross_forward, (cross_q, memory_all))
    cross_low = attn_cross.astype(jnp.bfloat16)
    branch_two = matmul(cross_low, cout_full, "rcd,de->rce")
    after_cross = after_self + live_rows * branch_two
    normed_three = rms_norm(after_cross, g_ffn.astype(jnp.float32))
    hidden_three = normed_three.astype(jnp.bfloat16)
    gate_up = matmul(hidden_three, gu_full, "rcd,df->rcf")
    gate = gate_up[..., :FF]
    upward = gate_up[..., FF:]
    mixed_ff = (jax.nn.gelu(gate, approximate=True) * upward).astype(jnp.bfloat16)
    branch_three = matmul(mixed_ff, down_full, "rcf,fd->rcd")
    output = (after_cross + live_rows * branch_three).astype(jnp.bfloat16)
    (
        g_self,
        qkv_full,
        out_full,
        bias_full,
        g_cross,
        cq_full,
        ckv_full,
        cout_full,
        g_ffn,
        gu_full,
        down_full,
    ) = (
        lax.all_gather(gain_self, "dp", axis=0, tiled=True),
        lax.all_gather(w_qkv, "dp", axis=0, tiled=True),
        lax.all_gather(w_attn_out, "dp", axis=0, tiled=True),
        lax.all_gather(rel_bias, "dp", axis=0, tiled=True),
        lax.all_gather(gain_cross, "dp", axis=0, tiled=True),
        lax.all_gather(c_query, "dp", axis=0, tiled=True),
        lax.all_gather(c_keyval, "dp", axis=0, tiled=True),
        lax.all_gather(c_out, "dp", axis=0, tiled=True),
        lax.all_gather(gain_ff, "dp", axis=0, tiled=True),
        lax.all_gather(w_gate_up, "dp", axis=0, tiled=True),
        lax.all_gather(w_down, "dp", axis=0, tiled=True),
    )
    grad_out = cotangent.astype(jnp.float32)
    down_in = (live_rows * grad_out).astype(jnp.bfloat16)
    grad_down = matmul(mixed_ff, down_in, "rcf,rcd->fd")
    grad_mixed = matmul(down_in, down_full, "rcd,fd->rcf")
    _, gelu_pull = jax.vjp(
        lambda gate_in, up_in: jax.nn.gelu(gate_in, approximate=True) * up_in, gate, upward
    )
    grad_gate, grad_upward = gelu_pull(grad_mixed)
    grad_gu_low = jnp.concatenate([grad_gate, grad_upward], axis=-1).astype(jnp.bfloat16)
    grad_gate_up = matmul(hidden_three, grad_gu_low, "rcd,rcf->df")
    grad_normed_three = matmul(grad_gu_low, gu_full, "rcf,df->rcd")
    _, pull_three = jax.vjp(rms_norm, after_cross, g_ffn.astype(jnp.float32))
    part_three, grad_gain_ff = pull_three(grad_normed_three)
    grad_after_cross = grad_out + part_three
    cross_in = (live_rows * grad_after_cross).astype(jnp.bfloat16)
    grad_cout = matmul(cross_low, cross_in, "rcd,rce->de")
    grad_cross_attn = matmul(cross_in, cout_full, "rce,de->rcd").astype(jnp.bfloat16)

    def cross_backward(items):
        query_row, kv_row, lse_row, grad_row = items
        queries_h = query_row.reshape(local_len, HEADS, HEAD_DIM)
        grad_h = grad_row.reshape(local_len, HEADS, HEAD_DIM)
        key_row = kv_row[:, :D].reshape(MEM, HEADS, HEAD_DIM)
        value_row = kv_row[:, D:].reshape(MEM, HEADS, HEAD_DIM)
        scores = matmul(queries_h, key_row, "qhd,khd->hqk") * scale
        probs, grad_scores, centre = score_grads(scores, lse_row, value_row, grad_h)
        grad_query = matmul(grad_scores, key_row, "hqk,khd->qhd") * scale
        grad_key = matmul(grad_scores, queries_h, "hqk,qhd->khd") * scale
        grad_value = matmul(probs.astype(jnp.bfloat16), grad_h, "hqk,qhd->khd")
        kv_grads = jnp.concatenate([grad_key.reshape(MEM, D), grad_value.reshape(MEM, D)], axis=-1)
        return (grad_query.reshape(local_len, D), kv_grads, centre)

    grad_cq_rows, grad_memkv_full, _ = lax.map(
        cross_backward, (cross_q, memory_all, lse_cross, grad_cross_attn)
    )
    grad_memkv = lax.psum_scatter(
        grad_memkv_full.astype(jnp.bfloat16), "seq", scatter_dimension=1, tiled=True
    )
    grad_ckv = matmul(memory, grad_memkv, "rmd,rme->de")
    grad_memory = matmul(grad_memkv, ckv_full, "rme,de->rmd").astype(jnp.bfloat16)
    grad_cq_low = grad_cq_rows.astype(jnp.bfloat16)
    grad_cquery = matmul(hidden_two, grad_cq_low, "rcd,rce->de")
    grad_normed_two = matmul(grad_cq_low, cq_full, "rce,de->rcd")
    _, pull_two = jax.vjp(rms_norm, after_self, g_cross.astype(jnp.float32))
    part_two, grad_gain_cross = pull_two(grad_normed_two)
    grad_after_self = grad_after_cross + part_two
    self_in = (live_rows * grad_after_self).astype(jnp.bfloat16)
    grad_wout = matmul(attn_low, self_in, "rcd,rce->de")
    grad_self_attn = matmul(self_in, out_full, "rce,de->rcd").astype(jnp.bfloat16)

    def self_backward(carry, items):
        query_row, kv_row, seg_row, segk_row, lse_row, grad_row = items
        queries_h = query_row.reshape(local_len, HEADS, HEAD_DIM)
        grad_h = grad_row.reshape(local_len, HEADS, HEAD_DIM)
        key_row = kv_row[:, :D].reshape(LEN, HEADS, HEAD_DIM)
        value_row = kv_row[:, D:].reshape(LEN, HEADS, HEAD_DIM)
        scores = self_scores(queries_h, key_row, seg_row, segk_row)
        probs, grad_scores, centre = score_grads(scores, lse_row, value_row, grad_h)
        grad_query = matmul(grad_scores, key_row, "hqk,khd->qhd") * scale
        grad_key = matmul(grad_scores, queries_h, "hqk,qhd->khd") * scale
        grad_value = matmul(probs.astype(jnp.bfloat16), grad_h, "hqk,qhd->khd")
        kv_grads = jnp.concatenate([grad_key.reshape(LEN, D), grad_value.reshape(LEN, D)], axis=-1)
        return (
            carry + grad_scores.astype(jnp.float32),
            (grad_query.reshape(local_len, D), kv_grads, centre),
        )

    zero_block = jnp.zeros((HEADS, local_len, LEN), jnp.float32)
    score_total, (grad_q_rows, grad_kv_full, _) = lax.scan(
        self_backward, zero_block, (queries, key_all, seg_local, seg_all, lse_self, grad_self_attn)
    )
    grad_kv = lax.psum_scatter(
        grad_kv_full.astype(jnp.bfloat16), "seq", scatter_dimension=1, tiled=True
    )
    grad_bias = jnp.einsum(
        "lh,lb->bh",
        unskewed(score_total, seq_index * local_len, local_len),
        bucket_hot,
        precision=highest,
        preferred_element_type=jnp.float32,
    )
    grad_qkv_low = jnp.concatenate([grad_q_rows.astype(jnp.bfloat16), grad_kv], axis=-1)
    grad_wqkv = matmul(hidden_one, grad_qkv_low, "rcd,rce->de")
    grad_normed_one = matmul(grad_qkv_low, qkv_full, "rce,de->rcd")
    _, pull_one = jax.vjp(rms_norm, dense, g_self.astype(jnp.float32))
    part_one, grad_gain_self = pull_one(grad_normed_one)
    grad_inputs = (grad_after_self + part_one).astype(jnp.bfloat16)
    (
        own_gself,
        own_qkv,
        own_wout,
        own_bias,
        own_gcross,
        own_cquery,
        own_ckv,
        own_cout,
        own_gff,
        own_gateup,
        own_down,
    ) = (
        lax.psum_scatter(
            grad_gain_self.astype(jnp.bfloat16), "dp", scatter_dimension=0, tiled=True
        ).astype(jnp.float32),
        lax.psum_scatter(
            grad_wqkv.astype(jnp.bfloat16), "dp", scatter_dimension=0, tiled=True
        ).astype(jnp.float32),
        lax.psum_scatter(
            grad_wout.astype(jnp.bfloat16), "dp", scatter_dimension=0, tiled=True
        ).astype(jnp.float32),
        lax.psum_scatter(
            grad_bias.astype(jnp.bfloat16), "dp", scatter_dimension=0, tiled=True
        ).astype(jnp.float32),
        lax.psum_scatter(
            grad_gain_cross.astype(jnp.bfloat16), "dp", scatter_dimension=0, tiled=True
        ).astype(jnp.float32),
        lax.psum_scatter(
            grad_cquery.astype(jnp.bfloat16), "dp", scatter_dimension=0, tiled=True
        ).astype(jnp.float32),
        lax.psum_scatter(
            grad_ckv.astype(jnp.bfloat16), "dp", scatter_dimension=0, tiled=True
        ).astype(jnp.float32),
        lax.psum_scatter(
            grad_cout.astype(jnp.bfloat16), "dp", scatter_dimension=0, tiled=True
        ).astype(jnp.float32),
        lax.psum_scatter(
            grad_gain_ff.astype(jnp.bfloat16), "dp", scatter_dimension=0, tiled=True
        ).astype(jnp.float32),
        lax.psum_scatter(
            grad_gate_up.astype(jnp.bfloat16), "dp", scatter_dimension=0, tiled=True
        ).astype(jnp.float32),
        lax.psum_scatter(
            grad_down.astype(jnp.bfloat16), "dp", scatter_dimension=0, tiled=True
        ).astype(jnp.float32),
    )
    summed = (
        lax.psum(own_gself.astype(jnp.bfloat16), "seq").astype(jnp.float32),
        lax.psum(own_qkv.astype(jnp.bfloat16), "seq").astype(jnp.float32),
        lax.psum(own_wout.astype(jnp.bfloat16), "seq").astype(jnp.float32),
        lax.psum(own_bias.astype(jnp.bfloat16), "seq").astype(jnp.float32),
        lax.psum(own_gcross.astype(jnp.bfloat16), "seq").astype(jnp.float32),
        lax.psum(own_cquery.astype(jnp.bfloat16), "seq").astype(jnp.float32),
        lax.psum(own_ckv.astype(jnp.bfloat16), "seq").astype(jnp.float32),
        lax.psum(own_cout.astype(jnp.bfloat16), "seq").astype(jnp.float32),
        lax.psum(own_gff.astype(jnp.bfloat16), "seq").astype(jnp.float32),
        lax.psum(own_gateup.astype(jnp.bfloat16), "seq").astype(jnp.float32),
        lax.psum(own_down.astype(jnp.bfloat16), "seq").astype(jnp.float32),
    )
    return (
        output,
        grad_inputs,
        grad_memory,
        summed[0],
        summed[1],
        summed[2],
        summed[3],
        summed[4],
        summed[5],
        summed[6],
        summed[7],
        summed[8],
        summed[9],
        summed[10],
    )


f32, bf16 = jnp.float32, jnp.bfloat16
BIG = 1.0e9
SCALE = HEAD_DIM ** (-0.5)
MESH = pl.DeviceIdType.MESH
GELU_A, GELU_B = 0.7978845608028654, 0.044715
N_SEM, N_LOCAL = 220, 32


def flip(v, k, bits):
    for i in range(bits):
        if (k >> i) & 1:
            b = 1 << i
            v = v + b - 2 * b * lax.rem(lax.div(v, b), 2)
    return v


def dot(a, b):
    return lax.dot_general(a, b, (((1,), (0,)), ((), ())), preferred_element_type=f32)


def dot_nt(a, b):
    return lax.dot_general(a, b, (((1,), (1,)), ((), ())), preferred_element_type=f32)


def dot_tn(a, b):
    return lax.dot_general(a, b, (((0,), (0,)), ((), ())), preferred_element_type=f32)


def inv_rms(v):
    return lax.rsqrt(jnp.mean(v * v, axis=-1, keepdims=True) + epsilon)


def norm_back(v, gain, w):
    r = inv_rms(v)
    gw = gain * w
    mean = jnp.mean(gw * v, axis=-1, keepdims=True)
    return r * gw - v * (r * r * r * mean), jnp.sum(w * (v * r), axis=0, keepdims=True)


def gelu_parts(gate):
    sq = gate * gate
    th = jnp.tanh(GELU_A * gate * (1.0 + GELU_B * sq))
    half = 0.5 * (1.0 + th)
    slope = half + 0.5 * gate * (1.0 - th * th) * (GELU_A * (1.0 + 3.0 * GELU_B * sq))
    return gate * half, slope


def softmax(scores):
    e = jnp.exp(scores - jnp.max(scores, axis=-1, keepdims=True))
    return (e * (1.0 / jnp.sum(e, axis=-1, keepdims=True))).astype(bf16)


def pad64(v):
    return jnp.concatenate([v, jnp.zeros((v.shape[0], 64), v.dtype)], axis=1)


def above64(v):
    return jnp.concatenate([jnp.zeros((v.shape[0], 64), v.dtype), v], axis=1)


def pack(ref, slot, parts):
    ref[slot, 0:256, :] = jnp.concatenate([parts[0], parts[1]], axis=1)
    ref[slot, 256:384, :] = jnp.concatenate([parts[2][0:128], parts[2][128:256]], axis=1)


def unpack(ref, slot):
    two = ref[slot, 0:256, :]
    last = ref[slot, 256:384, :]
    return (two[:, :64], two[:, 64:], jnp.concatenate([last[:, :64], last[:, 64:]], axis=0))


def assemble(ref, dst):
    for t in range(2):
        a = unpack(ref, 2 * t) + unpack(ref, 2 * t + 1)
        for j in range(3):
            at = 384 * t + 128 * j
            dst[:, at : at + 128] = jnp.concatenate([a[2 * j], a[2 * j + 1]], axis=1)


def disperse(val, ref):
    for gg in range(4):
        pack(ref, gg, [val[:, 192 * gg + 64 * h : 192 * gg + 64 * h + 64] for h in range(3)])


def block(i):
    return pl.ds(pl.multiple_of(i * 256, 256), 256)


def layer_kernel(
    x, mem, cot, segs, gain1, gain2, gain3, rel, buck, live, w_in, w_kv, w_ao, w_cq, w_co, w_gu, w_dn,
    out, gin, gmem, o_gu, o_dn, o_b, o_c, o_small,
    *,
    xrow, mrow, h1, wA, W3, wgu, wd, sm, sg, gains, lines, hot, tbias, qh, kh, vh, mkv, p_self, p_cross, opack,
    arecv, attn, qpack, qrecv, crecv, cattn, after_self, after_cross, h2, h3, prod, dgu, cotb, frecv, hrecv, outb,
    grad, low, dcq, acc, dqkv, rs1, rs2, rt1, rt2, gur, dnr, bsib, bdp, cdp, zg1, zg2, zd1, zd2, zb1, zb2, cfar,
    gsm, sm1, sm2, sgown, ssem, rsem, lsem,
):
    drecv, dqrecv, srecv = arecv, crecv, qrecv
    fown, tot, hown, fpart, xown = tbias.at[0], tbias.at[1], grad, outb, after_cross
    keep, hpart = p_cross.at[0], low.at[1]

    d, s = lax.axis_index("dp"), lax.axis_index("seq")
    c, z, g, r = lax.rem(s, 2), lax.div(s, 2), lax.rem(s, 4), lax.div(s, 4)
    used = {"remote": 0, "local": 0}
    flying = []

    def remote(src, dst, send_sem, recv_sem, dev):
        return pltpu.make_async_remote_copy(
            src_ref=src, dst_ref=dst, send_sem=ssem.at[send_sem], recv_sem=rsem.at[recv_sem],
            device_id=dev, device_id_type=MESH,
        )

    def fresh(n=1):
        used["remote"] += n
        assert used["remote"] <= N_SEM
        return used["remote"] - n

    def push(src, dst, dev):
        sem = fresh()
        copy = remote(src, dst, sem, sem, dev)
        copy.start()
        flying.append(copy)
        return copy

    def sent(copies):
        for copy in copies:
            copy.wait_send()
            flying[:] = [other for other in flying if other is not copy]

    def arrived(copies):
        for copy in copies:
            copy.wait_recv()

    def local(src, dst):
        copy = pltpu.make_async_copy(src, dst, lsem.at[used["local"]])
        used["local"] += 1
        copy.start()
        return copy

    def dpk(k):
        return (flip(d, k, 2), s)

    def seqk(k):
        return (d, flip(s, k, 3))

    def moved(srcs, dsts, devs, slot):
        base = fresh(2)
        for i in range(2):
            away = remote(srcs[i], dsts[i], base + i, base + slot, (d, devs[i]))
            here = pltpu.make_async_copy(srcs[i], dsts[i], rsem.at[base + slot])

            @pl.when(devs[i] != s)
            def _():
                away.start()

            @pl.when(devs[i] == s)
            def _():
                here.start()

        def wait_recv(places):
            for i in range(2):
                pltpu.make_async_copy(places[i], places[i], rsem.at[base + i]).wait()

        def wait_send():
            for i in range(2):
                away = remote(srcs[i], dsts[i], base + i, base + slot, (d, devs[i]))

                @pl.when(devs[i] != s)
                def _():
                    away.wait_send()

        return wait_recv, wait_send

    mine, mine_d = pl.ds(pl.multiple_of(d * 192, 64), 192), block(d)
    here = pl.ds(s * 128, 128)
    own_x = local(x.at[r], xrow.at[here])
    stage = [p_self.at[0, i, 0:192] for i in range(4)] + [p_self.at[1, 0, 0:192]]
    own_in = [
        local(w.at[:, 768 * i : 768 * i + 768], stage[p])
        for p, (w, i) in enumerate(((w_in, 0), (w_in, 1), (w_in, 2), (w_kv, 0), (w_kv, 1)))
    ]
    own_W3 = [local(w, W3.at[i, mine]) for i, w in enumerate((w_ao, w_cq, w_co))]
    own_m = local(mem.at[r], mrow.at[here])
    own_gu = []
    for p in range(8):
        at = pl.multiple_of((p // 4) * FF + (p % 4) * 512 + c * 256, 256)
        own_gu.append(local(w_gu.at[:, pl.ds(at, 256)], wgu.at[mine, pl.ds(p * 256, 256)]))
    own_dn = local(w_dn.at[block(c)], wd.at[mine_d])

    barrier = pltpu.get_barrier_semaphore()
    peers = [dpk(k) for k in (1, 2, 3)] + [seqk(k) for k in range(1, 8)]
    for p in peers:
        pl.semaphore_signal(barrier, inc=1, device_id=p, device_id_type=MESH)
    for i in range(2):
        sgown[i] = jnp.broadcast_to(segs[i : i + 1, :].astype(f32), (16, 128)).astype(bf16)
    sg[s] = sgown[r]
    at_bucket = lax.broadcasted_iota(jnp.int32, (8, 128), 1) == lax.broadcasted_iota(jnp.int32, (8, 128), 0) + 8 * d
    gains[...] = jnp.zeros((16, 768), f32)
    gains[0:12, 0:128] = dot_tn(rel[...].astype(f32), at_bucket.astype(f32))
    for q in range(4):

        @pl.when(d == q)
        def _():
            for i, gain in enumerate((gain1, gain2, gain3)):
                gains[12 + i : 13 + i, 192 * q : 192 * q + 192] = gain[...].astype(f32).reshape(1, 192)

    sm[d] = gains[...].astype(bf16)
    pl.semaphore_wait(barrier, len(peers))

    def row_of(k):
        return lax.div(flip(s, k, 3), 4)

    def spread(src, dst):
        return {m: push(src.at[row_of(2 * m)], dst.at[here], seqk(2 * m)) for m in (1, 2, 3)}

    def hand_on(dst, m):
        part = dst.at[pl.ds(flip(s, 2 * m, 3) * 128, 128)]
        return push(part, part, seqk(1))

    xd = spread(x, xrow)
    own_x.wait()
    xs = {0: hand_on(xrow, 0)}
    for cp in own_in:
        cp.wait()
    for q in range(4):

        @pl.when(g == q)
        def _():
            for p in range(5):
                wA[mine, 192 * p : 192 * p + 192] = stage[p][:, 192 * q : 192 * q + 192]

    wA_in = [push(wA.at[mine], wA.at[mine], dpk(k)) for k in (1, 2, 3)]
    sm_in = [push(sm.at[d], sm.at[d], dpk(k)) for k in (1, 2, 3)]
    sg_in = [push(sgown.at[row_of(k)], sg.at[s], seqk(k)) for k in range(1, 8)]

    def half_rows(dd, cc):
        return pl.ds(pl.multiple_of(dd * 192 + cc * 96, 32), 96)

    def send_W3(i):
        own_W3[i].wait()
        part = W3.at[i, half_rows(d, c)]
        return [push(part, part, dpk(k)) for k in (1, 2, 3)]

    def share_W3(i, copies):
        res = []
        for k, cp in zip((1, 2, 3), copies, strict=True):
            cp.wait_recv()
            part = W3.at[i, half_rows(flip(d, k, 2), c)]
            res.append(push(part, part, seqk(1)))
        return res

    W3_in = {0: send_W3(0)}
    W3_sib = {}

    arrived(sm_in)
    total = sm[0].astype(f32)
    for i in range(1, 4):
        total += sm[i].astype(f32)
    gains[...] = total
    near = jnp.concatenate([buck[i : i + 1, :] for i in range(4)], axis=1)
    by_dist = (lax.broadcasted_iota(jnp.int32, (128, 512), 0) == near).astype(bf16)
    turn = lax.broadcasted_iota(jnp.int32, (512, 1024), 0) + lax.broadcasted_iota(jnp.int32, (512, 1024), 1) == 768
    hot[...] = dot(by_dist, turn.astype(bf16)).astype(bf16)
    column = lax.broadcasted_iota(jnp.int32, (16, 1024), 1)
    line = dot(total[:, :128].astype(bf16), hot[...])
    lines[...] = jnp.where((column > 256) & (column < 769), line, masked_score)
    for h in range(3):
        row = jnp.broadcast_to(lines[pl.ds(3 * g + h, 1), :], (256, 1024))
        tbias[h] = pltpu.roll(row, 0, 1, stride=1, stride_axis=0)[:, 256:]

    def norm_block(m):
        rows = block(flip(z, m, 2))
        val = xrow[rows, :].astype(f32)
        h1[rows, :] = (val * inv_rms(val) * gains[12:13, :]).astype(bf16)

    arrived([xs[0]])
    norm_block(0)
    for m in (1, 2):
        arrived([xd[m]])
        xs[m] = hand_on(xrow, m)
    arrived([xs[1]])
    norm_block(1)
    arrived([xd[3]])
    xs[3] = hand_on(xrow, 3)
    md = spread(mem, mrow)
    own_m.wait()
    ms = {0: hand_on(mrow, 0)}
    arrived([xs[2]])
    norm_block(2)
    arrived([xs[3]])
    norm_block(3)

    arrived(sg_in)
    lane64 = lax.broadcasted_iota(jnp.int32, (128, 64), 1).astype(f32)
    inside = lane64 < 3.5
    for h in range(3):
        beyond = lax.broadcasted_iota(jnp.int32, (512, 128), 1) >= 64
        kh[h, 0:512, :] = jnp.where(beyond, -1.0, 0.0).astype(bf16)
        vh[h, 0:512, :] = jnp.zeros((512, 128), bf16)
    arrived(wA_in)
    W3_in[1] = send_W3(1)
    W3_in[2] = send_W3(2)

    def project(i, carry):
        rows = block(i)
        res = dot(h1[rows, :], wA[:, 0:576]).astype(bf16)
        qa, ka = [], []
        for j in range(2):
            seg = sg[2 * i + j, 0:1, :].astype(f32)
            same = jnp.transpose(jnp.broadcast_to(seg, (128, 128)))[:, :64] == lane64
            qa.append(jnp.where(same, BIG, 0.0))
            ka.append(jnp.where(inside & jnp.logical_not(same), -1.0, 0.0))
        qa = jnp.concatenate(qa, axis=0).astype(bf16)
        ka = jnp.concatenate(ka, axis=0).astype(bf16)
        lower = pl.ds(pl.multiple_of(i * 256 + 512, 256), 256)
        for h in range(3):
            qv = (res[:, 64 * h : 64 * h + 64].astype(f32) * SCALE).astype(bf16)
            qh[h, rows, :] = jnp.concatenate([qv, qa], axis=1)
            kh[h, lower, :] = jnp.concatenate([res[:, 192 + 64 * h : 256 + 64 * h], ka], axis=1)
            vh[h, lower, :] = pad64(res[:, 384 + 64 * h : 448 + 64 * h])
        return carry

    lax.fori_loop(0, 4, project, 0)

    for cp in own_gu:
        cp.wait()
    gu_in = [push(wgu.at[mine], wgu.at[mine], dpk(k)) for k in (1, 2, 3)]

    def window(b):
        return pl.ds(pl.multiple_of(b * 256, 256), 768)

    a_in = []
    for k in (2, 3, 1, 0):
        b = flip(g, k, 2)
        parts = []
        for h in range(3):
            p = softmax(dot_nt(qh[h, block(b), :], kh[h, window(b), :]) + tbias[h])
            p_self[h, b] = p
            parts.append(dot(p, vh[h, window(b), :])[:, :64].astype(bf16))
        if k == 0:
            pack(arecv, g, parts)
        else:
            pack(opack, b, parts)
            a_in.append(push(opack.at[b], arecv.at[g], seqk(k)))

    own_dn.wait()
    dn_in = [push(wd.at[mine_d], wd.at[mine_d], dpk(k)) for k in (1, 2, 3)]
    for m in (1, 2, 3):
        arrived([md[m]])
        ms[m] = hand_on(mrow, m)
    halves = [cotb.at[c, pl.ds(c * 128, 128)]] * 2
    dests = [4 * rr + z for rr in range(2)]
    cslot = lax.rem(z, 2)
    cot_recv, cot_sent = moved(
        [cot.at[0], cot.at[1]], [cotb.at[cslot, pl.ds(c * 128, 128)]] * 2, dests, c
    )
    W3_sib[0] = share_W3(0, W3_in[0])
    arrived(ms.values())

    def project_memory(i, carry):
        rows = block(i)
        res = dot(mrow[rows, :], wA[:, 576:960]).astype(bf16)
        for h in range(3):
            mkv[h, rows, :] = jnp.concatenate(
                [res[:, 64 * h : 64 * h + 64], res[:, 192 + 64 * h : 256 + 64 * h]], axis=1
            )
        return carry

    lax.fori_loop(0, 4, project_memory, 0)
    W3_sib[1] = share_W3(1, W3_in[1])

    arrived(a_in)
    assemble(arecv, attn)
    arrived(W3_sib[0])
    alive = live[r].astype(f32)
    res = xrow[block(g), :].astype(f32) + alive * dot(attn[...], W3[0])
    after_self[...] = res
    h2[...] = (res * inv_rms(res) * gains[13:14, :]).astype(bf16)
    arrived(W3_sib[1])
    disperse((dot(h2[...], W3[1]).astype(bf16).astype(f32) * SCALE).astype(bf16), qpack)
    q_in = {k: push(qpack.at[flip(g, k, 2)], qrecv.at[g], seqk(k)) for k in (2, 3, 1)}
    qrecv[g] = qpack[g]
    W3_sib[2] = share_W3(2, W3_in[2])
    cot_recv([cotb.at[c, pl.ds(0, 128)], cotb.at[c, pl.ds(128, 128)]])
    cot_sib = push(cotb.at[c], cotb.at[c], seqk(1))

    sent(a_in)
    c_in = []
    for k in (0, 1, 2, 3):
        b = flip(g, k, 2)
        if k:
            arrived([q_in[k]])
        qs = unpack(qrecv, b)
        parts = []
        for h in range(3):
            p = softmax(dot_nt(pad64(qs[h]), mkv[h]))
            p_cross[h, b] = p
            parts.append(dot(p, mkv[h])[:, 64:].astype(bf16))
        if k == 0:
            pack(crecv, g, parts)
        else:
            pack(opack, b, parts)
            c_in.append(push(opack.at[b], crecv.at[g], seqk(k)))
    arrived(W3_sib[2])
    arrived(c_in)
    assemble(crecv, cattn)
    res = after_self[...] + alive * dot(cattn[...], W3[2])
    after_cross[...] = res
    h3[c] = (res * inv_rms(res) * gains[14:15, :]).astype(bf16)
    h3_in = push(h3.at[c], h3.at[c], seqk(1))
    arrived([cot_sib])
    arrived(gu_in)
    arrived(dn_in)
    arrived([h3_in])

    def feed_forward(i, carry):
        t, n = lax.div(i, 4), lax.rem(i, 4)
        cols, more = block(n), pl.ds(pl.multiple_of(1024 + n * 256, 256), 256)
        gate = dot(h3[t], wgu[:, cols])
        up = dot(h3[t], wgu[:, more])
        act, slope = gelu_parts(gate)
        prod[t, :, cols] = (act * up).astype(bf16)
        down_in = (cotb[t].astype(f32) * alive).astype(bf16)
        gp = dot_nt(down_in, wd[cols, :])
        dgu[t, :, cols] = (gp * up * slope).astype(bf16)
        dgu[t, :, more] = (gp * act).astype(bf16)
        return carry

    lax.fori_loop(0, 8, feed_forward, 0)

    hpart[...] = dot_nt(dgu[1 - c], wgu[...]).astype(bf16)
    h_in = push(hpart, hrecv, seqk(1))
    hown[...] = dot_nt(dgu[c], wgu[...])
    fpart[...] = dot(prod[1 - c], wd[...]).astype(bf16)
    f_in = push(fpart, frecv, seqk(1))
    arrived([h_in])
    dv, dgain3 = norm_back(after_cross[...], gains[14:15, :], hown[...] + hrecv[...].astype(f32))
    gsm[...] = jnp.zeros((16, 768), f32)
    gsm[14:15, :] = dgain3
    grad[...] = cotb[c].astype(f32) + dv
    low[0] = (grad[...] * alive).astype(bf16)
    sent(c_in)
    sent(q_in.values())
    disperse(dot_nt(low[0], W3[2]).astype(bf16), opack)
    d_in = {k: push(opack.at[flip(g, k, 2)], drecv.at[g], seqk(k)) for k in (2, 3, 1)}
    drecv[g] = opack[g]

    fown[...] = dot(prod[c], wd[...])
    arrived([f_in])
    sent([f_in])
    outb[...] = (after_cross[...] + alive * (fown[...] + frecv[...].astype(f32))).astype(bf16)
    back = [2 * g + j for j in range(2)]
    out_recv, out_sent = moved([outb.at[pl.ds(0, 128)], outb.at[pl.ds(128, 128)]], [out.at[r]] * 2, back, r)

    sent(gu_in)
    sent(dn_in)

    def grad_gu(n, carry):
        cols = block(n)
        wgu[:, cols] = dot_tn(h3[...].reshape(512, 768), dgu[:, :, cols].reshape(512, 256)).astype(bf16)
        return carry

    lax.fori_loop(0, 8, grad_gu, 0)
    gu_back = [push(wgu.at[pl.ds(flip(d, k, 2) * 192, 192)], gur.at[k - 1], dpk(k)) for k in (1, 2, 3)]

    def grad_dn(n, carry):
        cols = block(n)
        down_in = (cotb[...].astype(f32) * alive).astype(bf16).reshape(512, 768)
        wd[cols, :] = dot_tn(prod[:, :, cols].reshape(512, 256), down_in).astype(bf16)
        return carry

    lax.fori_loop(0, 4, grad_dn, 0)
    dn_back = [push(wd.at[block(flip(d, k, 2))], dnr.at[k - 1], dpk(k)) for k in (1, 2, 3)]

    for h in range(3):
        acc[h, 0:1024, :] = jnp.zeros((1024, 128), f32)
    dq_in = []
    for k in (2, 3, 1, 0):
        b = flip(g, k, 2)
        if k:
            arrived([d_in[k]])
        dos, qs = unpack(drecv, b), unpack(qrecv, b)
        parts = []
        for h in range(3):
            p = p_cross[h, b]
            do = above64(dos[h])
            dp = dot_nt(do, mkv[h])
            pf = p.astype(f32)
            ds = (pf * (dp - jnp.sum(dp * pf, axis=-1, keepdims=True))).astype(bf16)
            parts.append((dot(ds, mkv[h])[:, :64] * SCALE).astype(bf16))
            acc[h, 0:1024, :] += dot_tn(ds, pad64(qs[h])) + dot_tn(p, do)
        if k == 0:
            pack(dqrecv, g, parts)
        else:
            pack(qpack, b, parts)
            dq_in.append(push(qpack.at[b], dqrecv.at[g], seqk(k)))

    def keep_memory(i, carry):
        rows = block(i)
        vals = [acc[h, rows, :][:, :64] for h in range(3)] + [acc[h, rows, :][:, 64:] for h in range(3)]
        dqkv[rows, 0:384] = jnp.concatenate(vals, axis=1).astype(bf16)
        return carry

    lax.fori_loop(0, 4, keep_memory, 0)
    arrived(dq_in)
    assemble(dqrecv, dcq)
    dv, dgain2 = norm_back(after_self[...], gains[13:14, :], dot_nt(dcq[...], W3[1]))
    gsm[13:14, :] = dgain2
    grad[...] += dv
    sent([h_in])
    low[1] = (grad[...] * alive).astype(bf16)
    sent(d_in.values())
    disperse(dot_nt(low[1], W3[0]).astype(bf16), opack)
    s_in = {k: push(opack.at[flip(g, k, 2)], srecv.at[g], seqk(k)) for k in (2, 3, 1)}
    srecv[g] = opack[g]

    b_sib = []
    lefts = (attn, h2, cattn)
    rights = (low.at[1], dcq, low.at[0])
    for i in (2, 1, 0):
        sent(W3_in[i])
        sent(W3_sib[i])
        W3[i] = dot_tn(lefts[i][...], rights[i][...]).astype(bf16)
        b_sib.append([push(W3.at[i, half_rows(q, 1 - c)], bsib.at[i, q], seqk(1)) for q in range(4)])

    def reduce_rows(compute, first, second, total):
        part3 = compute(flip(g, 3, 2))
        in3 = push(part3, first.at[0], seqk(1))
        part2 = compute(flip(g, 2, 2))
        part1 = compute(flip(g, 1, 2))
        in1 = push(part1, first.at[1], seqk(1))
        arrived([in3])
        part2[...] = (part2[...].astype(f32) + first[0].astype(f32)).astype(bf16)
        far = push(part2, second, seqk(2))
        part0 = compute(g)
        arrived([in1])
        total[...] = part0[...].astype(f32) + first[1].astype(f32)
        return far

    sent(wA_in)
    for i in range(3):
        keep[i, :, 0:384] = dot_tn(mrow[:, 256 * i : 256 * i + 256], dqkv[:, 0:384]).astype(bf16)

    def memory_part(b):
        mrow[block(b), :] = dot_nt(dqkv[block(b), 0:384], wA[:, 576:960]).astype(bf16)
        return mrow.at[block(b)]

    sent(ms.values())
    m_far = reduce_rows(memory_part, rt1, rt2, tot)

    b_dp = {}
    for n, i in enumerate((2, 1, 0)):
        arrived(b_sib[n])
        for q in range(4):
            rows = half_rows(q, c)
            W3[i, rows, :] = (W3[i, rows, :].astype(f32) + bsib[i, q].astype(f32)).astype(bf16)
        b_dp[i] = [push(W3.at[i, half_rows(flip(d, k, 2), c)], bdp.at[i, k - 1], dpk(k)) for k in (1, 2, 3)]

    for i in range(3):
        wA[256 * i : 256 * i + 256, 576:960] = keep[i, :, 0:384]
    arrived([m_far])
    out_recv([out.at[0], out.at[1]])
    out_sent()
    outb[...] = (tot[...] + rt2[...].astype(f32)).astype(bf16)
    mem_recv, mem_sent = moved([outb.at[pl.ds(0, 128)], outb.at[pl.ds(128, 128)]], [gmem.at[r]] * 2, back, r)

    for h in range(3):
        acc[h] = jnp.zeros((1536, 128), f32)
        tbias[h] = jnp.zeros((256, 768), f32)
    for k in (0, 1, 2, 3):
        b = flip(g, k, 2)
        if k:
            arrived([s_in[k]])
        dos = unpack(srecv, b)
        for h in range(3):
            p = p_self[h, b]
            do = pad64(dos[h])
            dp = dot_nt(do, vh[h, window(b), :])
            pf = p.astype(f32)
            ds = pf * (dp - jnp.sum(dp * pf, axis=-1, keepdims=True))
            tbias[h] += ds
            ds = ds.astype(bf16)
            dqkv[block(b), 64 * h : 64 * h + 64] = (dot(ds, kh[h, window(b), :])[:, :64] * SCALE).astype(bf16)
            acc[h, window(b), :] += dot_tn(ds, pad64(qh[h, block(b), :][:, :64])) + dot_tn(p, above64(dos[h]))

    def keep_self(i, carry):
        rows, lower = block(i), pl.ds(pl.multiple_of(i * 256 + 512, 256), 256)
        for h in range(3):
            dqkv[rows, 192 + 64 * h : 256 + 64 * h] = acc[h, lower, :][:, :64].astype(bf16)
            dqkv[rows, 384 + 64 * h : 448 + 64 * h] = acc[h, lower, :][:, 64:].astype(bf16)
        return carry

    lax.fori_loop(0, 4, keep_self, 0)

    own_tokens = xrow[block(g), :]
    xown[...] = own_tokens.astype(f32)
    sent([*xs.values()])

    def self_part(b):
        xrow[block(b), :] = dot_nt(dqkv[block(b), :], wA[:, 0:576]).astype(bf16)
        return xrow.at[block(b)]

    x_far = reduce_rows(self_part, rs1, rs2, after_self)

    def grad_qkv(n, carry):
        cols = pl.ds(pl.multiple_of(n * 128, 128), 128)
        wA[cols, 0:576] = dot_tn(h1[:, cols], dqkv[...]).astype(bf16)
        return carry

    lax.fori_loop(0, 6, grad_qkv, 0)
    c_dp = [push(wA.at[pl.ds(flip(d, k, 2) * 192, 192)], cdp.at[k - 1], dpk(k)) for k in (1, 2, 3)]

    for h in range(3):
        wide = jnp.concatenate([jnp.zeros((256, 256), f32), tbias[h]], axis=1)
        rows = lax.broadcasted_iota(jnp.int32, (256, 1024), 0)
        for i in range(8):
            bit = lax.rem(lax.div(rows, 1 << i), 2) == 1
            wide = jnp.where(bit, pltpu.roll(wide, 1024 - (1 << i), 1), wide)
        row = jnp.sum(wide, axis=0, keepdims=True)
        lines[h : h + 1, :] = row
    val = lines[...]
    top = val.astype(bf16)
    rest = val - top.astype(f32)
    mid = rest.astype(bf16)
    last = (rest - mid.astype(f32)).astype(bf16)
    by_bucket = dot_nt(top, hot[...]) + dot_nt(mid, hot[...]) + dot_nt(last, hot[...])
    row16 = lax.broadcasted_iota(jnp.int32, (16, 128), 0)
    spot = jnp.zeros((16, 128), f32)
    for h in range(3):
        spot = jnp.where(row16 == 3 * g + h, jnp.broadcast_to(by_bucket[h : h + 1, :], (16, 128)), spot)
    gsm[:, 0:128] += spot

    def summed(ref, rows, got, n):
        val = ref[rows, :].astype(f32)
        for k in range(n):
            val += got[k].astype(f32)
        ref[rows, :] = val.astype(bf16)

    def z_half(full, height, first):
        keep, give = lax.rem(z, 2), 1 - lax.rem(z, 2)
        n = height // 2
        cp = push(full.at[pl.ds(give * n, n)], first, seqk(2))
        return cp, full.at[pl.ds(keep * n, n)]

    base_gu, base_dn = d * 192, d * 256
    arrived(gu_back)
    summed(wgu, mine, gur, 3)
    half = lax.rem(z, 2)
    quarter = lax.div(z, 2)

    def at_rows(base, n, i):
        return pl.ds(pl.multiple_of(base + n * i, 16), n)

    def add(ref, rows, got):
        ref[rows, :] = (ref[rows, :].astype(f32) + got[...].astype(f32)).astype(bf16)

    gu1 = push(wgu.at[at_rows(base_gu, 96, 1 - half)], zg1, seqk(2))
    arrived(dn_back)
    summed(wd, mine_d, dnr, 3)
    dn1 = push(wd.at[at_rows(base_dn, 128, 1 - half)], zd1, seqk(2))
    arrived([gu1])
    add(wgu, at_rows(base_gu, 96, half), zg1)
    gu2 = push(wgu.at[at_rows(base_gu + 96 * half, 48, 1 - quarter)], zg2, seqk(4))
    arrived([dn1])
    add(wd, at_rows(base_dn, 128, half), zd1)
    dn2 = push(wd.at[at_rows(base_dn + 128 * half, 64, 1 - quarter)], zd2, seqk(4))

    for i in (2, 1, 0):
        arrived(b_dp[i])
        rows = half_rows(d, c)
        val = W3[i, rows, :].astype(f32)
        for k in range(3):
            val += bdp[i, k].astype(f32)
        W3[i, rows, :] = val.astype(bf16)
    base_b = d * 192 + c * 96
    b1 = [push(W3.at[i, at_rows(base_b, 48, 1 - half)], zb1.at[i], seqk(2)) for i in range(3)]

    arrived([gu2])
    q_rows = at_rows(base_gu + 96 * half, 48, quarter)
    add(wgu, q_rows, zg2)
    gu_place = o_gu.at[c, at_rows(96 * half, 48, quarter)]
    gu_own = local(wgu.at[q_rows], gu_place)
    gu3 = push(wgu.at[q_rows], gu_place, seqk(4))
    arrived([dn2])
    dq_rows = at_rows(base_dn + 128 * half, 64, quarter)
    add(wd, dq_rows, zd2)
    dn_place = o_dn.at[c, at_rows(128 * half, 64, quarter)]
    dn_own = local(wd.at[dq_rows], dn_place)
    dn3 = push(wd.at[dq_rows], dn_place, seqk(4))

    b2 = []
    b_cols = [pl.ds(pl.multiple_of(q * 384, 128), 384) for q in (quarter, 1 - quarter)]
    kept = at_rows(base_b, 48, half)
    for i in range(3):
        arrived([b1[i]])
        W3[i, kept, :] = (W3[i, kept, :].astype(f32) + zb1[i].astype(f32)).astype(bf16)
        b2.append(push(W3.at[i, kept, b_cols[1]], zb2.at[i], seqk(4)))

    arrived([x_far])
    dv, dgain1 = norm_back(xown[...], gains[12:13, :], after_self[...] + rs2[...].astype(f32))
    gsm[12:13, :] = dgain1
    sm_dp = [push(gsm, sm1.at[k - 1], dpk(k)) for k in (1, 2, 3)]
    mem_recv([gmem.at[0], gmem.at[1]])
    mem_sent()
    outb[...] = (grad[...] + dv).astype(bf16)
    gin_recv, gin_sent = moved([outb.at[pl.ds(0, 128)], outb.at[pl.ds(128, 128)]], [gin.at[r]] * 2, back, r)

    arrived(c_dp)
    val = wA[mine, :].astype(f32)
    for k in range(3):
        val += cdp[k].astype(f32)
    wA[mine, :] = val.astype(bf16)
    c_far = push(wA.at[mine], cfar, seqk(4))

    arrived([gu3])
    gu_own.wait()
    half_gu = o_gu.at[c, at_rows(0, 96, half)]
    gu4 = push(half_gu, half_gu, seqk(2))
    arrived([dn3])
    dn_own.wait()
    half_dn = o_dn.at[c, at_rows(0, 128, half)]
    dn4 = push(half_dn, half_dn, seqk(2))
    b3, b_own = [], []
    for i in range(3):
        arrived([b2[i]])
        W3[i, kept, b_cols[0]] = (W3[i, kept, b_cols[0]].astype(f32) + zb2[i].astype(f32)).astype(bf16)
        place = o_b.at[i, c, at_rows(0, 48, half), b_cols[0]]
        b_own.append(local(W3.at[i, kept, b_cols[0]], place))
        b3.append(push(W3.at[i, kept, b_cols[0]], place, seqk(4)))
    b4 = []
    for i in range(3):
        arrived([b3[i]])
        b_own[i].wait()
        place = o_b.at[i, c, at_rows(0, 48, half)]
        b4.append(push(place, place, seqk(2)))

    arrived(sm_dp)
    sent(sm_dp)
    gsm[...] = gsm[...] + sm1[0] + sm1[1] + sm1[2]
    sm_seq = [push(gsm, sm2.at[k - 1], seqk(k)) for k in range(1, 8)]

    arrived([c_far])
    sent([c_far])
    wA[mine, :] = (wA[mine, :].astype(f32) + cfar[...].astype(f32)).astype(bf16)
    stores = [local(wA.at[mine], o_c.at[g])]
    c_pair = push(wA.at[mine], o_c.at[g], seqk(2))
    c_s1 = push(wA.at[mine], o_c.at[g], seqk(1))

    arrived([gu4])
    gu5 = push(o_gu.at[c], o_gu.at[c], seqk(1))
    arrived([dn4])
    dn5 = push(o_dn.at[c], o_dn.at[c], seqk(1))
    arrived(b4)
    b5 = [push(o_b.at[i, c], o_b.at[i, c], seqk(1)) for i in range(3)]
    arrived([c_pair])
    c_s2 = push(o_c.at[flip(g, 2, 2)], o_c.at[flip(g, 2, 2)], seqk(1))

    arrived(sm_seq)
    val = gsm[...]
    for k in range(7):
        val = val + sm2[k]
    o_small[...] = val
    arrived([c_s1, gu5, dn5, *b5, c_s2])
    gin_recv([gin.at[0], gin.at[1]])
    gin_sent()
    cot_sent()
    for cp in stores:
        cp.wait()
    for cp in list(flying):
        cp.wait_send()


def scratch():
    def vm(kind, *shape):
        return pltpu.VMEM(shape, kind)

    return dict(
        xrow=vm(bf16, 1024, 768),
        mrow=vm(bf16, 1024, 768),
        h1=vm(bf16, 1024, 768),
        wA=vm(bf16, 768, 960),
        W3=vm(bf16, 3, 768, 768),
        wgu=vm(bf16, 768, 2048),
        wd=vm(bf16, 1024, 768),
        sm=vm(bf16, 4, 16, 768),
        sg=vm(bf16, 8, 16, 128),
        gains=vm(f32, 16, 768),
        lines=vm(f32, 16, 1024),
        hot=vm(bf16, 128, 1024),
        tbias=vm(f32, 3, 256, 768),
        qh=vm(bf16, 3, 1024, 128),
        kh=vm(bf16, 3, 1536, 128),
        vh=vm(bf16, 3, 1536, 128),
        mkv=vm(bf16, 3, 1024, 128),
        p_self=vm(bf16, 3, 4, 256, 768),
        p_cross=vm(bf16, 3, 4, 256, 1024),
        opack=vm(bf16, 4, 384, 128),
        arecv=vm(bf16, 4, 384, 128),
        attn=vm(bf16, 256, 768),
        qpack=vm(bf16, 4, 384, 128),
        qrecv=vm(bf16, 4, 384, 128),
        crecv=vm(bf16, 4, 384, 128),
        cattn=vm(bf16, 256, 768),
        after_self=vm(f32, 256, 768),
        after_cross=vm(f32, 256, 768),
        h2=vm(bf16, 256, 768),
        h3=vm(bf16, 2, 256, 768),
        prod=vm(bf16, 2, 256, 1024),
        dgu=vm(bf16, 2, 256, 2048),
        cotb=vm(bf16, 2, 256, 768),
        frecv=vm(bf16, 256, 768),
        hrecv=vm(bf16, 256, 768),
        outb=vm(bf16, 256, 768),
        grad=vm(f32, 256, 768),
        low=vm(bf16, 2, 256, 768),
        dcq=vm(bf16, 256, 768),
        acc=vm(f32, 3, 1536, 128),
        dqkv=vm(bf16, 1024, 576),
        rs1=vm(bf16, 2, 256, 768),
        rs2=vm(bf16, 256, 768),
        rt1=vm(bf16, 2, 256, 768),
        rt2=vm(bf16, 256, 768),
        gur=vm(bf16, 3, 192, 2048),
        dnr=vm(bf16, 3, 256, 768),
        bsib=vm(bf16, 3, 4, 96, 768),
        bdp=vm(bf16, 3, 3, 96, 768),
        cdp=vm(bf16, 3, 192, 960),
        zg1=vm(bf16, 96, 2048),
        zg2=vm(bf16, 48, 2048),
        zd1=vm(bf16, 128, 768),
        zd2=vm(bf16, 64, 768),
        zb1=vm(bf16, 3, 48, 768),
        zb2=vm(bf16, 3, 48, 384),
        cfar=vm(bf16, 192, 960),
        gsm=vm(f32, 16, 768),
        sm1=vm(f32, 3, 16, 768),
        sm2=vm(f32, 7, 16, 768),
        sgown=vm(bf16, 2, 16, 128),
        ssem=pltpu.SemaphoreType.DMA((N_SEM,)),
        rsem=pltpu.SemaphoreType.DMA((N_SEM,)),
        lsem=pltpu.SemaphoreType.DMA((N_LOCAL,)),
    )


def finish_kernel(
    out, gin, gmem, o_gu, o_dn, o_b, o_c, o_small,
    y_out, y_gin, y_gmem, y_g1, y_qkv, y_ao, y_rel, y_g2, y_cq, y_kv, y_co, y_g3, y_gu, y_dn, rel_t,
):
    d = lax.axis_index("dp")
    y_out[...] = out[...]
    y_gin[...] = gin[...]
    y_gmem[...] = gmem[...]
    for half in range(2):
        for q in range(4):
            for c in range(2):
                at = 2048 * half + 512 * q + 256 * c
                y_gu[:, at : at + 256] = o_gu[c, :, 1024 * half + 256 * q : 1024 * half + 256 * q + 256].astype(f32)
    y_dn[...] = o_dn[...].astype(f32)
    for i, y in enumerate((y_ao, y_cq, y_co)):
        y[...] = o_b[i, 0].astype(f32)
    for p in range(5):
        y, at = (y_qkv, 768 * p) if p < 3 else (y_kv, 768 * (p - 3))
        for t in range(2):
            two = [o_c[2 * t + j, :, 192 * p : 192 * p + 192].astype(f32) for j in range(2)]
            y[:, at + 384 * t : at + 384 * t + 384] = jnp.concatenate(two, axis=1)
    for i, y in enumerate((y_g1, y_g2, y_g3)):
        line = o_small[12 + i : 13 + i, :]
        val = line[:, 0:192]
        for q in range(1, 4):
            val = jnp.where(d == q, line[:, 192 * q : 192 * q + 192], val)
        y[...] = val
    rel_t[...] = jnp.transpose(o_small[:, 0:128])
    y_rel[...] = rel_t[pl.ds(pl.multiple_of(8 * d, 8), 8), 0:12]


def per_device_kernel(
    inputs, memory, cotangent, segment_ids, row_live, buckets, gain_self, w_qkv, w_attn_out, rel_bias, gain_cross,
    c_query, c_keyval, c_out, gain_ff, w_gate_up, w_down,
):
    anywhere = pl.BlockSpec(memory_space=pl.ANY)
    vmem = pl.BlockSpec(memory_space=pltpu.VMEM)
    smem = pl.BlockSpec(memory_space=pltpu.SMEM)
    shapes = (
        ((2, 128, 768), bf16), ((2, 128, 768), bf16), ((2, 128, 768), bf16),
        ((2, 192, 2048), bf16), ((2, 256, 768), bf16), ((3, 2, 96, 768), bf16), ((4, 192, 960), bf16),
        ((16, 768), f32),
    )
    parts = pl.pallas_call(
        layer_kernel,
        out_shape=[jax.ShapeDtypeStruct(*sh) for sh in shapes],
        in_specs=[anywhere] * 3 + [vmem] * 6 + [smem] + [anywhere] * 7,
        out_specs=[anywhere] * 7 + [vmem],
        scratch_shapes=scratch(),
        compiler_params=pltpu.CompilerParams(collective_id=0, has_side_effects=True, vmem_limit_bytes=66500000),
        name="layer",
    )(
        inputs, memory, cotangent, segment_ids, gain_self, gain_cross, gain_ff, rel_bias,
        buckets.reshape(8, 128), row_live, w_qkv, c_keyval, w_attn_out, c_query, c_out, w_gate_up, w_down,
    )
    act = pl.BlockSpec((1, 64, 768), lambda i: (i // 2, i % 2, 0))
    whole = pl.BlockSpec((16, 768), lambda i: (0, 0))

    def rows(n, width):
        return pl.BlockSpec((n, width), lambda i: (i, 0)), jax.ShapeDtypeStruct((4 * n, width), f32)

    line = pl.BlockSpec((1, 192), lambda i: (0, 0)), jax.ShapeDtypeStruct((1, 192), f32)
    square = rows(48, 768)
    tokens = act, jax.ShapeDtypeStruct((2, 128, 768), bf16)
    down = (
        pl.BlockSpec((2, 64, 768), lambda i: (0, i, 0)),
        jax.ShapeDtypeStruct((2, 256, 768), f32),
    )
    table = pl.BlockSpec((8, 12), lambda i: (0, 0)), jax.ShapeDtypeStruct((8, 12), f32)
    outs = (
        tokens, tokens, tokens, line, rows(48, 2304), square, table, line, square, rows(48, 1536), square, line,
        rows(48, 4096), down,
    )
    res = pl.pallas_call(
        finish_kernel,
        grid=(4,),
        out_shape=[o for _, o in outs],
        in_specs=[
            act, act, act,
            pl.BlockSpec((2, 48, 2048), lambda i: (0, i, 0)),
            pl.BlockSpec((2, 64, 768), lambda i: (0, i, 0)),
            pl.BlockSpec((3, 1, 48, 768), lambda i: (0, i // 2, i % 2, 0)),
            pl.BlockSpec((4, 48, 960), lambda i: (0, i, 0)),
            whole,
        ],
        out_specs=[b for b, _ in outs],
        scratch_shapes=[pltpu.VMEM((128, 16), f32)],
        compiler_params=pltpu.CompilerParams(vmem_limit_bytes=66500000),
        name="finish",
    )(*parts)
    res = list(res)
    for i in (3, 7, 11):
        res[i] = res[i].reshape(192)
    res[13] = res[13].reshape(512, 768)
    return tuple(res)


def solution(mesh):
    in_specs = (
        P("dp", "seq", None),
        P("dp", "seq", None),
        P("dp", "seq", None),
        P("dp", "seq"),
        P("dp"),
        P(),
        P("dp"),
        P("dp", None),
        P("dp", None),
        P("dp", None),
        P("dp"),
        P("dp", None),
        P("dp", None),
        P("dp", None),
        P("dp"),
        P("dp", None),
        P("dp", None),
    )
    out_specs = (
        P("dp", "seq", None),
        P("dp", "seq", None),
        P("dp", "seq", None),
        P("dp"),
        P("dp", None),
        P("dp", None),
        P("dp", None),
        P("dp"),
        P("dp", None),
        P("dp", None),
        P("dp", None),
        P("dp"),
        P("dp", None),
        P("dp", None),
    )
    fits = dict(mesh.shape) == {"dp": 4, "seq": 8}
    return jax.shard_map(
        per_device_kernel if fits else per_device, mesh=mesh, in_specs=in_specs, out_specs=out_specs, check_vma=False
    )
```

```python
import jax
import jax.numpy as jnp
from jax import lax
from jax.experimental import pallas as pl
from jax.experimental.pallas import tpu as pltpu
from jax.sharding import PartitionSpec as P

D = 768
HEADS = 12
HEAD_DIM = 64
FF = 2048
BUCKETS = 32
LEN = 1024
MEM = 1024


epsilon = 1e-06
masked_score = -1000000000.0
highest = lax.Precision.HIGHEST


def rms_norm(values, gain):
    return values * lax.rsqrt(jnp.mean(values * values, axis=-1, keepdims=True) + epsilon) * gain


def matmul(left, right, form):
    return jnp.einsum(form, left, right, preferred_element_type=jnp.float32)


def softmax_parts(scores):
    top = jnp.max(scores, axis=-1, keepdims=True)
    expo = jnp.exp(scores - top)
    total = jnp.sum(expo, axis=-1, keepdims=True)
    return (expo / total, (top + jnp.log(total))[..., 0])


def score_grads(scores, lse_row, value_row, grad_row):
    probs = jnp.exp(scores - lse_row[..., None])
    grad_probs = matmul(grad_row, value_row, "qhd,khd->hqk")
    centre = jnp.sum(grad_probs * probs, axis=-1, keepdims=True)
    grad_scores = (probs * (grad_probs - centre)).astype(jnp.bfloat16)
    return (probs, grad_scores, centre[..., 0])


def one_hot_of(buckets):
    return (buckets[:, None] == jnp.arange(BUCKETS, dtype=jnp.int32)).astype(jnp.float32)


def skewed(by_dist, start, rows):
    table = jnp.concatenate([jnp.zeros((LEN - 1, HEADS), by_dist.dtype), by_dist], axis=0)
    window = lax.dynamic_slice_in_dim(table, start, rows + LEN - 1, axis=0)
    line = jnp.pad(window[::-1].T, ((0, 0), (0, 1)))
    width = rows + LEN
    flat = jnp.broadcast_to(line[:, None, :], (HEADS, rows, width)).reshape(HEADS, rows * width)
    return flat[:, : rows * (width - 1)].reshape(HEADS, rows, width - 1)[:, :, rows - 1 :]


def unskewed(block, start, rows):
    width = rows + LEN
    wide = jnp.pad(block, ((0, 0), (0, 0), (rows - 1, 0))).reshape(HEADS, rows * (width - 1))
    line = jnp.sum(jnp.pad(wide, ((0, 0), (0, rows))).reshape(HEADS, rows, width), axis=1)
    window = line[:, : width - 1][:, ::-1].T
    table = jnp.zeros((2 * LEN - 1, HEADS), block.dtype)
    return lax.dynamic_update_slice_in_dim(table, window, start, axis=0)[LEN - 1 :]


def per_device(
    inputs,
    memory,
    cotangent,
    segment_ids,
    row_live,
    buckets,
    gain_self,
    w_qkv,
    w_attn_out,
    rel_bias,
    gain_cross,
    c_query,
    c_keyval,
    c_out,
    gain_ff,
    w_gate_up,
    w_down,
):
    (
        g_self,
        qkv_full,
        out_full,
        bias_full,
        g_cross,
        cq_full,
        ckv_full,
        cout_full,
        g_ffn,
        gu_full,
        down_full,
    ) = (
        lax.all_gather(gain_self, "dp", axis=0, tiled=True),
        lax.all_gather(w_qkv, "dp", axis=0, tiled=True),
        lax.all_gather(w_attn_out, "dp", axis=0, tiled=True),
        lax.all_gather(rel_bias, "dp", axis=0, tiled=True),
        lax.all_gather(gain_cross, "dp", axis=0, tiled=True),
        lax.all_gather(c_query, "dp", axis=0, tiled=True),
        lax.all_gather(c_keyval, "dp", axis=0, tiled=True),
        lax.all_gather(c_out, "dp", axis=0, tiled=True),
        lax.all_gather(gain_ff, "dp", axis=0, tiled=True),
        lax.all_gather(w_gate_up, "dp", axis=0, tiled=True),
        lax.all_gather(w_down, "dp", axis=0, tiled=True),
    )
    num_rows, local_len, _ = inputs.shape
    seq_index = lax.axis_index("seq")
    scale = HEAD_DIM ** (-0.5)
    dense = inputs.astype(jnp.float32)
    live_rows = row_live.astype(jnp.float32)[:, None, None]
    normed_one = rms_norm(dense, g_self.astype(jnp.float32))
    hidden_one = normed_one.astype(jnp.bfloat16)
    qkv_local = matmul(hidden_one, qkv_full, "rcd,de->rce").astype(jnp.bfloat16)
    queries = qkv_local[..., :D]
    key_value = qkv_local[..., D:]
    seg_local = segment_ids.astype(jnp.bfloat16)
    key_all, seg_all = (
        lax.all_gather(key_value, "seq", axis=1, tiled=True),
        lax.all_gather(seg_local, "seq", axis=1, tiled=True),
    )
    positions = seq_index * local_len + jnp.arange(local_len, dtype=jnp.int32)
    offsets = positions[:, None] - jnp.arange(LEN, dtype=jnp.int32)[None, :]
    causal = offsets >= 0
    bucket_hot = one_hot_of(buckets)
    by_dist = jnp.einsum(
        "lb,bh->lh",
        bucket_hot,
        bias_full.astype(jnp.float32),
        precision=highest,
        preferred_element_type=jnp.float32,
    )
    bias_block = skewed(by_dist, seq_index * local_len, local_len)

    def self_scores(queries_h, key_row, seg_row, segk_row):
        raw = matmul(queries_h, key_row, "qhd,khd->hqk") * scale + bias_block
        allowed = causal & (seg_row[:, None] == segk_row[None, :])
        return jnp.where(allowed[None], raw, masked_score)

    def self_forward(items):
        query_row, kv_row, seg_row, segk_row = items
        key_row = kv_row[:, :D].reshape(LEN, HEADS, HEAD_DIM)
        value_row = kv_row[:, D:].reshape(LEN, HEADS, HEAD_DIM)
        scores = self_scores(
            query_row.reshape(local_len, HEADS, HEAD_DIM), key_row, seg_row, segk_row
        )
        probs, lse_row = softmax_parts(scores)
        mixed = matmul(probs.astype(jnp.bfloat16), value_row, "hqk,khd->qhd")
        return (mixed.reshape(local_len, D), lse_row)

    attn_self, lse_self = lax.map(self_forward, (queries, key_all, seg_local, seg_all))
    attn_low = attn_self.astype(jnp.bfloat16)
    branch_one = matmul(attn_low, out_full, "rcd,de->rce")
    after_self = dense + live_rows * branch_one
    normed_two = rms_norm(after_self, g_cross.astype(jnp.float32))
    hidden_two = normed_two.astype(jnp.bfloat16)
    cross_q = matmul(hidden_two, cq_full, "rcd,de->rce").astype(jnp.bfloat16)
    memory_kv = matmul(memory, ckv_full, "rmd,de->rme").astype(jnp.bfloat16)
    memory_all = lax.all_gather(memory_kv, "seq", axis=1, tiled=True)

    def cross_forward(items):
        query_row, kv_row = items
        key_row = kv_row[:, :D].reshape(MEM, HEADS, HEAD_DIM)
        value_row = kv_row[:, D:].reshape(MEM, HEADS, HEAD_DIM)
        scores = (
            matmul(query_row.reshape(local_len, HEADS, HEAD_DIM), key_row, "qhd,khd->hqk") * scale
        )
        probs, lse_row = softmax_parts(scores)
        mixed = matmul(probs.astype(jnp.bfloat16), value_row, "hqk,khd->qhd")
        return (mixed.reshape(local_len, D), lse_row)

    attn_cross, lse_cross = lax.map(cross_forward, (cross_q, memory_all))
    cross_low = attn_cross.astype(jnp.bfloat16)
    branch_two = matmul(cross_low, cout_full, "rcd,de->rce")
    after_cross = after_self + live_rows * branch_two
    normed_three = rms_norm(after_cross, g_ffn.astype(jnp.float32))
    hidden_three = normed_three.astype(jnp.bfloat16)
    gate_up = matmul(hidden_three, gu_full, "rcd,df->rcf")
    gate = gate_up[..., :FF]
    upward = gate_up[..., FF:]
    mixed_ff = (jax.nn.gelu(gate, approximate=True) * upward).astype(jnp.bfloat16)
    branch_three = matmul(mixed_ff, down_full, "rcf,fd->rcd")
    output = (after_cross + live_rows * branch_three).astype(jnp.bfloat16)
    (
        g_self,
        qkv_full,
        out_full,
        bias_full,
        g_cross,
        cq_full,
        ckv_full,
        cout_full,
        g_ffn,
        gu_full,
        down_full,
    ) = (
        lax.all_gather(gain_self, "dp", axis=0, tiled=True),
        lax.all_gather(w_qkv, "dp", axis=0, tiled=True),
        lax.all_gather(w_attn_out, "dp", axis=0, tiled=True),
        lax.all_gather(rel_bias, "dp", axis=0, tiled=True),
        lax.all_gather(gain_cross, "dp", axis=0, tiled=True),
        lax.all_gather(c_query, "dp", axis=0, tiled=True),
        lax.all_gather(c_keyval, "dp", axis=0, tiled=True),
        lax.all_gather(c_out, "dp", axis=0, tiled=True),
        lax.all_gather(gain_ff, "dp", axis=0, tiled=True),
        lax.all_gather(w_gate_up, "dp", axis=0, tiled=True),
        lax.all_gather(w_down, "dp", axis=0, tiled=True),
    )
    grad_out = cotangent.astype(jnp.float32)
    down_in = (live_rows * grad_out).astype(jnp.bfloat16)
    grad_down = matmul(mixed_ff, down_in, "rcf,rcd->fd")
    grad_mixed = matmul(down_in, down_full, "rcd,fd->rcf")
    _, gelu_pull = jax.vjp(
        lambda gate_in, up_in: jax.nn.gelu(gate_in, approximate=True) * up_in, gate, upward
    )
    grad_gate, grad_upward = gelu_pull(grad_mixed)
    grad_gu_low = jnp.concatenate([grad_gate, grad_upward], axis=-1).astype(jnp.bfloat16)
    grad_gate_up = matmul(hidden_three, grad_gu_low, "rcd,rcf->df")
    grad_normed_three = matmul(grad_gu_low, gu_full, "rcf,df->rcd")
    _, pull_three = jax.vjp(rms_norm, after_cross, g_ffn.astype(jnp.float32))
    part_three, grad_gain_ff = pull_three(grad_normed_three)
    grad_after_cross = grad_out + part_three
    cross_in = (live_rows * grad_after_cross).astype(jnp.bfloat16)
    grad_cout = matmul(cross_low, cross_in, "rcd,rce->de")
    grad_cross_attn = matmul(cross_in, cout_full, "rce,de->rcd").astype(jnp.bfloat16)

    def cross_backward(items):
        query_row, kv_row, lse_row, grad_row = items
        queries_h = query_row.reshape(local_len, HEADS, HEAD_DIM)
        grad_h = grad_row.reshape(local_len, HEADS, HEAD_DIM)
        key_row = kv_row[:, :D].reshape(MEM, HEADS, HEAD_DIM)
        value_row = kv_row[:, D:].reshape(MEM, HEADS, HEAD_DIM)
        scores = matmul(queries_h, key_row, "qhd,khd->hqk") * scale
        probs, grad_scores, centre = score_grads(scores, lse_row, value_row, grad_h)
        grad_query = matmul(grad_scores, key_row, "hqk,khd->qhd") * scale
        grad_key = matmul(grad_scores, queries_h, "hqk,qhd->khd") * scale
        grad_value = matmul(probs.astype(jnp.bfloat16), grad_h, "hqk,qhd->khd")
        kv_grads = jnp.concatenate([grad_key.reshape(MEM, D), grad_value.reshape(MEM, D)], axis=-1)
        return (grad_query.reshape(local_len, D), kv_grads, centre)

    grad_cq_rows, grad_memkv_full, _ = lax.map(
        cross_backward, (cross_q, memory_all, lse_cross, grad_cross_attn)
    )
    grad_memkv = lax.psum_scatter(
        grad_memkv_full.astype(jnp.bfloat16), "seq", scatter_dimension=1, tiled=True
    )
    grad_ckv = matmul(memory, grad_memkv, "rmd,rme->de")
    grad_memory = matmul(grad_memkv, ckv_full, "rme,de->rmd").astype(jnp.bfloat16)
    grad_cq_low = grad_cq_rows.astype(jnp.bfloat16)
    grad_cquery = matmul(hidden_two, grad_cq_low, "rcd,rce->de")
    grad_normed_two = matmul(grad_cq_low, cq_full, "rce,de->rcd")
    _, pull_two = jax.vjp(rms_norm, after_self, g_cross.astype(jnp.float32))
    part_two, grad_gain_cross = pull_two(grad_normed_two)
    grad_after_self = grad_after_cross + part_two
    self_in = (live_rows * grad_after_self).astype(jnp.bfloat16)
    grad_wout = matmul(attn_low, self_in, "rcd,rce->de")
    grad_self_attn = matmul(self_in, out_full, "rce,de->rcd").astype(jnp.bfloat16)

    def self_backward(carry, items):
        query_row, kv_row, seg_row, segk_row, lse_row, grad_row = items
        queries_h = query_row.reshape(local_len, HEADS, HEAD_DIM)
        grad_h = grad_row.reshape(local_len, HEADS, HEAD_DIM)
        key_row = kv_row[:, :D].reshape(LEN, HEADS, HEAD_DIM)
        value_row = kv_row[:, D:].reshape(LEN, HEADS, HEAD_DIM)
        scores = self_scores(queries_h, key_row, seg_row, segk_row)
        probs, grad_scores, centre = score_grads(scores, lse_row, value_row, grad_h)
        grad_query = matmul(grad_scores, key_row, "hqk,khd->qhd") * scale
        grad_key = matmul(grad_scores, queries_h, "hqk,qhd->khd") * scale
        grad_value = matmul(probs.astype(jnp.bfloat16), grad_h, "hqk,qhd->khd")
        kv_grads = jnp.concatenate([grad_key.reshape(LEN, D), grad_value.reshape(LEN, D)], axis=-1)
        return (
            carry + grad_scores.astype(jnp.float32),
            (grad_query.reshape(local_len, D), kv_grads, centre),
        )

    zero_block = jnp.zeros((HEADS, local_len, LEN), jnp.float32)
    score_total, (grad_q_rows, grad_kv_full, _) = lax.scan(
        self_backward, zero_block, (queries, key_all, seg_local, seg_all, lse_self, grad_self_attn)
    )
    grad_kv = lax.psum_scatter(
        grad_kv_full.astype(jnp.bfloat16), "seq", scatter_dimension=1, tiled=True
    )
    grad_bias = jnp.einsum(
        "lh,lb->bh",
        unskewed(score_total, seq_index * local_len, local_len),
        bucket_hot,
        precision=highest,
        preferred_element_type=jnp.float32,
    )
    grad_qkv_low = jnp.concatenate([grad_q_rows.astype(jnp.bfloat16), grad_kv], axis=-1)
    grad_wqkv = matmul(hidden_one, grad_qkv_low, "rcd,rce->de")
    grad_normed_one = matmul(grad_qkv_low, qkv_full, "rce,de->rcd")
    _, pull_one = jax.vjp(rms_norm, dense, g_self.astype(jnp.float32))
    part_one, grad_gain_self = pull_one(grad_normed_one)
    grad_inputs = (grad_after_self + part_one).astype(jnp.bfloat16)
    (
        own_gself,
        own_qkv,
        own_wout,
        own_bias,
        own_gcross,
        own_cquery,
        own_ckv,
        own_cout,
        own_gff,
        own_gateup,
        own_down,
    ) = (
        lax.psum_scatter(
            grad_gain_self.astype(jnp.bfloat16), "dp", scatter_dimension=0, tiled=True
        ).astype(jnp.float32),
        lax.psum_scatter(
            grad_wqkv.astype(jnp.bfloat16), "dp", scatter_dimension=0, tiled=True
        ).astype(jnp.float32),
        lax.psum_scatter(
            grad_wout.astype(jnp.bfloat16), "dp", scatter_dimension=0, tiled=True
        ).astype(jnp.float32),
        lax.psum_scatter(
            grad_bias.astype(jnp.bfloat16), "dp", scatter_dimension=0, tiled=True
        ).astype(jnp.float32),
        lax.psum_scatter(
            grad_gain_cross.astype(jnp.bfloat16), "dp", scatter_dimension=0, tiled=True
        ).astype(jnp.float32),
        lax.psum_scatter(
            grad_cquery.astype(jnp.bfloat16), "dp", scatter_dimension=0, tiled=True
        ).astype(jnp.float32),
        lax.psum_scatter(
            grad_ckv.astype(jnp.bfloat16), "dp", scatter_dimension=0, tiled=True
        ).astype(jnp.float32),
        lax.psum_scatter(
            grad_cout.astype(jnp.bfloat16), "dp", scatter_dimension=0, tiled=True
        ).astype(jnp.float32),
        lax.psum_scatter(
            grad_gain_ff.astype(jnp.bfloat16), "dp", scatter_dimension=0, tiled=True
        ).astype(jnp.float32),
        lax.psum_scatter(
            grad_gate_up.astype(jnp.bfloat16), "dp", scatter_dimension=0, tiled=True
        ).astype(jnp.float32),
        lax.psum_scatter(
            grad_down.astype(jnp.bfloat16), "dp", scatter_dimension=0, tiled=True
        ).astype(jnp.float32),
    )
    summed = (
        lax.psum(own_gself.astype(jnp.bfloat16), "seq").astype(jnp.float32),
        lax.psum(own_qkv.astype(jnp.bfloat16), "seq").astype(jnp.float32),
        lax.psum(own_wout.astype(jnp.bfloat16), "seq").astype(jnp.float32),
        lax.psum(own_bias.astype(jnp.bfloat16), "seq").astype(jnp.float32),
        lax.psum(own_gcross.astype(jnp.bfloat16), "seq").astype(jnp.float32),
        lax.psum(own_cquery.astype(jnp.bfloat16), "seq").astype(jnp.float32),
        lax.psum(own_ckv.astype(jnp.bfloat16), "seq").astype(jnp.float32),
        lax.psum(own_cout.astype(jnp.bfloat16), "seq").astype(jnp.float32),
        lax.psum(own_gff.astype(jnp.bfloat16), "seq").astype(jnp.float32),
        lax.psum(own_gateup.astype(jnp.bfloat16), "seq").astype(jnp.float32),
        lax.psum(own_down.astype(jnp.bfloat16), "seq").astype(jnp.float32),
    )
    return (
        output,
        grad_inputs,
        grad_memory,
        summed[0],
        summed[1],
        summed[2],
        summed[3],
        summed[4],
        summed[5],
        summed[6],
        summed[7],
        summed[8],
        summed[9],
        summed[10],
    )


f32, bf16 = jnp.float32, jnp.bfloat16
BIG = 1.0e9
SCALE = HEAD_DIM ** (-0.5)
MESH = pl.DeviceIdType.MESH
GELU_A, GELU_B = 0.7978845608028654, 0.044715
N_SEM, N_LOCAL = 232, 32


def flip(v, k, bits):
    for i in range(bits):
        if (k >> i) & 1:
            b = 1 << i
            v = v + b - 2 * b * lax.rem(lax.div(v, b), 2)
    return v


def dot(a, b):
    return lax.dot_general(a, b, (((1,), (0,)), ((), ())), preferred_element_type=f32)


def dot_nt(a, b):
    return lax.dot_general(a, b, (((1,), (1,)), ((), ())), preferred_element_type=f32)


def dot_tn(a, b):
    return lax.dot_general(a, b, (((0,), (0,)), ((), ())), preferred_element_type=f32)


def inv_rms(v):
    return lax.rsqrt(jnp.mean(v * v, axis=-1, keepdims=True) + epsilon)


def norm_back(v, gain, w):
    r = inv_rms(v)
    gw = gain * w
    mean = jnp.mean(gw * v, axis=-1, keepdims=True)
    return r * gw - v * (r * r * r * mean), jnp.sum(w * (v * r), axis=0, keepdims=True)


def gelu_parts(gate):
    sq = gate * gate
    th = jnp.tanh(GELU_A * gate * (1.0 + GELU_B * sq))
    half = 0.5 * (1.0 + th)
    slope = half + 0.5 * gate * (1.0 - th * th) * (GELU_A * (1.0 + 3.0 * GELU_B * sq))
    return gate * half, slope


def softmax(scores):
    e = jnp.exp(scores - jnp.max(scores, axis=-1, keepdims=True))
    return (e * (1.0 / jnp.sum(e, axis=-1, keepdims=True))).astype(bf16)


def pad64(v):
    return jnp.concatenate([v, jnp.zeros((v.shape[0], 64), v.dtype)], axis=1)


def above64(v):
    return jnp.concatenate([jnp.zeros((v.shape[0], 64), v.dtype), v], axis=1)


def pack(ref, slot, parts):
    ref[slot, 0:256, :] = jnp.concatenate([parts[0], parts[1]], axis=1)
    ref[slot, 256:384, :] = jnp.concatenate([parts[2][0:128], parts[2][128:256]], axis=1)


def unpack(ref, slot):
    two = ref[slot, 0:256, :]
    last = ref[slot, 256:384, :]
    return (two[:, :64], two[:, 64:], jnp.concatenate([last[:, :64], last[:, 64:]], axis=0))


def assemble(ref, dst):
    for t in range(2):
        a = unpack(ref, 2 * t) + unpack(ref, 2 * t + 1)
        for j in range(3):
            at = 384 * t + 128 * j
            dst[:, at : at + 128] = jnp.concatenate([a[2 * j], a[2 * j + 1]], axis=1)


def disperse(val, ref):
    for gg in range(4):
        pack(ref, gg, [val[:, 192 * gg + 64 * h : 192 * gg + 64 * h + 64] for h in range(3)])


def block(i):
    return pl.ds(pl.multiple_of(i * 256, 256), 256)


def layer_kernel(
    x, mem, cot, segs, gain1, gain2, gain3, rel, buck, live, w_in, w_kv, w_ao, w_cq, w_co, w_gu, w_dn,
    out, gin, gmem, o_gu, o_dn, o_b, o_q, o_m, o_small,
    *,
    xrow, mrow, h1, wQ, wM, W3, wgu, wd, sm, sg, gains, lines, hot, tbias, qh, kh, vh, mkv, p_self, p_cross,
    opack, arecv, attn, qpack, qrecv, crecv, cattn, after_self, after_cross, h2, h3, prod, dgu, cotb, frecv,
    hrecv, outb, grad, low, dcq, acc, dqkv, rs1, rs2, rt1, rt2, gur, dnr, bsib, bdp, qdp, mdp, zg1, zg2, zd1, zd2,
    zb1, zb2, qfar, mfar, gsm, sm1, sm2, sgown, ssem, rsem, lsem,
):
    drecv, dqrecv, srecv = arecv, crecv, qrecv
    fown, tot, hown, fpart, xown = tbias.at[0], tbias.at[1], grad, outb, after_cross
    keep, hpart = p_cross.at[0], low.at[1]

    d, s = lax.axis_index("dp"), lax.axis_index("seq")
    c, z, g, r = lax.rem(s, 2), lax.div(s, 2), lax.rem(s, 4), lax.div(s, 4)
    used = {"remote": 0, "local": 0}
    flying = []

    def remote(src, dst, send_sem, recv_sem, dev):
        return pltpu.make_async_remote_copy(
            src_ref=src, dst_ref=dst, send_sem=ssem.at[send_sem], recv_sem=rsem.at[recv_sem],
            device_id=dev, device_id_type=MESH,
        )

    def fresh(n=1):
        used["remote"] += n
        assert used["remote"] <= N_SEM
        return used["remote"] - n

    def push(src, dst, dev):
        sem = fresh()
        copy = remote(src, dst, sem, sem, dev)
        copy.start()
        flying.append(copy)
        return copy

    def sent(copies):
        for copy in copies:
            copy.wait_send()
            flying[:] = [other for other in flying if other is not copy]

    def arrived(copies):
        for copy in copies:
            copy.wait_recv()

    def local(src, dst):
        copy = pltpu.make_async_copy(src, dst, lsem.at[used["local"]])
        used["local"] += 1
        copy.start()
        return copy

    def dpk(k):
        return (flip(d, k, 2), s)

    def seqk(k):
        return (d, flip(s, k, 3))

    class Gather:
        def __init__(self, whole, part):
            self.part = part
            own = whole(d)
            self.first = {k: push(own, own, dpk(k)) for k in (1, 2)}
            self.second = []

        def relay(self):
            for k, half in ((1, 0), (2, 1)):
                arrived([self.first[k]])
                src = self.part(flip(d, k, 2), half)
                self.second.append(push(src, src, dpk(3 - k)))

        def done(self):
            arrived(self.second)

        def gone(self):
            sent([*self.first.values(), *self.second])

    class Reduce:
        def __init__(self, part, got):
            self.part, self.got = part, got
            self.first = {}
            for k, half in ((1, 0), (2, 1)):
                for j, kk in ((0, k), (1, 3)):
                    copy = push(part(flip(d, kk, 2), half), got.at[3 * half + j], dpk(k))
                    self.first[half, j] = copy

        def middle(self):
            self.second = {}
            for k, half in ((1, 0), (2, 1)):
                arrived([self.first[half, 1]])
                ref = self.part(flip(d, 3 - k, 2), half)
                ref[...] = (ref[...].astype(f32) + self.got[3 * half + 1].astype(f32)).astype(bf16)
                self.second[half] = push(ref, self.got.at[3 * half + 2], dpk(3 - k))

        def end(self):
            for half in (0, 1):
                arrived([self.first[half, 0], self.second[half]])
                ref = self.part(d, half)
                total = ref[...].astype(f32) + self.got[3 * half].astype(f32) + self.got[3 * half + 2].astype(f32)
                ref[...] = total.astype(bf16)

    def moved(srcs, dsts, devs, slot):
        base = fresh(2)
        for i in range(2):
            away = remote(srcs[i], dsts[i], base + i, base + slot, (d, devs[i]))
            here = pltpu.make_async_copy(srcs[i], dsts[i], rsem.at[base + slot])

            @pl.when(devs[i] != s)
            def _():
                away.start()

            @pl.when(devs[i] == s)
            def _():
                here.start()

        def wait_recv(places):
            for i in range(2):
                pltpu.make_async_copy(places[i], places[i], rsem.at[base + i]).wait()

        def wait_send():
            for i in range(2):
                away = remote(srcs[i], dsts[i], base + i, base + slot, (d, devs[i]))

                @pl.when(devs[i] != s)
                def _():
                    away.wait_send()

        return wait_recv, wait_send

    mine, mine_d = pl.ds(pl.multiple_of(d * 192, 64), 192), block(d)
    here = pl.ds(s * 128, 128)
    own_x = local(x.at[r], xrow.at[here])
    stage = [p_self.at[0, i, 0:192] for i in range(4)] + [p_self.at[1, 0, 0:192]]
    own_in = [
        local(w.at[:, 768 * i : 768 * i + 768], stage[p])
        for p, (w, i) in enumerate(((w_in, 0), (w_in, 1), (w_in, 2), (w_kv, 0), (w_kv, 1)))
    ]
    own_W3 = [local(w, W3.at[i, mine]) for i, w in enumerate((w_ao, w_cq, w_co))]
    own_m = local(mem.at[r], mrow.at[here])
    own_gu = []
    for p in range(8):
        at = pl.multiple_of((p // 4) * FF + (p % 4) * 512 + c * 256, 256)
        own_gu.append(local(w_gu.at[:, pl.ds(at, 256)], wgu.at[mine, pl.ds(p * 256, 256)]))
    own_dn = local(w_dn.at[block(c)], wd.at[mine_d])

    barrier = pltpu.get_barrier_semaphore()
    peers = [dpk(k) for k in (1, 2, 3)] + [seqk(k) for k in range(1, 8)]
    for p in peers:
        pl.semaphore_signal(barrier, inc=1, device_id=p, device_id_type=MESH)
    for i in range(2):
        sgown[i] = jnp.broadcast_to(segs[i : i + 1, :].astype(f32), (16, 128)).astype(bf16)
    sg[s] = sgown[r]
    at_bucket = lax.broadcasted_iota(jnp.int32, (8, 128), 1) == lax.broadcasted_iota(jnp.int32, (8, 128), 0) + 8 * d
    gains[...] = jnp.zeros((16, 768), f32)
    gains[0:12, 0:128] = dot_tn(rel[...].astype(f32), at_bucket.astype(f32))
    for q in range(4):

        @pl.when(d == q)
        def _():
            for i, gain in enumerate((gain1, gain2, gain3)):
                gains[12 + i : 13 + i, 192 * q : 192 * q + 192] = gain[...].astype(f32).reshape(1, 192)

    sm[d] = gains[...].astype(bf16)
    pl.semaphore_wait(barrier, len(peers))

    def row_of(k):
        return lax.div(flip(s, k, 3), 4)

    def spread(src, dst):
        return {m: push(src.at[row_of(2 * m)], dst.at[here], seqk(2 * m)) for m in (1, 2, 3)}

    def hand_on(dst, m):
        part = dst.at[pl.ds(flip(s, 2 * m, 3) * 128, 128)]
        return push(part, part, seqk(1))

    xd = spread(x, xrow)
    own_x.wait()
    xs = {0: hand_on(xrow, 0)}
    for cp in own_in:
        cp.wait()
    for q in range(4):

        @pl.when(g == q)
        def _():
            for p in range(5):
                dst, at = (wQ, 192 * p) if p < 3 else (wM, 192 * (p - 3))
                dst[mine, at : at + 192] = stage[p][:, 192 * q : 192 * q + 192]

    def part192(ref):
        return lambda dd, half: ref.at[pl.ds(pl.multiple_of(dd * 192 + 96 * half, 32), 96)]

    def whole192(ref):
        return lambda dd: ref.at[pl.ds(pl.multiple_of(dd * 192, 64), 192)]

    def part_dn(dd, half):
        return wd.at[pl.ds(pl.multiple_of(dd * 256 + 128 * half, 128), 128)]

    def part_b(i):
        return lambda dd, half: W3.at[i, pl.ds(pl.multiple_of(dd * 192 + c * 96 + 48 * half, 16), 48)]

    q_w = Gather(whole192(wQ), part192(wQ))
    sm_in = [push(sm.at[d], sm.at[d], dpk(k)) for k in (1, 2, 3)]
    sg_in = [push(sgown.at[row_of(k)], sg.at[s], seqk(k)) for k in range(1, 8)]

    def half_rows(dd, cc):
        return pl.ds(pl.multiple_of(dd * 192 + cc * 96, 32), 96)

    def send_W3(i):
        own_W3[i].wait()
        return Gather(lambda dd: W3.at[i, half_rows(dd, c)], part_b(i))

    def share_W3(i):
        W3_w[i].done()
        return [push(W3.at[i, rows], W3.at[i, rows], seqk(1)) for rows in (half_rows(flip(d, k, 2), c) for k in (1, 2, 3))]

    m_w = Gather(whole192(wM), part192(wM))
    W3_w = {0: send_W3(0)}
    W3_sib = {}

    arrived(sm_in)
    total = sm[0].astype(f32)
    for i in range(1, 4):
        total += sm[i].astype(f32)
    gains[...] = total
    near = jnp.concatenate([buck[i : i + 1, :] for i in range(4)], axis=1)
    by_dist = (lax.broadcasted_iota(jnp.int32, (128, 512), 0) == near).astype(bf16)
    turn = lax.broadcasted_iota(jnp.int32, (512, 1024), 0) + lax.broadcasted_iota(jnp.int32, (512, 1024), 1) == 768
    hot[...] = dot(by_dist, turn.astype(bf16)).astype(bf16)
    column = lax.broadcasted_iota(jnp.int32, (16, 1024), 1)
    line = dot(total[:, :128].astype(bf16), hot[...])
    lines[...] = jnp.where((column > 256) & (column < 769), line, masked_score)
    for h in range(3):
        row = jnp.broadcast_to(lines[pl.ds(3 * g + h, 1), :], (256, 1024))
        tbias[h] = pltpu.roll(row, 0, 1, stride=1, stride_axis=0)[:, 256:]

    def norm_block(m):
        rows = block(flip(z, m, 2))
        val = xrow[rows, :].astype(f32)
        h1[rows, :] = (val * inv_rms(val) * gains[12:13, :]).astype(bf16)

    arrived([xs[0]])
    norm_block(0)
    for m in (1, 2):
        arrived([xd[m]])
        xs[m] = hand_on(xrow, m)
    q_w.relay()
    arrived([xs[1]])
    norm_block(1)
    m_w.relay()
    W3_w[1] = send_W3(1)
    arrived([xd[3]])
    xs[3] = hand_on(xrow, 3)
    md = spread(mem, mrow)
    own_m.wait()
    ms = {0: hand_on(mrow, 0)}
    W3_w[0].relay()
    W3_w[2] = send_W3(2)
    arrived([xs[2]])
    norm_block(2)
    arrived([xs[3]])
    norm_block(3)

    arrived(sg_in)
    lane64 = lax.broadcasted_iota(jnp.int32, (128, 64), 1).astype(f32)
    inside = lane64 < 3.5
    for h in range(3):
        beyond = lax.broadcasted_iota(jnp.int32, (512, 128), 1) >= 64
        kh[h, 0:512, :] = jnp.where(beyond, -1.0, 0.0).astype(bf16)
        vh[h, 0:512, :] = jnp.zeros((512, 128), bf16)
    q_w.done()

    def project(i, carry):
        rows = block(i)
        res = dot(h1[rows, :], wQ[...]).astype(bf16)
        qa, ka = [], []
        for j in range(2):
            seg = sg[2 * i + j, 0:1, :].astype(f32)
            same = jnp.transpose(jnp.broadcast_to(seg, (128, 128)))[:, :64] == lane64
            qa.append(jnp.where(same, BIG, 0.0))
            ka.append(jnp.where(inside & jnp.logical_not(same), -1.0, 0.0))
        qa = jnp.concatenate(qa, axis=0).astype(bf16)
        ka = jnp.concatenate(ka, axis=0).astype(bf16)
        lower = pl.ds(pl.multiple_of(i * 256 + 512, 256), 256)
        for h in range(3):
            qv = (res[:, 64 * h : 64 * h + 64].astype(f32) * SCALE).astype(bf16)
            qh[h, rows, :] = jnp.concatenate([qv, qa], axis=1)
            kh[h, lower, :] = jnp.concatenate([res[:, 192 + 64 * h : 256 + 64 * h], ka], axis=1)
            vh[h, lower, :] = pad64(res[:, 384 + 64 * h : 448 + 64 * h])
        return carry

    lax.fori_loop(0, 4, project, 0)

    for cp in own_gu:
        cp.wait()
    gu_w = Gather(whole192(wgu), part192(wgu))
    W3_w[1].relay()

    def window(b):
        return pl.ds(pl.multiple_of(b * 256, 256), 768)

    a_in = []
    for k in (2, 3, 1, 0):
        b = flip(g, k, 2)
        parts = []
        for h in range(3):
            p = softmax(dot_nt(qh[h, block(b), :], kh[h, window(b), :]) + tbias[h])
            p_self[h, b] = p
            parts.append(dot(p, vh[h, window(b), :])[:, :64].astype(bf16))
        if k == 0:
            pack(arecv, g, parts)
        else:
            pack(opack, b, parts)
            a_in.append(push(opack.at[b], arecv.at[g], seqk(k)))

    own_dn.wait()
    dn_w = Gather(lambda dd: wd.at[block(dd)], part_dn)
    W3_w[2].relay()
    for m in (1, 2, 3):
        arrived([md[m]])
        ms[m] = hand_on(mrow, m)
    halves = [cotb.at[c, pl.ds(c * 128, 128)]] * 2
    dests = [4 * rr + z for rr in range(2)]
    cslot = lax.rem(z, 2)
    cot_recv, cot_sent = moved(
        [cot.at[0], cot.at[1]], [cotb.at[cslot, pl.ds(c * 128, 128)]] * 2, dests, c
    )
    W3_sib[0] = share_W3(0)
    m_w.done()
    arrived(ms.values())

    def project_memory(i, carry):
        rows = block(i)
        res = dot(mrow[rows, :], wM[...]).astype(bf16)
        for h in range(3):
            mkv[h, rows, :] = jnp.concatenate(
                [res[:, 64 * h : 64 * h + 64], res[:, 192 + 64 * h : 256 + 64 * h]], axis=1
            )
        return carry

    lax.fori_loop(0, 4, project_memory, 0)
    W3_sib[1] = share_W3(1)

    arrived(a_in)
    assemble(arecv, attn)
    arrived(W3_sib[0])
    alive = live[r].astype(f32)
    res = xrow[block(g), :].astype(f32) + alive * dot(attn[...], W3[0])
    after_self[...] = res
    h2[...] = (res * inv_rms(res) * gains[13:14, :]).astype(bf16)
    arrived(W3_sib[1])
    disperse((dot(h2[...], W3[1]).astype(bf16).astype(f32) * SCALE).astype(bf16), qpack)
    q_in = {k: push(qpack.at[flip(g, k, 2)], qrecv.at[g], seqk(k)) for k in (2, 3, 1)}
    qrecv[g] = qpack[g]
    W3_sib[2] = share_W3(2)
    gu_w.relay()
    cot_recv([cotb.at[c, pl.ds(0, 128)], cotb.at[c, pl.ds(128, 128)]])
    cot_sib = push(cotb.at[c], cotb.at[c], seqk(1))

    sent(a_in)
    c_in = []
    for k in (0, 1, 2, 3):
        b = flip(g, k, 2)
        if k:
            arrived([q_in[k]])
        qs = unpack(qrecv, b)
        parts = []
        for h in range(3):
            p = softmax(dot_nt(pad64(qs[h]), mkv[h]))
            p_cross[h, b] = p
            parts.append(dot(p, mkv[h])[:, 64:].astype(bf16))
        if k == 0:
            pack(crecv, g, parts)
        else:
            pack(opack, b, parts)
            c_in.append(push(opack.at[b], crecv.at[g], seqk(k)))
    dn_w.relay()
    arrived(W3_sib[2])
    arrived(c_in)
    assemble(crecv, cattn)
    res = after_self[...] + alive * dot(cattn[...], W3[2])
    after_cross[...] = res
    h3[c] = (res * inv_rms(res) * gains[14:15, :]).astype(bf16)
    h3_in = push(h3.at[c], h3.at[c], seqk(1))
    arrived([cot_sib])
    gu_w.done()
    dn_w.done()
    arrived([h3_in])

    def feed_forward(i, carry):
        t, n = lax.div(i, 4), lax.rem(i, 4)
        cols, more = block(n), pl.ds(pl.multiple_of(1024 + n * 256, 256), 256)
        gate = dot(h3[t], wgu[:, cols])
        up = dot(h3[t], wgu[:, more])
        act, slope = gelu_parts(gate)
        prod[t, :, cols] = (act * up).astype(bf16)
        down_in = (cotb[t].astype(f32) * alive).astype(bf16)
        gp = dot_nt(down_in, wd[cols, :])
        dgu[t, :, cols] = (gp * up * slope).astype(bf16)
        dgu[t, :, more] = (gp * act).astype(bf16)
        return carry

    lax.fori_loop(0, 8, feed_forward, 0)

    hpart[...] = dot_nt(dgu[1 - c], wgu[...]).astype(bf16)
    h_in = push(hpart, hrecv, seqk(1))
    hown[...] = dot_nt(dgu[c], wgu[...])
    fpart[...] = dot(prod[1 - c], wd[...]).astype(bf16)
    f_in = push(fpart, frecv, seqk(1))
    arrived([h_in])
    dv, dgain3 = norm_back(after_cross[...], gains[14:15, :], hown[...] + hrecv[...].astype(f32))
    gsm[...] = jnp.zeros((16, 768), f32)
    gsm[14:15, :] = dgain3
    grad[...] = cotb[c].astype(f32) + dv
    low[0] = (grad[...] * alive).astype(bf16)
    sent(c_in)
    sent(q_in.values())
    disperse(dot_nt(low[0], W3[2]).astype(bf16), opack)
    d_in = {k: push(opack.at[flip(g, k, 2)], drecv.at[g], seqk(k)) for k in (2, 3, 1)}
    drecv[g] = opack[g]

    gu_w.gone()
    dn_w.gone()

    def grad_gu(n, carry):
        cols = block(n)
        wgu[:, cols] = dot_tn(h3[...].reshape(512, 768), dgu[:, :, cols].reshape(512, 256)).astype(bf16)
        return carry

    def grad_dn(n, carry):
        cols = block(n)
        down_in = (cotb[...].astype(f32) * alive).astype(bf16).reshape(512, 768)
        wd[cols, :] = dot_tn(prod[:, :, cols].reshape(512, 256), down_in).astype(bf16)
        return carry

    def part_gu(i):
        cols = pl.ds(1024 * i, 1024)
        return lambda dd, half: wgu.at[pl.ds(pl.multiple_of(dd * 192 + 96 * half, 32), 96), cols]

    half, quarter = lax.rem(z, 2), lax.div(z, 2)

    class Around:
        def __init__(self, view, ref, base, out, got):
            self.half, self.part = view(ref, base)
            self.out_half, self.out_part = view(out, 0)
            self.out, self.got = out, got

        def step1(self):
            self.copy = push(self.half(1 - half), self.got[0], seqk(2))

        def add(self, ref, got):
            arrived([self.copy])
            ref[...] = (ref[...].astype(f32) + got[...].astype(f32)).astype(bf16)

        def step2(self):
            self.add(self.half(half), self.got[0])
            self.copy = push(self.part(1 - quarter), self.got[1], seqk(4))

        def step3(self):
            self.add(self.part(quarter), self.got[1])
            place = self.out_part(quarter)
            self.own = local(self.part(quarter), place)
            self.copy = push(self.part(quarter), place, seqk(4))

        def step4(self):
            arrived([self.copy])
            self.own.wait()
            place = self.out_half(half)
            self.copy = push(place, place, seqk(2))

        def step5(self):
            arrived([self.copy])
            self.copy = push(self.out, self.out, seqk(1))

    def by_rows(n, cols):
        def view(ref, base):
            def rows(at, m):
                return ref.at[pl.ds(pl.multiple_of(base + at, 16), m), cols]

            return lambda i: rows(n * i, n), lambda i: rows(n * half + (n // 2) * i, n // 2)

        return view

    def by_columns(ref, base):
        def rows(cols):
            return ref.at[pl.ds(pl.multiple_of(base + 48 * half, 16), 48), cols]

        return (
            lambda i: ref.at[pl.ds(pl.multiple_of(base + 48 * i, 16), 48)],
            lambda i: rows(pl.ds(pl.multiple_of(384 * i, 128), 384)),
        )

    g_z, u_z = [
        Around(by_rows(96, pl.ds(1024 * i, 1024)), wgu, d * 192, o_gu.at[c], (zg1.at[i], zg2.at[i])) for i in range(2)
    ]
    g_z.out, u_z.out = [o_gu.at[c, :, pl.ds(1024 * i, 1024)] for i in range(2)]
    n_z = Around(by_rows(128, pl.ds(0, 768)), wd, d * 256, o_dn.at[c], (zd1, zd2))
    b_z = [Around(by_columns, W3.at[i], d * 192 + c * 96, o_b.at[i, c], (zb1.at[i], zb2.at[i])) for i in range(3)]

    lax.fori_loop(0, 4, grad_gu, 0)
    g_rs = Reduce(part_gu(0), gur.at[0])
    lax.fori_loop(4, 8, grad_gu, 0)

    fown[...] = dot(prod[c], wd[...])
    arrived([f_in])
    sent([f_in])
    outb[...] = (after_cross[...] + alive * (fown[...] + frecv[...].astype(f32))).astype(bf16)
    back = [2 * g + j for j in range(2)]
    out_recv, out_sent = moved([outb.at[pl.ds(0, 128)], outb.at[pl.ds(128, 128)]], [out.at[r]] * 2, back, r)
    lax.fori_loop(0, 4, grad_dn, 0)

    lefts = (attn, h2, cattn)
    rights = (low.at[1], dcq, low.at[0])
    b_sib = {}

    def grad_square(i):
        W3_w[i].gone()
        sent(W3_sib[i])
        W3[i] = dot_tn(lefts[i][...], rights[i][...]).astype(bf16)
        b_sib[i] = [push(W3.at[i, half_rows(q, 1 - c)], bsib.at[i, q], seqk(1)) for q in range(4)]

    def chip_square(i):
        arrived(b_sib[i])
        for q in range(4):
            rows = half_rows(q, c)
            W3[i, rows, :] = (W3[i, rows, :].astype(f32) + bsib[i, q].astype(f32)).astype(bf16)
        return Reduce(part_b(i), bdp.at[i])

    grad_square(2)

    for h in range(3):
        acc[h, 0:1024, :] = jnp.zeros((1024, 128), f32)
    dq_in = []

    def cross_back(k):
        b = flip(g, k, 2)
        if k:
            arrived([d_in[k]])
        dos, qs = unpack(drecv, b), unpack(qrecv, b)
        parts = []
        for h in range(3):
            p = p_cross[h, b]
            do = above64(dos[h])
            dp = dot_nt(do, mkv[h])
            pf = p.astype(f32)
            ds = (pf * (dp - jnp.sum(dp * pf, axis=-1, keepdims=True))).astype(bf16)
            parts.append((dot(ds, mkv[h])[:, :64] * SCALE).astype(bf16))
            acc[h, 0:1024, :] += dot_tn(ds, pad64(qs[h])) + dot_tn(p, do)
        if k == 0:
            pack(dqrecv, g, parts)
        else:
            pack(qpack, b, parts)
            dq_in.append(push(qpack.at[b], dqrecv.at[g], seqk(k)))

    cross_back(2)
    u_rs = Reduce(part_gu(1), gur.at[1])
    cross_back(3)
    g_rs.middle()
    cross_back(1)
    cross_back(0)
    n_rs = Reduce(part_dn, dnr)

    def keep_memory(i, carry):
        rows = block(i)
        vals = [acc[h, rows, :][:, :64] for h in range(3)] + [acc[h, rows, :][:, 64:] for h in range(3)]
        dqkv[rows, 0:384] = jnp.concatenate(vals, axis=1).astype(bf16)
        return carry

    lax.fori_loop(0, 4, keep_memory, 0)
    arrived(dq_in)
    assemble(dqrecv, dcq)
    dv, dgain2 = norm_back(after_self[...], gains[13:14, :], dot_nt(dcq[...], W3[1]))
    gsm[13:14, :] = dgain2
    grad[...] += dv
    sent([h_in])
    low[1] = (grad[...] * alive).astype(bf16)
    sent(d_in.values())
    disperse(dot_nt(low[1], W3[0]).astype(bf16), opack)
    s_in = {k: push(opack.at[flip(g, k, 2)], srecv.at[g], seqk(k)) for k in (2, 3, 1)}
    srecv[g] = opack[g]

    u_rs.middle()
    g_rs.end()
    g_z.step1()
    b_rs = {2: chip_square(2)}
    grad_square(1)
    grad_square(0)

    class Rows:
        def __init__(self, compute, first, second):
            self.compute, self.first, self.second = compute, first, second
            self.in3 = push(compute(flip(g, 3, 2)), first.at[0], seqk(1))
            self.part2 = compute(flip(g, 2, 2))
            self.in1 = push(compute(flip(g, 1, 2)), first.at[1], seqk(1))

        def far(self):
            arrived([self.in3])
            self.part2[...] = (self.part2[...].astype(f32) + self.first[0].astype(f32)).astype(bf16)
            self.out = push(self.part2, self.second, seqk(2))
            self.part0 = self.compute(g)

        def total(self):
            arrived([self.in1, self.out])
            return self.part0[...].astype(f32) + self.first[1].astype(f32) + self.second[...].astype(f32)

    m_w.gone()
    sent(ms.values())
    for i in range(3):
        keep[i, :, 0:384] = dot_tn(mrow[:, 256 * i : 256 * i + 256], dqkv[:, 0:384]).astype(bf16)

    def memory_part(b):
        mrow[block(b), :] = dot_nt(dqkv[block(b), 0:384], wM[...]).astype(bf16)
        return mrow.at[block(b)]

    m_rows = Rows(memory_part, rt1, rt2)
    m_rows.far()
    for i in range(3):
        wM[256 * i : 256 * i + 256, :] = keep[i, :, 0:384]

    for h in range(3):
        acc[h] = jnp.zeros((1536, 128), f32)
        tbias[h] = jnp.zeros((256, 768), f32)

    def self_back(k):
        b = flip(g, k, 2)
        if k:
            arrived([s_in[k]])
        dos = unpack(srecv, b)
        for h in range(3):
            p = p_self[h, b]
            do = pad64(dos[h])
            dp = dot_nt(do, vh[h, window(b), :])
            pf = p.astype(f32)
            ds = pf * (dp - jnp.sum(dp * pf, axis=-1, keepdims=True))
            tbias[h] += ds
            ds = ds.astype(bf16)
            dqkv[block(b), 64 * h : 64 * h + 64] = (dot(ds, kh[h, window(b), :])[:, :64] * SCALE).astype(bf16)
            acc[h, window(b), :] += dot_tn(ds, pad64(qh[h, block(b), :][:, :64])) + dot_tn(p, above64(dos[h]))

    self_back(0)
    n_rs.middle()
    m_rs = Reduce(part192(wM), mdp)
    u_rs.end()
    u_z.step1()
    self_back(2)
    b_rs[1] = chip_square(1)
    b_rs[0] = chip_square(0)
    g_z.step2()
    self_back(3)
    self_back(1)

    def keep_self(i, carry):
        rows, lower = block(i), pl.ds(pl.multiple_of(i * 256 + 512, 256), 256)
        for h in range(3):
            dqkv[rows, 192 + 64 * h : 256 + 64 * h] = acc[h, lower, :][:, :64].astype(bf16)
            dqkv[rows, 384 + 64 * h : 448 + 64 * h] = acc[h, lower, :][:, 64:].astype(bf16)
        return carry

    lax.fori_loop(0, 4, keep_self, 0)
    xown[...] = xrow[block(g), :].astype(f32)
    sent(xs.values())

    def self_part(b):
        xrow[block(b), :] = dot_nt(dqkv[block(b), :], wQ[...]).astype(bf16)
        return xrow.at[block(b)]

    x_rows = Rows(self_part, rs1, rs2)
    x_rows.far()
    n_rs.end()
    n_z.step1()
    u_z.step2()
    g_z.step3()
    q_w.gone()

    def grad_qkv(n, carry):
        cols = pl.ds(pl.multiple_of(n * 128, 128), 128)
        wQ[cols, :] = dot_tn(h1[:, cols], dqkv[...]).astype(bf16)
        return carry

    lax.fori_loop(0, 6, grad_qkv, 0)
    q_rs = Reduce(part192(wQ), qdp)

    b_rs[2].middle()
    m_rs.middle()

    for h in range(3):
        wide = jnp.concatenate([jnp.zeros((256, 256), f32), tbias[h]], axis=1)
        rows = lax.broadcasted_iota(jnp.int32, (256, 1024), 0)
        for i in range(8):
            bit = lax.rem(lax.div(rows, 1 << i), 2) == 1
            wide = jnp.where(bit, pltpu.roll(wide, 1024 - (1 << i), 1), wide)
        lines[h : h + 1, :] = jnp.sum(wide, axis=0, keepdims=True)
    val = lines[...]
    top = val.astype(bf16)
    rest = val - top.astype(f32)
    mid = rest.astype(bf16)
    last = (rest - mid.astype(f32)).astype(bf16)
    by_bucket = dot_nt(top, hot[...]) + dot_nt(mid, hot[...]) + dot_nt(last, hot[...])
    row16 = lax.broadcasted_iota(jnp.int32, (16, 128), 0)
    spot = jnp.zeros((16, 128), f32)
    for h in range(3):
        spot = jnp.where(row16 == 3 * g + h, jnp.broadcast_to(by_bucket[h : h + 1, :], (16, 128)), spot)
    gsm[:, 0:128] += spot

    b_rs[1].middle()
    b_rs[0].middle()

    total = m_rows.total()
    out_recv([out.at[0], out.at[1]])
    out_sent()
    outb[...] = total.astype(bf16)
    mem_recv, mem_sent = moved([outb.at[pl.ds(0, 128)], outb.at[pl.ds(128, 128)]], [gmem.at[r]] * 2, back, r)

    n_z.step2()
    u_z.step3()
    g_z.step4()

    dv, dgain1 = norm_back(xown[...], gains[12:13, :], x_rows.total())
    gsm[12:13, :] = dgain1
    sm_dp = [push(gsm, sm1.at[k - 1], dpk(k)) for k in (1, 2, 3)]
    mem_recv([gmem.at[0], gmem.at[1]])
    mem_sent()
    outb[...] = (grad[...] + dv).astype(bf16)
    gin_recv, gin_sent = moved([outb.at[pl.ds(0, 128)], outb.at[pl.ds(128, 128)]], [gin.at[r]] * 2, back, r)
    q_rs.middle()

    m_rs.end()
    m_far = push(wM.at[mine], mfar, seqk(4))
    for i in (2, 1, 0):
        b_rs[i].end()
        b_z[i].step1()
    n_z.step3()
    u_z.step4()
    g_z.step5()
    q_rs.end()
    q_far = push(wQ.at[mine], qfar, seqk(4))

    arrived(sm_dp)
    sent(sm_dp)
    gsm[...] = gsm[...] + sm1[0] + sm1[1] + sm1[2]
    sm_seq = [push(gsm, sm2.at[k - 1], seqk(k)) for k in range(1, 8)]
    for i in (2, 1, 0):
        b_z[i].step2()

    def far_sum(ref, copy, got, place):
        arrived([copy])
        sent([copy])
        ref[mine, :] = (ref[mine, :].astype(f32) + got[...].astype(f32)).astype(bf16)
        here_too = local(ref.at[mine], place.at[g])
        return here_too, push(ref.at[mine], place.at[g], seqk(2)), push(ref.at[mine], place.at[g], seqk(1))

    m_own, m_pair, m_s1 = far_sum(wM, m_far, mfar, o_m)
    n_z.step4()
    u_z.step5()
    for i in (2, 1, 0):
        b_z[i].step3()
    q_own, q_pair, q_s1 = far_sum(wQ, q_far, qfar, o_q)

    arrived(sm_seq)
    val = gsm[...]
    for k in range(7):
        val = val + sm2[k]
    o_small[...] = val
    other = flip(g, 2, 2)
    arrived([m_pair])
    m_s2 = push(o_m.at[other], o_m.at[other], seqk(1))
    n_z.step5()
    for i in (2, 1, 0):
        b_z[i].step4()
    arrived([q_pair])
    q_s2 = push(o_q.at[other], o_q.at[other], seqk(1))
    for i in (2, 1, 0):
        b_z[i].step5()
    gin_recv([gin.at[0], gin.at[1]])
    gin_sent()
    cot_sent()
    m_own.wait()
    q_own.wait()
    arrived([m_s1, q_s1, m_s2, q_s2])
    for chain in (g_z, u_z, n_z, *b_z):
        arrived([chain.copy])
    for cp in list(flying):
        cp.wait_send()


def scratch():
    def vm(kind, *shape):
        return pltpu.VMEM(shape, kind)

    return dict(
        xrow=vm(bf16, 1024, 768),
        mrow=vm(bf16, 1024, 768),
        h1=vm(bf16, 1024, 768),
        wQ=vm(bf16, 768, 576),
        wM=vm(bf16, 768, 384),
        W3=vm(bf16, 3, 768, 768),
        wgu=vm(bf16, 768, 2048),
        wd=vm(bf16, 1024, 768),
        sm=vm(bf16, 4, 16, 768),
        sg=vm(bf16, 8, 16, 128),
        gains=vm(f32, 16, 768),
        lines=vm(f32, 16, 1024),
        hot=vm(bf16, 128, 1024),
        tbias=vm(f32, 3, 256, 768),
        qh=vm(bf16, 3, 1024, 128),
        kh=vm(bf16, 3, 1536, 128),
        vh=vm(bf16, 3, 1536, 128),
        mkv=vm(bf16, 3, 1024, 128),
        p_self=vm(bf16, 3, 4, 256, 768),
        p_cross=vm(bf16, 3, 4, 256, 1024),
        opack=vm(bf16, 4, 384, 128),
        arecv=vm(bf16, 4, 384, 128),
        attn=vm(bf16, 256, 768),
        qpack=vm(bf16, 4, 384, 128),
        qrecv=vm(bf16, 4, 384, 128),
        crecv=vm(bf16, 4, 384, 128),
        cattn=vm(bf16, 256, 768),
        after_self=vm(f32, 256, 768),
        after_cross=vm(f32, 256, 768),
        h2=vm(bf16, 256, 768),
        h3=vm(bf16, 2, 256, 768),
        prod=vm(bf16, 2, 256, 1024),
        dgu=vm(bf16, 2, 256, 2048),
        cotb=vm(bf16, 2, 256, 768),
        frecv=vm(bf16, 256, 768),
        hrecv=vm(bf16, 256, 768),
        outb=vm(bf16, 256, 768),
        grad=vm(f32, 256, 768),
        low=vm(bf16, 2, 256, 768),
        dcq=vm(bf16, 256, 768),
        acc=vm(f32, 3, 1536, 128),
        dqkv=vm(bf16, 1024, 576),
        rs1=vm(bf16, 2, 256, 768),
        rs2=vm(bf16, 256, 768),
        rt1=vm(bf16, 2, 256, 768),
        rt2=vm(bf16, 256, 768),
        gur=vm(bf16, 2, 6, 96, 1024),
        dnr=vm(bf16, 6, 128, 768),
        bsib=vm(bf16, 3, 4, 96, 768),
        bdp=vm(bf16, 3, 6, 48, 768),
        qdp=vm(bf16, 6, 96, 576),
        mdp=vm(bf16, 6, 96, 384),
        zg1=vm(bf16, 2, 96, 1024),
        zg2=vm(bf16, 2, 48, 1024),
        zd1=vm(bf16, 128, 768),
        zd2=vm(bf16, 64, 768),
        zb1=vm(bf16, 3, 48, 768),
        zb2=vm(bf16, 3, 48, 384),
        qfar=vm(bf16, 192, 576),
        mfar=vm(bf16, 192, 384),
        gsm=vm(f32, 16, 768),
        sm1=vm(f32, 3, 16, 768),
        sm2=vm(f32, 7, 16, 768),
        sgown=vm(bf16, 2, 16, 128),
        ssem=pltpu.SemaphoreType.DMA((N_SEM,)),
        rsem=pltpu.SemaphoreType.DMA((N_SEM,)),
        lsem=pltpu.SemaphoreType.DMA((N_LOCAL,)),
    )


def finish_kernel(
    out, gin, gmem, o_gu, o_dn, o_b, o_q, o_m, o_small,
    y_out, y_gin, y_gmem, y_g1, y_qkv, y_ao, y_rel, y_g2, y_cq, y_kv, y_co, y_g3, y_gu, y_dn, rel_t,
):
    d = lax.axis_index("dp")
    y_out[...] = out[...]
    y_gin[...] = gin[...]
    y_gmem[...] = gmem[...]
    for half in range(2):
        for q in range(4):
            for c in range(2):
                at = 2048 * half + 512 * q + 256 * c
                y_gu[:, at : at + 256] = o_gu[c, :, 1024 * half + 256 * q : 1024 * half + 256 * q + 256].astype(f32)
    y_dn[...] = o_dn[...].astype(f32)
    for i, y in enumerate((y_ao, y_cq, y_co)):
        y[...] = o_b[i, 0].astype(f32)
    for p in range(5):
        y, src, i = (y_qkv, o_q, p) if p < 3 else (y_kv, o_m, p - 3)
        for t in range(2):
            two = [src[2 * t + j, :, 192 * i : 192 * i + 192].astype(f32) for j in range(2)]
            y[:, 768 * i + 384 * t : 768 * i + 384 * t + 384] = jnp.concatenate(two, axis=1)
    for i, y in enumerate((y_g1, y_g2, y_g3)):
        line = o_small[12 + i : 13 + i, :]
        val = line[:, 0:192]
        for q in range(1, 4):
            val = jnp.where(d == q, line[:, 192 * q : 192 * q + 192], val)
        y[...] = val
    rel_t[...] = jnp.transpose(o_small[:, 0:128])
    y_rel[...] = rel_t[pl.ds(pl.multiple_of(8 * d, 8), 8), 0:12]


def per_device_kernel(
    inputs, memory, cotangent, segment_ids, row_live, buckets, gain_self, w_qkv, w_attn_out, rel_bias, gain_cross,
    c_query, c_keyval, c_out, gain_ff, w_gate_up, w_down,
):
    anywhere = pl.BlockSpec(memory_space=pl.ANY)
    vmem = pl.BlockSpec(memory_space=pltpu.VMEM)
    smem = pl.BlockSpec(memory_space=pltpu.SMEM)
    shapes = (
        ((2, 128, 768), bf16), ((2, 128, 768), bf16), ((2, 128, 768), bf16),
        ((2, 192, 2048), bf16), ((2, 256, 768), bf16), ((3, 2, 96, 768), bf16), ((4, 192, 576), bf16), ((4, 192, 384), bf16),
        ((16, 768), f32),
    )
    parts = pl.pallas_call(
        layer_kernel,
        out_shape=[jax.ShapeDtypeStruct(*sh) for sh in shapes],
        in_specs=[anywhere] * 3 + [vmem] * 6 + [smem] + [anywhere] * 7,
        out_specs=[anywhere] * 8 + [vmem],
        scratch_shapes=scratch(),
        compiler_params=pltpu.CompilerParams(collective_id=0, has_side_effects=True, vmem_limit_bytes=66500000),
        name="layer",
    )(
        inputs, memory, cotangent, segment_ids, gain_self, gain_cross, gain_ff, rel_bias,
        buckets.reshape(8, 128), row_live, w_qkv, c_keyval, w_attn_out, c_query, c_out, w_gate_up, w_down,
    )
    act = pl.BlockSpec((1, 64, 768), lambda i: (i // 2, i % 2, 0))
    whole = pl.BlockSpec((16, 768), lambda i: (0, 0))

    def rows(n, width):
        return pl.BlockSpec((n, width), lambda i: (i, 0)), jax.ShapeDtypeStruct((4 * n, width), f32)

    line = pl.BlockSpec((1, 192), lambda i: (0, 0)), jax.ShapeDtypeStruct((1, 192), f32)
    square = rows(48, 768)
    tokens = act, jax.ShapeDtypeStruct((2, 128, 768), bf16)
    down = (
        pl.BlockSpec((2, 64, 768), lambda i: (0, i, 0)),
        jax.ShapeDtypeStruct((2, 256, 768), f32),
    )
    table = pl.BlockSpec((8, 12), lambda i: (0, 0)), jax.ShapeDtypeStruct((8, 12), f32)
    outs = (
        tokens, tokens, tokens, line, rows(48, 2304), square, table, line, square, rows(48, 1536), square, line,
        rows(48, 4096), down,
    )
    res = pl.pallas_call(
        finish_kernel,
        grid=(4,),
        out_shape=[o for _, o in outs],
        in_specs=[
            act, act, act,
            pl.BlockSpec((2, 48, 2048), lambda i: (0, i, 0)),
            pl.BlockSpec((2, 64, 768), lambda i: (0, i, 0)),
            pl.BlockSpec((3, 1, 48, 768), lambda i: (0, i // 2, i % 2, 0)),
            pl.BlockSpec((4, 48, 576), lambda i: (0, i, 0)),
            pl.BlockSpec((4, 48, 384), lambda i: (0, i, 0)),
            whole,
        ],
        out_specs=[b for b, _ in outs],
        scratch_shapes=[pltpu.VMEM((128, 16), f32)],
        compiler_params=pltpu.CompilerParams(vmem_limit_bytes=66500000),
        name="finish",
    )(*parts)
    res = list(res)
    for i in (3, 7, 11):
        res[i] = res[i].reshape(192)
    res[13] = res[13].reshape(512, 768)
    return tuple(res)


def solution(mesh):
    in_specs = (
        P("dp", "seq", None),
        P("dp", "seq", None),
        P("dp", "seq", None),
        P("dp", "seq"),
        P("dp"),
        P(),
        P("dp"),
        P("dp", None),
        P("dp", None),
        P("dp", None),
        P("dp"),
        P("dp", None),
        P("dp", None),
        P("dp", None),
        P("dp"),
        P("dp", None),
        P("dp", None),
    )
    out_specs = (
        P("dp", "seq", None),
        P("dp", "seq", None),
        P("dp", "seq", None),
        P("dp"),
        P("dp", None),
        P("dp", None),
        P("dp", None),
        P("dp"),
        P("dp", None),
        P("dp", None),
        P("dp", None),
        P("dp"),
        P("dp", None),
        P("dp", None),
    )
    fits = dict(mesh.shape) == {"dp": 4, "seq": 8}
    return jax.shard_map(
        per_device_kernel if fits else per_device, mesh=mesh, in_specs=in_specs, out_specs=out_specs, check_vma=False
    )
```

```python
import jax
import jax.numpy as jnp
from jax import lax
from jax.experimental import pallas as pl
from jax.experimental.pallas import tpu as pltpu
from jax.sharding import PartitionSpec as P

D = 768
HEADS = 12
HEAD_DIM = 64
FF = 2048
BUCKETS = 32
LEN = 1024
MEM = 1024


epsilon = 1e-06
masked_score = -1000000000.0
highest = lax.Precision.HIGHEST


def rms_norm(values, gain):
    return values * lax.rsqrt(jnp.mean(values * values, axis=-1, keepdims=True) + epsilon) * gain


def matmul(left, right, form):
    return jnp.einsum(form, left, right, preferred_element_type=jnp.float32)


def softmax_parts(scores):
    top = jnp.max(scores, axis=-1, keepdims=True)
    expo = jnp.exp(scores - top)
    total = jnp.sum(expo, axis=-1, keepdims=True)
    return (expo / total, (top + jnp.log(total))[..., 0])


def score_grads(scores, lse_row, value_row, grad_row):
    probs = jnp.exp(scores - lse_row[..., None])
    grad_probs = matmul(grad_row, value_row, "qhd,khd->hqk")
    centre = jnp.sum(grad_probs * probs, axis=-1, keepdims=True)
    grad_scores = (probs * (grad_probs - centre)).astype(jnp.bfloat16)
    return (probs, grad_scores, centre[..., 0])


def one_hot_of(buckets):
    return (buckets[:, None] == jnp.arange(BUCKETS, dtype=jnp.int32)).astype(jnp.float32)


def skewed(by_dist, start, rows):
    table = jnp.concatenate([jnp.zeros((LEN - 1, HEADS), by_dist.dtype), by_dist], axis=0)
    window = lax.dynamic_slice_in_dim(table, start, rows + LEN - 1, axis=0)
    line = jnp.pad(window[::-1].T, ((0, 0), (0, 1)))
    width = rows + LEN
    flat = jnp.broadcast_to(line[:, None, :], (HEADS, rows, width)).reshape(HEADS, rows * width)
    return flat[:, : rows * (width - 1)].reshape(HEADS, rows, width - 1)[:, :, rows - 1 :]


def unskewed(block, start, rows):
    width = rows + LEN
    wide = jnp.pad(block, ((0, 0), (0, 0), (rows - 1, 0))).reshape(HEADS, rows * (width - 1))
    line = jnp.sum(jnp.pad(wide, ((0, 0), (0, rows))).reshape(HEADS, rows, width), axis=1)
    window = line[:, : width - 1][:, ::-1].T
    table = jnp.zeros((2 * LEN - 1, HEADS), block.dtype)
    return lax.dynamic_update_slice_in_dim(table, window, start, axis=0)[LEN - 1 :]


def per_device(
    inputs,
    memory,
    cotangent,
    segment_ids,
    row_live,
    buckets,
    gain_self,
    w_qkv,
    w_attn_out,
    rel_bias,
    gain_cross,
    c_query,
    c_keyval,
    c_out,
    gain_ff,
    w_gate_up,
    w_down,
):
    (
        g_self,
        qkv_full,
        out_full,
        bias_full,
        g_cross,
        cq_full,
        ckv_full,
        cout_full,
        g_ffn,
        gu_full,
        down_full,
    ) = (
        lax.all_gather(gain_self, "dp", axis=0, tiled=True),
        lax.all_gather(w_qkv, "dp", axis=0, tiled=True),
        lax.all_gather(w_attn_out, "dp", axis=0, tiled=True),
        lax.all_gather(rel_bias, "dp", axis=0, tiled=True),
        lax.all_gather(gain_cross, "dp", axis=0, tiled=True),
        lax.all_gather(c_query, "dp", axis=0, tiled=True),
        lax.all_gather(c_keyval, "dp", axis=0, tiled=True),
        lax.all_gather(c_out, "dp", axis=0, tiled=True),
        lax.all_gather(gain_ff, "dp", axis=0, tiled=True),
        lax.all_gather(w_gate_up, "dp", axis=0, tiled=True),
        lax.all_gather(w_down, "dp", axis=0, tiled=True),
    )
    num_rows, local_len, _ = inputs.shape
    seq_index = lax.axis_index("seq")
    scale = HEAD_DIM ** (-0.5)
    dense = inputs.astype(jnp.float32)
    live_rows = row_live.astype(jnp.float32)[:, None, None]
    normed_one = rms_norm(dense, g_self.astype(jnp.float32))
    hidden_one = normed_one.astype(jnp.bfloat16)
    qkv_local = matmul(hidden_one, qkv_full, "rcd,de->rce").astype(jnp.bfloat16)
    queries = qkv_local[..., :D]
    key_value = qkv_local[..., D:]
    seg_local = segment_ids.astype(jnp.bfloat16)
    key_all, seg_all = (
        lax.all_gather(key_value, "seq", axis=1, tiled=True),
        lax.all_gather(seg_local, "seq", axis=1, tiled=True),
    )
    positions = seq_index * local_len + jnp.arange(local_len, dtype=jnp.int32)
    offsets = positions[:, None] - jnp.arange(LEN, dtype=jnp.int32)[None, :]
    causal = offsets >= 0
    bucket_hot = one_hot_of(buckets)
    by_dist = jnp.einsum(
        "lb,bh->lh",
        bucket_hot,
        bias_full.astype(jnp.float32),
        precision=highest,
        preferred_element_type=jnp.float32,
    )
    bias_block = skewed(by_dist, seq_index * local_len, local_len)

    def self_scores(queries_h, key_row, seg_row, segk_row):
        raw = matmul(queries_h, key_row, "qhd,khd->hqk") * scale + bias_block
        allowed = causal & (seg_row[:, None] == segk_row[None, :])
        return jnp.where(allowed[None], raw, masked_score)

    def self_forward(items):
        query_row, kv_row, seg_row, segk_row = items
        key_row = kv_row[:, :D].reshape(LEN, HEADS, HEAD_DIM)
        value_row = kv_row[:, D:].reshape(LEN, HEADS, HEAD_DIM)
        scores = self_scores(
            query_row.reshape(local_len, HEADS, HEAD_DIM), key_row, seg_row, segk_row
        )
        probs, lse_row = softmax_parts(scores)
        mixed = matmul(probs.astype(jnp.bfloat16), value_row, "hqk,khd->qhd")
        return (mixed.reshape(local_len, D), lse_row)

    attn_self, lse_self = lax.map(self_forward, (queries, key_all, seg_local, seg_all))
    attn_low = attn_self.astype(jnp.bfloat16)
    branch_one = matmul(attn_low, out_full, "rcd,de->rce")
    after_self = dense + live_rows * branch_one
    normed_two = rms_norm(after_self, g_cross.astype(jnp.float32))
    hidden_two = normed_two.astype(jnp.bfloat16)
    cross_q = matmul(hidden_two, cq_full, "rcd,de->rce").astype(jnp.bfloat16)
    memory_kv = matmul(memory, ckv_full, "rmd,de->rme").astype(jnp.bfloat16)
    memory_all = lax.all_gather(memory_kv, "seq", axis=1, tiled=True)

    def cross_forward(items):
        query_row, kv_row = items
        key_row = kv_row[:, :D].reshape(MEM, HEADS, HEAD_DIM)
        value_row = kv_row[:, D:].reshape(MEM, HEADS, HEAD_DIM)
        scores = (
            matmul(query_row.reshape(local_len, HEADS, HEAD_DIM), key_row, "qhd,khd->hqk") * scale
        )
        probs, lse_row = softmax_parts(scores)
        mixed = matmul(probs.astype(jnp.bfloat16), value_row, "hqk,khd->qhd")
        return (mixed.reshape(local_len, D), lse_row)

    attn_cross, lse_cross = lax.map(cross_forward, (cross_q, memory_all))
    cross_low = attn_cross.astype(jnp.bfloat16)
    branch_two = matmul(cross_low, cout_full, "rcd,de->rce")
    after_cross = after_self + live_rows * branch_two
    normed_three = rms_norm(after_cross, g_ffn.astype(jnp.float32))
    hidden_three = normed_three.astype(jnp.bfloat16)
    gate_up = matmul(hidden_three, gu_full, "rcd,df->rcf")
    gate = gate_up[..., :FF]
    upward = gate_up[..., FF:]
    mixed_ff = (jax.nn.gelu(gate, approximate=True) * upward).astype(jnp.bfloat16)
    branch_three = matmul(mixed_ff, down_full, "rcf,fd->rcd")
    output = (after_cross + live_rows * branch_three).astype(jnp.bfloat16)
    (
        g_self,
        qkv_full,
        out_full,
        bias_full,
        g_cross,
        cq_full,
        ckv_full,
        cout_full,
        g_ffn,
        gu_full,
        down_full,
    ) = (
        lax.all_gather(gain_self, "dp", axis=0, tiled=True),
        lax.all_gather(w_qkv, "dp", axis=0, tiled=True),
        lax.all_gather(w_attn_out, "dp", axis=0, tiled=True),
        lax.all_gather(rel_bias, "dp", axis=0, tiled=True),
        lax.all_gather(gain_cross, "dp", axis=0, tiled=True),
        lax.all_gather(c_query, "dp", axis=0, tiled=True),
        lax.all_gather(c_keyval, "dp", axis=0, tiled=True),
        lax.all_gather(c_out, "dp", axis=0, tiled=True),
        lax.all_gather(gain_ff, "dp", axis=0, tiled=True),
        lax.all_gather(w_gate_up, "dp", axis=0, tiled=True),
        lax.all_gather(w_down, "dp", axis=0, tiled=True),
    )
    grad_out = cotangent.astype(jnp.float32)
    down_in = (live_rows * grad_out).astype(jnp.bfloat16)
    grad_down = matmul(mixed_ff, down_in, "rcf,rcd->fd")
    grad_mixed = matmul(down_in, down_full, "rcd,fd->rcf")
    _, gelu_pull = jax.vjp(
        lambda gate_in, up_in: jax.nn.gelu(gate_in, approximate=True) * up_in, gate, upward
    )
    grad_gate, grad_upward = gelu_pull(grad_mixed)
    grad_gu_low = jnp.concatenate([grad_gate, grad_upward], axis=-1).astype(jnp.bfloat16)
    grad_gate_up = matmul(hidden_three, grad_gu_low, "rcd,rcf->df")
    grad_normed_three = matmul(grad_gu_low, gu_full, "rcf,df->rcd")
    _, pull_three = jax.vjp(rms_norm, after_cross, g_ffn.astype(jnp.float32))
    part_three, grad_gain_ff = pull_three(grad_normed_three)
    grad_after_cross = grad_out + part_three
    cross_in = (live_rows * grad_after_cross).astype(jnp.bfloat16)
    grad_cout = matmul(cross_low, cross_in, "rcd,rce->de")
    grad_cross_attn = matmul(cross_in, cout_full, "rce,de->rcd").astype(jnp.bfloat16)

    def cross_backward(items):
        query_row, kv_row, lse_row, grad_row = items
        queries_h = query_row.reshape(local_len, HEADS, HEAD_DIM)
        grad_h = grad_row.reshape(local_len, HEADS, HEAD_DIM)
        key_row = kv_row[:, :D].reshape(MEM, HEADS, HEAD_DIM)
        value_row = kv_row[:, D:].reshape(MEM, HEADS, HEAD_DIM)
        scores = matmul(queries_h, key_row, "qhd,khd->hqk") * scale
        probs, grad_scores, centre = score_grads(scores, lse_row, value_row, grad_h)
        grad_query = matmul(grad_scores, key_row, "hqk,khd->qhd") * scale
        grad_key = matmul(grad_scores, queries_h, "hqk,qhd->khd") * scale
        grad_value = matmul(probs.astype(jnp.bfloat16), grad_h, "hqk,qhd->khd")
        kv_grads = jnp.concatenate([grad_key.reshape(MEM, D), grad_value.reshape(MEM, D)], axis=-1)
        return (grad_query.reshape(local_len, D), kv_grads, centre)

    grad_cq_rows, grad_memkv_full, _ = lax.map(
        cross_backward, (cross_q, memory_all, lse_cross, grad_cross_attn)
    )
    grad_memkv = lax.psum_scatter(
        grad_memkv_full.astype(jnp.bfloat16), "seq", scatter_dimension=1, tiled=True
    )
    grad_ckv = matmul(memory, grad_memkv, "rmd,rme->de")
    grad_memory = matmul(grad_memkv, ckv_full, "rme,de->rmd").astype(jnp.bfloat16)
    grad_cq_low = grad_cq_rows.astype(jnp.bfloat16)
    grad_cquery = matmul(hidden_two, grad_cq_low, "rcd,rce->de")
    grad_normed_two = matmul(grad_cq_low, cq_full, "rce,de->rcd")
    _, pull_two = jax.vjp(rms_norm, after_self, g_cross.astype(jnp.float32))
    part_two, grad_gain_cross = pull_two(grad_normed_two)
    grad_after_self = grad_after_cross + part_two
    self_in = (live_rows * grad_after_self).astype(jnp.bfloat16)
    grad_wout = matmul(attn_low, self_in, "rcd,rce->de")
    grad_self_attn = matmul(self_in, out_full, "rce,de->rcd").astype(jnp.bfloat16)

    def self_backward(carry, items):
        query_row, kv_row, seg_row, segk_row, lse_row, grad_row = items
        queries_h = query_row.reshape(local_len, HEADS, HEAD_DIM)
        grad_h = grad_row.reshape(local_len, HEADS, HEAD_DIM)
        key_row = kv_row[:, :D].reshape(LEN, HEADS, HEAD_DIM)
        value_row = kv_row[:, D:].reshape(LEN, HEADS, HEAD_DIM)
        scores = self_scores(queries_h, key_row, seg_row, segk_row)
        probs, grad_scores, centre = score_grads(scores, lse_row, value_row, grad_h)
        grad_query = matmul(grad_scores, key_row, "hqk,khd->qhd") * scale
        grad_key = matmul(grad_scores, queries_h, "hqk,qhd->khd") * scale
        grad_value = matmul(probs.astype(jnp.bfloat16), grad_h, "hqk,qhd->khd")
        kv_grads = jnp.concatenate([grad_key.reshape(LEN, D), grad_value.reshape(LEN, D)], axis=-1)
        return (
            carry + grad_scores.astype(jnp.float32),
            (grad_query.reshape(local_len, D), kv_grads, centre),
        )

    zero_block = jnp.zeros((HEADS, local_len, LEN), jnp.float32)
    score_total, (grad_q_rows, grad_kv_full, _) = lax.scan(
        self_backward, zero_block, (queries, key_all, seg_local, seg_all, lse_self, grad_self_attn)
    )
    grad_kv = lax.psum_scatter(
        grad_kv_full.astype(jnp.bfloat16), "seq", scatter_dimension=1, tiled=True
    )
    grad_bias = jnp.einsum(
        "lh,lb->bh",
        unskewed(score_total, seq_index * local_len, local_len),
        bucket_hot,
        precision=highest,
        preferred_element_type=jnp.float32,
    )
    grad_qkv_low = jnp.concatenate([grad_q_rows.astype(jnp.bfloat16), grad_kv], axis=-1)
    grad_wqkv = matmul(hidden_one, grad_qkv_low, "rcd,rce->de")
    grad_normed_one = matmul(grad_qkv_low, qkv_full, "rce,de->rcd")
    _, pull_one = jax.vjp(rms_norm, dense, g_self.astype(jnp.float32))
    part_one, grad_gain_self = pull_one(grad_normed_one)
    grad_inputs = (grad_after_self + part_one).astype(jnp.bfloat16)
    (
        own_gself,
        own_qkv,
        own_wout,
        own_bias,
        own_gcross,
        own_cquery,
        own_ckv,
        own_cout,
        own_gff,
        own_gateup,
        own_down,
    ) = (
        lax.psum_scatter(
            grad_gain_self.astype(jnp.bfloat16), "dp", scatter_dimension=0, tiled=True
        ).astype(jnp.float32),
        lax.psum_scatter(
            grad_wqkv.astype(jnp.bfloat16), "dp", scatter_dimension=0, tiled=True
        ).astype(jnp.float32),
        lax.psum_scatter(
            grad_wout.astype(jnp.bfloat16), "dp", scatter_dimension=0, tiled=True
        ).astype(jnp.float32),
        lax.psum_scatter(
            grad_bias.astype(jnp.bfloat16), "dp", scatter_dimension=0, tiled=True
        ).astype(jnp.float32),
        lax.psum_scatter(
            grad_gain_cross.astype(jnp.bfloat16), "dp", scatter_dimension=0, tiled=True
        ).astype(jnp.float32),
        lax.psum_scatter(
            grad_cquery.astype(jnp.bfloat16), "dp", scatter_dimension=0, tiled=True
        ).astype(jnp.float32),
        lax.psum_scatter(
            grad_ckv.astype(jnp.bfloat16), "dp", scatter_dimension=0, tiled=True
        ).astype(jnp.float32),
        lax.psum_scatter(
            grad_cout.astype(jnp.bfloat16), "dp", scatter_dimension=0, tiled=True
        ).astype(jnp.float32),
        lax.psum_scatter(
            grad_gain_ff.astype(jnp.bfloat16), "dp", scatter_dimension=0, tiled=True
        ).astype(jnp.float32),
        lax.psum_scatter(
            grad_gate_up.astype(jnp.bfloat16), "dp", scatter_dimension=0, tiled=True
        ).astype(jnp.float32),
        lax.psum_scatter(
            grad_down.astype(jnp.bfloat16), "dp", scatter_dimension=0, tiled=True
        ).astype(jnp.float32),
    )
    summed = (
        lax.psum(own_gself.astype(jnp.bfloat16), "seq").astype(jnp.float32),
        lax.psum(own_qkv.astype(jnp.bfloat16), "seq").astype(jnp.float32),
        lax.psum(own_wout.astype(jnp.bfloat16), "seq").astype(jnp.float32),
        lax.psum(own_bias.astype(jnp.bfloat16), "seq").astype(jnp.float32),
        lax.psum(own_gcross.astype(jnp.bfloat16), "seq").astype(jnp.float32),
        lax.psum(own_cquery.astype(jnp.bfloat16), "seq").astype(jnp.float32),
        lax.psum(own_ckv.astype(jnp.bfloat16), "seq").astype(jnp.float32),
        lax.psum(own_cout.astype(jnp.bfloat16), "seq").astype(jnp.float32),
        lax.psum(own_gff.astype(jnp.bfloat16), "seq").astype(jnp.float32),
        lax.psum(own_gateup.astype(jnp.bfloat16), "seq").astype(jnp.float32),
        lax.psum(own_down.astype(jnp.bfloat16), "seq").astype(jnp.float32),
    )
    return (
        output,
        grad_inputs,
        grad_memory,
        summed[0],
        summed[1],
        summed[2],
        summed[3],
        summed[4],
        summed[5],
        summed[6],
        summed[7],
        summed[8],
        summed[9],
        summed[10],
    )


f32, bf16 = jnp.float32, jnp.bfloat16
BIG = 1.0e9
SCALE = HEAD_DIM ** (-0.5)
MESH = pl.DeviceIdType.MESH
GELU_A, GELU_B = 0.7978845608028654, 0.044715
N_SEM, N_LOCAL = 232, 32


def flip(v, k, bits):
    for i in range(bits):
        if (k >> i) & 1:
            b = 1 << i
            v = v + b - 2 * b * lax.rem(lax.div(v, b), 2)
    return v


def dot(a, b):
    return lax.dot_general(a, b, (((1,), (0,)), ((), ())), preferred_element_type=f32)


def dot_nt(a, b):
    return lax.dot_general(a, b, (((1,), (1,)), ((), ())), preferred_element_type=f32)


def dot_tn(a, b):
    return lax.dot_general(a, b, (((0,), (0,)), ((), ())), preferred_element_type=f32)


def inv_rms(v):
    return lax.rsqrt(jnp.mean(v * v, axis=-1, keepdims=True) + epsilon)


def norm_back(v, gain, w):
    r = inv_rms(v)
    gw = gain * w
    mean = jnp.mean(gw * v, axis=-1, keepdims=True)
    return r * gw - v * (r * r * r * mean), jnp.sum(w * (v * r), axis=0, keepdims=True)


def gelu_parts(gate):
    sq = gate * gate
    th = jnp.tanh(GELU_A * gate * (1.0 + GELU_B * sq))
    half = 0.5 * (1.0 + th)
    slope = half + 0.5 * gate * (1.0 - th * th) * (GELU_A * (1.0 + 3.0 * GELU_B * sq))
    return gate * half, slope


def softmax(scores):
    e = jnp.exp(scores - jnp.max(scores, axis=-1, keepdims=True))
    return (e * (1.0 / jnp.sum(e, axis=-1, keepdims=True))).astype(bf16)


def pad64(v):
    return jnp.concatenate([v, jnp.zeros((v.shape[0], 64), v.dtype)], axis=1)


def above64(v):
    return jnp.concatenate([jnp.zeros((v.shape[0], 64), v.dtype), v], axis=1)


def pack(ref, slot, parts):
    ref[slot, 0:256, :] = jnp.concatenate([parts[0], parts[1]], axis=1)
    ref[slot, 256:384, :] = jnp.concatenate([parts[2][0:128], parts[2][128:256]], axis=1)


def unpack(ref, slot):
    two = ref[slot, 0:256, :]
    last = ref[slot, 256:384, :]
    return (two[:, :64], two[:, 64:], jnp.concatenate([last[:, :64], last[:, 64:]], axis=0))


def assemble(ref, dst):
    for t in range(2):
        a = unpack(ref, 2 * t) + unpack(ref, 2 * t + 1)
        for j in range(3):
            at = 384 * t + 128 * j
            dst[:, at : at + 128] = jnp.concatenate([a[2 * j], a[2 * j + 1]], axis=1)


def disperse(val, ref):
    for gg in range(4):
        pack(ref, gg, [val[:, 192 * gg + 64 * h : 192 * gg + 64 * h + 64] for h in range(3)])


def block(i):
    return pl.ds(pl.multiple_of(i * 256, 256), 256)


def layer_kernel(
    x, mem, cot, segs, gain1, gain2, gain3, rel, buck, live, w_in, w_kv, w_ao, w_cq, w_co, w_gu, w_dn,
    out, gin, gmem, o_gu, o_dn, o_b, o_q, o_m, o_small,
    *,
    xrow, mrow, h1, wQ, wM, W3, wgu, wd, sm, sg, gains, lines, hot, tbias, qh, kh, vh, mkv, p_self, p_cross,
    opack, arecv, attn, qpack, qrecv, crecv, cattn, after_self, after_cross, h2, h3, prod, dgu, cotb, frecv,
    hrecv, outb, grad, low, dcq, acc, dqkv, rs1, rs2, rt1, rt2, gur, dnr, bsib, bdp, qdp, mdp, zg1, zg2, zd1, zd2,
    zb1, zb2, qfar, mfar, gsm, sm1, sm2, sgown, ssem, rsem, lsem,
):
    drecv, dqrecv, srecv = arecv, crecv, qrecv
    fown, fpart, xown = tbias.at[2], outb, after_cross
    keep, hpart = p_cross.at[0], low.at[1]

    d, s = lax.axis_index("dp"), lax.axis_index("seq")
    c, z, g, r = lax.rem(s, 2), lax.div(s, 2), lax.rem(s, 4), lax.div(s, 4)
    used = {"remote": 0, "local": 0}
    flying = []

    def remote(src, dst, send_sem, recv_sem, dev):
        return pltpu.make_async_remote_copy(
            src_ref=src, dst_ref=dst, send_sem=ssem.at[send_sem], recv_sem=rsem.at[recv_sem],
            device_id=dev, device_id_type=MESH,
        )

    def fresh(n=1):
        used["remote"] += n
        assert used["remote"] <= N_SEM
        return used["remote"] - n

    def push(src, dst, dev):
        sem = fresh()
        copy = remote(src, dst, sem, sem, dev)
        copy.start()
        flying.append(copy)
        return copy

    def sent(copies):
        for copy in copies:
            copy.wait_send()
            flying[:] = [other for other in flying if other is not copy]

    def arrived(copies):
        for copy in copies:
            copy.wait_recv()

    def local(src, dst):
        copy = pltpu.make_async_copy(src, dst, lsem.at[used["local"]])
        used["local"] += 1
        copy.start()
        return copy

    def dpk(k):
        return (flip(d, k, 2), s)

    def seqk(k):
        return (d, flip(s, k, 3))

    class Gather:
        def __init__(self, whole, part):
            self.part = part
            own = whole(d)
            self.first = {k: push(own, own, dpk(k)) for k in (1, 2)}
            self.second = []

        def relay(self):
            for k, half in ((1, 0), (2, 1)):
                arrived([self.first[k]])
                src = self.part(flip(d, k, 2), half)
                self.second.append(push(src, src, dpk(3 - k)))

        def done(self):
            arrived(self.second)

        def gone(self):
            sent([*self.first.values(), *self.second])

    class Reduce:
        def __init__(self, part, got):
            self.part, self.got = part, got
            self.first = {}
            for k, half in ((1, 0), (2, 1)):
                for j, kk in ((0, k), (1, 3)):
                    copy = push(part(flip(d, kk, 2), half), got.at[3 * half + j], dpk(k))
                    self.first[half, j] = copy

        def middle(self):
            self.second = {}
            for k, half in ((1, 0), (2, 1)):
                arrived([self.first[half, 1]])
                ref = self.part(flip(d, 3 - k, 2), half)
                ref[...] = (ref[...].astype(f32) + self.got[3 * half + 1].astype(f32)).astype(bf16)
                self.second[half] = push(ref, self.got.at[3 * half + 2], dpk(3 - k))

        def end(self):
            for half in (0, 1):
                arrived([self.first[half, 0], self.second[half]])
                ref = self.part(d, half)
                total = ref[...].astype(f32) + self.got[3 * half].astype(f32) + self.got[3 * half + 2].astype(f32)
                ref[...] = total.astype(bf16)

    def moved(srcs, dsts, devs, slot):
        base = fresh(2)
        for i in range(2):
            away = remote(srcs[i], dsts[i], base + i, base + slot, (d, devs[i]))
            here = pltpu.make_async_copy(srcs[i], dsts[i], rsem.at[base + slot])

            @pl.when(devs[i] != s)
            def _():
                away.start()

            @pl.when(devs[i] == s)
            def _():
                here.start()

        def wait_recv(places):
            for i in range(2):
                pltpu.make_async_copy(places[i], places[i], rsem.at[base + i]).wait()

        def wait_send():
            for i in range(2):
                away = remote(srcs[i], dsts[i], base + i, base + slot, (d, devs[i]))

                @pl.when(devs[i] != s)
                def _():
                    away.wait_send()

        return wait_recv, wait_send

    mine, mine_d = pl.ds(pl.multiple_of(d * 192, 64), 192), block(d)
    here = pl.ds(s * 128, 128)
    own_x = local(x.at[r], xrow.at[here])
    stage = [p_self.at[0, i, 0:192] for i in range(4)] + [p_self.at[1, 0, 0:192]]
    own_in = [
        local(w.at[:, 768 * i : 768 * i + 768], stage[p])
        for p, (w, i) in enumerate(((w_in, 0), (w_in, 1), (w_in, 2), (w_kv, 0), (w_kv, 1)))
    ]
    own_W3 = [local(w, W3.at[i, mine]) for i, w in enumerate((w_ao, w_cq, w_co))]
    own_m = local(mem.at[r], mrow.at[here])
    own_gu = []
    for p in range(8):
        at = pl.multiple_of((p // 4) * FF + (p % 4) * 512 + c * 256, 256)
        own_gu.append(local(w_gu.at[:, pl.ds(at, 256)], wgu.at[mine, pl.ds(512 * (p % 4) + 256 * (p // 4), 256)]))
    own_dn = local(w_dn.at[block(c)], wd.at[mine_d])

    barrier = pltpu.get_barrier_semaphore()
    peers = [dpk(k) for k in (1, 2, 3)] + [seqk(k) for k in range(1, 8)]
    for p in peers:
        pl.semaphore_signal(barrier, inc=1, device_id=p, device_id_type=MESH)
    for i in range(2):
        sgown[i] = jnp.broadcast_to(segs[i : i + 1, :].astype(f32), (16, 128)).astype(bf16)
    sg[s] = sgown[r]
    at_bucket = lax.broadcasted_iota(jnp.int32, (8, 128), 1) == lax.broadcasted_iota(jnp.int32, (8, 128), 0) + 8 * d
    gains[...] = jnp.zeros((16, 768), f32)
    gains[0:12, 0:128] = dot_tn(rel[...].astype(f32), at_bucket.astype(f32))
    for q in range(4):

        @pl.when(d == q)
        def _():
            for i, gain in enumerate((gain1, gain2, gain3)):
                gains[12 + i : 13 + i, 192 * q : 192 * q + 192] = gain[...].astype(f32).reshape(1, 192)

    sm[d] = gains[...].astype(bf16)
    pl.semaphore_wait(barrier, len(peers))

    def row_of(k):
        return lax.div(flip(s, k, 3), 4)

    def spread(src, dst):
        return {m: push(src.at[row_of(2 * m)], dst.at[here], seqk(2 * m)) for m in (1, 2, 3)}

    def hand_on(dst, m):
        part = dst.at[pl.ds(flip(s, 2 * m, 3) * 128, 128)]
        return push(part, part, seqk(1))

    sm_in = [push(sm.at[d], sm.at[d], dpk(k)) for k in (1, 2, 3)]
    sg_in = [push(sgown.at[row_of(k)], sg.at[s], seqk(k)) for k in range(1, 8)]
    xd = spread(x, xrow)
    own_x.wait()
    xs = {0: hand_on(xrow, 0)}
    for cp in own_in:
        cp.wait()
    for q in range(4):

        @pl.when(g == q)
        def _():
            for p in range(5):
                dst, at = (wQ, 192 * p) if p < 3 else (wM, 192 * (p - 3))
                dst[mine, at : at + 192] = stage[p][:, 192 * q : 192 * q + 192]

    def part192(ref):
        return lambda dd, half: ref.at[pl.ds(pl.multiple_of(dd * 192 + 96 * half, 32), 96)]

    def whole192(ref):
        return lambda dd: ref.at[pl.ds(pl.multiple_of(dd * 192, 64), 192)]

    def part_dn(dd, half):
        return wd.at[pl.ds(pl.multiple_of(dd * 256 + 128 * half, 128), 128)]

    def part_b(i):
        return lambda dd, half: W3.at[i, pl.ds(pl.multiple_of(dd * 192 + c * 96 + 48 * half, 16), 48)]

    q_w = Gather(whole192(wQ), part192(wQ))

    def half_rows(dd, cc):
        return pl.ds(pl.multiple_of(dd * 192 + cc * 96, 32), 96)

    def send_W3(i):
        own_W3[i].wait()
        return Gather(lambda dd: W3.at[i, half_rows(dd, c)], part_b(i))

    def share_W3(i):
        W3_w[i].done()
        return [push(W3.at[i, rows], W3.at[i, rows], seqk(1)) for rows in (half_rows(flip(d, k, 2), c) for k in (1, 2, 3))]

    m_w = Gather(whole192(wM), part192(wM))
    W3_w = {0: send_W3(0)}
    W3_sib = {}

    arrived(sm_in)
    total = sm[0].astype(f32)
    for i in range(1, 4):
        total += sm[i].astype(f32)
    gains[...] = total
    near = jnp.concatenate([buck[i : i + 1, :] for i in range(4)], axis=1)
    by_dist = (lax.broadcasted_iota(jnp.int32, (128, 512), 0) == near).astype(bf16)
    turn = lax.broadcasted_iota(jnp.int32, (512, 1024), 0) + lax.broadcasted_iota(jnp.int32, (512, 1024), 1) == 768
    hot[...] = dot(by_dist, turn.astype(bf16)).astype(bf16)
    column = lax.broadcasted_iota(jnp.int32, (16, 1024), 1)
    line = dot(total[:, :128].astype(bf16), hot[...])
    lines[...] = jnp.where((column > 256) & (column < 769), line, masked_score)
    for h in range(3):
        row = jnp.broadcast_to(lines[pl.ds(3 * g + h, 1), :], (256, 1024))
        tbias[h] = pltpu.roll(row, 0, 1, stride=1, stride_axis=0)[:, 256:]

    def norm_block(m):
        rows = block(flip(z, m, 2))
        val = xrow[rows, :].astype(f32)
        h1[rows, :] = (val * inv_rms(val) * gains[12:13, :]).astype(bf16)

    arrived([xs[0]])
    norm_block(0)
    for m in (1, 2):
        arrived([xd[m]])
        xs[m] = hand_on(xrow, m)
    q_w.relay()
    arrived([xs[1]])
    norm_block(1)
    m_w.relay()
    W3_w[1] = send_W3(1)
    arrived([xd[3]])
    xs[3] = hand_on(xrow, 3)
    md = spread(mem, mrow)
    own_m.wait()
    ms = {0: hand_on(mrow, 0)}
    W3_w[0].relay()
    W3_w[2] = send_W3(2)
    arrived([xs[2]])
    norm_block(2)
    arrived([xs[3]])
    norm_block(3)

    arrived(sg_in)
    lane64 = lax.broadcasted_iota(jnp.int32, (128, 64), 1).astype(f32)
    inside = lane64 < 3.5
    for h in range(3):
        beyond = lax.broadcasted_iota(jnp.int32, (512, 128), 1) >= 64
        kh[h, 0:512, :] = jnp.where(beyond, -1.0, 0.0).astype(bf16)
        vh[h, 0:512, :] = jnp.zeros((512, 128), bf16)
    q_w.done()

    def project(i, carry):
        rows = block(i)
        res = dot(h1[rows, :], wQ[...]).astype(bf16)
        qa, ka = [], []
        for j in range(2):
            seg = sg[2 * i + j, 0:1, :].astype(f32)
            same = jnp.transpose(jnp.broadcast_to(seg, (128, 128)))[:, :64] == lane64
            qa.append(jnp.where(same, BIG, 0.0))
            ka.append(jnp.where(inside & jnp.logical_not(same), -1.0, 0.0))
        qa = jnp.concatenate(qa, axis=0).astype(bf16)
        ka = jnp.concatenate(ka, axis=0).astype(bf16)
        lower = pl.ds(pl.multiple_of(i * 256 + 512, 256), 256)
        for h in range(3):
            qv = (res[:, 64 * h : 64 * h + 64].astype(f32) * SCALE).astype(bf16)
            qh[h, rows, :] = jnp.concatenate([qv, qa], axis=1)
            kh[h, lower, :] = jnp.concatenate([res[:, 192 + 64 * h : 256 + 64 * h], ka], axis=1)
            vh[h, lower, :] = pad64(res[:, 384 + 64 * h : 448 + 64 * h])
        return carry

    lax.fori_loop(0, 4, project, 0)

    for cp in own_gu:
        cp.wait()
    gu_w = Gather(whole192(wgu), part192(wgu))
    W3_w[1].relay()

    def window(b):
        return pl.ds(pl.multiple_of(b * 256, 256), 768)

    a_in = []
    for k in (2, 3, 1, 0):
        b = flip(g, k, 2)
        parts = []
        for h in range(3):
            p = softmax(dot_nt(qh[h, block(b), :], kh[h, window(b), :]) + tbias[h])
            p_self[h, b] = p
            parts.append(dot(p, vh[h, window(b), :])[:, :64].astype(bf16))
        if k == 0:
            pack(arecv, g, parts)
        else:
            pack(opack, b, parts)
            a_in.append(push(opack.at[b], arecv.at[g], seqk(k)))
        if k == 2:
            W3_w[2].relay()

    own_dn.wait()
    dn_w = Gather(lambda dd: wd.at[block(dd)], part_dn)
    for m in (1, 2, 3):
        arrived([md[m]])
        ms[m] = hand_on(mrow, m)
    halves = [cotb.at[c, pl.ds(c * 128, 128)]] * 2
    dests = [4 * rr + z for rr in range(2)]
    cslot = lax.rem(z, 2)
    cot_recv, cot_sent = moved(
        [cot.at[0], cot.at[1]], [cotb.at[cslot, pl.ds(c * 128, 128)]] * 2, dests, c
    )
    W3_sib[0] = share_W3(0)
    m_w.done()
    arrived(ms.values())

    def project_memory(i, carry):
        rows = block(i)
        res = dot(mrow[rows, :], wM[...]).astype(bf16)
        for h in range(3):
            mkv[h, rows, :] = jnp.concatenate(
                [res[:, 64 * h : 64 * h + 64], res[:, 192 + 64 * h : 256 + 64 * h]], axis=1
            )
        return carry

    lax.fori_loop(0, 4, project_memory, 0)
    W3_sib[1] = share_W3(1)

    arrived(a_in)
    assemble(arecv, attn)
    arrived(W3_sib[0])
    alive = live[r].astype(f32)
    res = xrow[block(g), :].astype(f32) + alive * dot(attn[...], W3[0])
    after_self[...] = res
    h2[...] = (res * inv_rms(res) * gains[13:14, :]).astype(bf16)
    arrived(W3_sib[1])
    disperse((dot(h2[...], W3[1]).astype(bf16).astype(f32) * SCALE).astype(bf16), qpack)
    q_in = {k: push(qpack.at[flip(g, k, 2)], qrecv.at[g], seqk(k)) for k in (2, 3, 1)}
    qrecv[g] = qpack[g]
    gu_w.relay()
    cot_recv([cotb.at[c, pl.ds(0, 128)], cotb.at[c, pl.ds(128, 128)]])
    cot_sib = push(cotb.at[c], cotb.at[c], seqk(1))

    sent(a_in)
    c_in = []
    for k in (0, 1, 2, 3):
        b = flip(g, k, 2)
        if k:
            arrived([q_in[k]])
        qs = unpack(qrecv, b)
        parts = []
        for h in range(3):
            p = softmax(dot_nt(pad64(qs[h]), mkv[h]))
            p_cross[h, b] = p
            parts.append(dot(p, mkv[h])[:, 64:].astype(bf16))
        if k == 0:
            pack(crecv, g, parts)
        else:
            pack(opack, b, parts)
            c_in.append(push(opack.at[b], crecv.at[g], seqk(k)))
        if k == 0:
            W3_sib[2] = share_W3(2)
        if k == 1:
            dn_w.relay()
    arrived(W3_sib[2])
    arrived(c_in)
    assemble(crecv, cattn)
    res = after_self[...] + alive * dot(cattn[...], W3[2])
    after_cross[...] = res
    h3[c] = (res * inv_rms(res) * gains[14:15, :]).astype(bf16)
    h3_in = push(h3.at[c], h3.at[c], seqk(1))
    arrived([cot_sib])
    gu_w.done()
    dn_w.done()
    arrived([h3_in])

    gu_w.gone()
    dn_w.gone()
    tbias[0:2] = jnp.zeros((2, 256, 768), f32)

    def feed_forward(n, carry):
        cols = block(n)
        both = pl.ds(pl.multiple_of(n * 512, 512), 512)
        gates, ups = pl.ds(pl.multiple_of(n * 512, 512), 256), pl.ds(pl.multiple_of(n * 512 + 256, 256), 256)
        for t in range(2):
            gate, up = dot(h3[t], wgu[:, gates]), dot(h3[t], wgu[:, ups])
            act, slope = gelu_parts(gate)
            prod[t, :, cols] = (act * up).astype(bf16)
            gp = dot_nt((cotb[t].astype(f32) * alive).astype(bf16), wd[cols, :])
            dgu[t, :, gates] = (gp * up * slope).astype(bf16)
            dgu[t, :, ups] = (gp * act).astype(bf16)
            tbias[t] += dot_nt(dgu[t, :, both], wgu[:, both])
        for part in (gates, ups):
            wgu[:, part] = dot_tn(h3[...].reshape(512, 768), dgu[:, :, part].reshape(512, 256)).astype(bf16)
        return carry

    def grad_dn(n, carry):
        cols = block(n)
        down_in = (cotb[...].astype(f32) * alive).astype(bf16).reshape(512, 768)
        wd[cols, :] = dot_tn(prod[:, :, cols].reshape(512, 256), down_in).astype(bf16)
        return carry

    def part_gu(i):
        cols = pl.ds(1024 * i, 1024)
        return lambda dd, half: wgu.at[pl.ds(pl.multiple_of(dd * 192 + 96 * half, 32), 96), cols]

    far_side = lax.div(z, 2)
    outer = lax.rem(z, 2) == far_side
    inner = jnp.logical_not(outer)

    def push_if(src, dst, dev, sends, gets):
        copy = remote(src, dst, fresh(1), used["remote"] - 1, dev)

        class Copy:
            def wait_send(self):
                pl.when(sends)(copy.wait_send)

            def wait_recv(self):
                pl.when(gets)(copy.wait_recv)

        pl.when(sends)(copy.start)
        res = Copy()
        flying.append(res)
        return res

    class Around:
        def __init__(self, own, out, half, got):
            self.own, self.out, self.half, self.got = own, out, half, got

        def add(self, ref, got):
            @pl.when(inner)
            def _():
                ref[...] = (ref[...].astype(f32) + got[...].astype(f32)).astype(bf16)

        def step1(self):
            self.copy = push_if(self.own, self.got[0], seqk(2), outer, inner)

        def step2(self):
            arrived([self.copy])
            self.add(self.own, self.got[0])
            self.copy = push_if(self.half(self.own, 1 - far_side), self.got[1], seqk(6), inner, inner)

        def step3(self):
            arrived([self.copy])
            src, dst = self.half(self.own, far_side), self.half(self.out, far_side)
            self.add(src, self.got[1])
            self.copy = push_if(src, dst, seqk(6), inner, inner)
            self.back = [push_if(src, dst, seqk(2), inner, outer)]
            self.keep = pltpu.make_async_copy(src, dst, lsem.at[used["local"]])
            used["local"] += 1
            pl.when(inner)(self.keep.start)

        def step4(self):
            arrived([self.copy])
            pl.when(inner)(self.keep.wait)
            place = self.half(self.out, 1 - far_side)
            self.back.append(push_if(place, place, seqk(2), inner, outer))

        def step5(self):
            arrived(self.back)
            self.copy = push(self.out, self.out, seqk(1))

    def halves(n):
        return lambda ref, i: ref.at[pl.ds(pl.multiple_of(n * i, 16), n)]

    cols_gu = [pl.ds(1024 * i, 1024) for i in range(2)]
    g_z, u_z = [
        Around(wgu.at[mine, cols_gu[i]], o_gu.at[c, :, cols_gu[i]], halves(96), (zg1.at[i], zg2.at[i])) for i in range(2)
    ]
    n_z = Around(wd.at[mine_d], o_dn.at[c], halves(128), (zd1, zd2))
    b_z = [Around(W3.at[i, half_rows(d, c)], o_b.at[i, c], halves(48), (zb1.at[i], zb2.at[i])) for i in range(3)]

    lax.fori_loop(0, 2, feed_forward, 0)
    g_rs = Reduce(part_gu(0), gur.at[0])
    lax.fori_loop(2, 4, feed_forward, 0)
    u_rs = Reduce(part_gu(1), gur.at[1])
    hpart[...] = tbias[1 - c].astype(bf16)
    h_in = push(hpart, hrecv, seqk(1))
    fpart[...] = dot(prod[1 - c], wd[...]).astype(bf16)
    f_in = push(fpart, frecv, seqk(1))
    arrived([h_in])
    dv, dgain3 = norm_back(after_cross[...], gains[14:15, :], tbias[c] + hrecv[...].astype(f32))
    gsm[...] = jnp.zeros((16, 768), f32)
    gsm[14:15, :] = dgain3
    grad[...] = cotb[c].astype(f32) + dv
    low[0] = (grad[...] * alive).astype(bf16)
    sent(c_in)
    sent(q_in.values())
    disperse(dot_nt(low[0], W3[2]).astype(bf16), opack)
    d_in = {k: push(opack.at[flip(g, k, 2)], drecv.at[g], seqk(k)) for k in (2, 3, 1)}
    drecv[g] = opack[g]
    g_rs.middle()
    fown[...] = dot(prod[c], wd[...])
    lax.fori_loop(0, 4, grad_dn, 0)

    arrived([f_in])
    sent([f_in])
    outb[...] = (after_cross[...] + alive * (fown[...] + frecv[...].astype(f32))).astype(bf16)
    back = [2 * g + j for j in range(2)]
    out_recv, out_sent = moved([outb.at[pl.ds(0, 128)], outb.at[pl.ds(128, 128)]], [out.at[r]] * 2, back, r)

    lefts = (attn, h2, cattn)
    rights = (low.at[1], dcq, low.at[0])
    b_sib = {}

    def grad_square(i):
        W3_w[i].gone()
        sent(W3_sib[i])
        W3[i] = dot_tn(lefts[i][...], rights[i][...]).astype(bf16)
        b_sib[i] = [push(W3.at[i, half_rows(q, 1 - c)], bsib.at[i, q], seqk(1)) for q in range(4)]

    def chip_square(i):
        arrived(b_sib[i])
        for q in range(4):
            rows = half_rows(q, c)
            W3[i, rows, :] = (W3[i, rows, :].astype(f32) + bsib[i, q].astype(f32)).astype(bf16)
        return Reduce(part_b(i), bdp.at[i])

    grad_square(2)

    for h in range(3):
        acc[h, 0:1024, :] = jnp.zeros((1024, 128), f32)
    dq_in = []

    def cross_back(k):
        b = flip(g, k, 2)
        if k:
            arrived([d_in[k]])
        dos, qs = unpack(drecv, b), unpack(qrecv, b)
        parts = []
        for h in range(3):
            p = p_cross[h, b]
            do = above64(dos[h])
            dp = dot_nt(do, mkv[h])
            pf = p.astype(f32)
            ds = (pf * (dp - jnp.sum(dp * pf, axis=-1, keepdims=True))).astype(bf16)
            parts.append((dot(ds, mkv[h])[:, :64] * SCALE).astype(bf16))
            acc[h, 0:1024, :] += dot_tn(ds, pad64(qs[h])) + dot_tn(p, do)
        if k == 0:
            pack(dqrecv, g, parts)
        else:
            pack(qpack, b, parts)
            dq_in.append(push(qpack.at[b], dqrecv.at[g], seqk(k)))

    cross_back(2)
    n_rs = Reduce(part_dn, dnr)
    cross_back(3)
    u_rs.middle()
    cross_back(1)
    g_rs.end()
    g_z.step1()
    cross_back(0)
    b_rs = {2: chip_square(2)}

    def keep_memory(i, carry):
        rows = block(i)
        vals = [acc[h, rows, :][:, :64] for h in range(3)] + [acc[h, rows, :][:, 64:] for h in range(3)]
        dqkv[rows, 0:384] = jnp.concatenate(vals, axis=1).astype(bf16)
        return carry

    lax.fori_loop(0, 4, keep_memory, 0)
    arrived(dq_in)
    assemble(dqrecv, dcq)
    dv, dgain2 = norm_back(after_self[...], gains[13:14, :], dot_nt(dcq[...], W3[1]))
    gsm[13:14, :] = dgain2
    grad[...] += dv
    sent([h_in])
    low[1] = (grad[...] * alive).astype(bf16)
    sent(d_in.values())
    disperse(dot_nt(low[1], W3[0]).astype(bf16), opack)
    s_in = {k: push(opack.at[flip(g, k, 2)], srecv.at[g], seqk(k)) for k in (2, 3, 1)}
    srecv[g] = opack[g]

    u_rs.end()
    u_z.step1()
    n_rs.middle()
    grad_square(1)
    grad_square(0)

    class Rows:
        def __init__(self, compute, first, second):
            self.compute, self.first, self.second = compute, first, second
            self.in3 = push(compute(flip(g, 3, 2)), first.at[0], seqk(1))
            self.part2 = compute(flip(g, 2, 2))
            self.in1 = push(compute(flip(g, 1, 2)), first.at[1], seqk(1))

        def far(self):
            arrived([self.in3])
            self.part2[...] = (self.part2[...].astype(f32) + self.first[0].astype(f32)).astype(bf16)
            self.out = push(self.part2, self.second, seqk(2))
            self.part0 = self.compute(g)

        def total(self):
            arrived([self.in1, self.out])
            return self.part0[...].astype(f32) + self.first[1].astype(f32) + self.second[...].astype(f32)

    m_w.gone()
    sent(ms.values())
    for i in range(3):
        keep[i, :, 0:384] = dot_tn(mrow[:, 256 * i : 256 * i + 256], dqkv[:, 0:384]).astype(bf16)

    def memory_part(b):
        mrow[block(b), :] = dot_nt(dqkv[block(b), 0:384], wM[...]).astype(bf16)
        return mrow.at[block(b)]

    m_rows = Rows(memory_part, rt1, rt2)
    m_rows.far()
    for i in range(3):
        wM[256 * i : 256 * i + 256, :] = keep[i, :, 0:384]

    g_z.step2()
    m_rs = Reduce(part192(wM), mdp)

    for h in range(3):
        acc[h] = jnp.zeros((1536, 128), f32)
        tbias[h] = jnp.zeros((256, 768), f32)

    def self_back(k):
        b = flip(g, k, 2)
        if k:
            arrived([s_in[k]])
        dos = unpack(srecv, b)
        for h in range(3):
            p = p_self[h, b]
            do = pad64(dos[h])
            dp = dot_nt(do, vh[h, window(b), :])
            pf = p.astype(f32)
            ds = pf * (dp - jnp.sum(dp * pf, axis=-1, keepdims=True))
            tbias[h] += ds
            ds = ds.astype(bf16)
            dqkv[block(b), 64 * h : 64 * h + 64] = (dot(ds, kh[h, window(b), :])[:, :64] * SCALE).astype(bf16)
            acc[h, window(b), :] += dot_tn(ds, pad64(qh[h, block(b), :][:, :64])) + dot_tn(p, above64(dos[h]))

    self_back(0)
    b_rs[1] = chip_square(1)
    b_rs[0] = chip_square(0)
    n_rs.end()
    n_z.step1()
    g_z.step3()
    self_back(2)
    m_rs.middle()
    b_rs[2].middle()
    u_z.step2()
    self_back(3)
    g_z.step4()

    total = m_rows.total()
    out_recv([out.at[0], out.at[1]])
    out_sent()
    outb[...] = total.astype(bf16)
    mem_recv, mem_sent = moved([outb.at[pl.ds(0, 128)], outb.at[pl.ds(128, 128)]], [gmem.at[r]] * 2, back, r)

    self_back(1)
    u_z.step3()

    def keep_self(i, carry):
        rows, lower = block(i), pl.ds(pl.multiple_of(i * 256 + 512, 256), 256)
        for h in range(3):
            dqkv[rows, 192 + 64 * h : 256 + 64 * h] = acc[h, lower, :][:, :64].astype(bf16)
            dqkv[rows, 384 + 64 * h : 448 + 64 * h] = acc[h, lower, :][:, 64:].astype(bf16)
        return carry

    lax.fori_loop(0, 4, keep_self, 0)
    xown[...] = xrow[block(g), :].astype(f32)
    sent(xs.values())

    def self_part(b):
        xrow[block(b), :] = dot_nt(dqkv[block(b), :], wQ[...]).astype(bf16)
        return xrow.at[block(b)]

    x_rows = Rows(self_part, rs1, rs2)
    x_rows.far()
    m_rs.end()
    m_far = push(wM.at[mine], mfar, seqk(4))
    b_rs[1].middle()
    b_rs[0].middle()
    n_z.step2()
    q_w.gone()

    def grad_qkv(n, carry):
        cols = pl.ds(pl.multiple_of(n * 128, 128), 128)
        wQ[cols, :] = dot_tn(h1[:, cols], dqkv[...]).astype(bf16)
        return carry

    lax.fori_loop(0, 6, grad_qkv, 0)
    q_rs = Reduce(part192(wQ), qdp)

    b_rs[2].end()
    b_z[2].step1()

    for h in range(3):
        wide = jnp.concatenate([jnp.zeros((256, 256), f32), tbias[h]], axis=1)
        rows = lax.broadcasted_iota(jnp.int32, (256, 1024), 0)
        for i in range(8):
            bit = lax.rem(lax.div(rows, 1 << i), 2) == 1
            wide = jnp.where(bit, pltpu.roll(wide, 1024 - (1 << i), 1), wide)
        lines[h : h + 1, :] = jnp.sum(wide, axis=0, keepdims=True)
    val = lines[...]
    top = val.astype(bf16)
    rest = val - top.astype(f32)
    mid = rest.astype(bf16)
    last = (rest - mid.astype(f32)).astype(bf16)
    by_bucket = dot_nt(top, hot[...]) + dot_nt(mid, hot[...]) + dot_nt(last, hot[...])
    row16 = lax.broadcasted_iota(jnp.int32, (16, 128), 0)
    spot = jnp.zeros((16, 128), f32)
    for h in range(3):
        spot = jnp.where(row16 == 3 * g + h, jnp.broadcast_to(by_bucket[h : h + 1, :], (16, 128)), spot)
    gsm[:, 0:128] += spot

    for i in (1, 0):
        b_rs[i].end()
        b_z[i].step1()
    u_z.step4()
    g_z.step5()
    n_z.step3()
    q_rs.middle()

    b_z[2].step2()
    q_rs.end()
    q_far = push(wQ.at[mine], qfar, seqk(4))

    dv, dgain1 = norm_back(xown[...], gains[12:13, :], x_rows.total())
    gsm[12:13, :] = dgain1
    sm_dp = [push(gsm, sm1.at[k - 1], dpk(k)) for k in (1, 2, 3)]
    mem_recv([gmem.at[0], gmem.at[1]])
    mem_sent()
    outb[...] = (grad[...] + dv).astype(bf16)
    gin_recv, gin_sent = moved([outb.at[pl.ds(0, 128)], outb.at[pl.ds(128, 128)]], [gin.at[r]] * 2, back, r)

    def far_sum(ref, copy, got, place):
        arrived([copy])
        sent([copy])
        ref[mine, :] = (ref[mine, :].astype(f32) + got[...].astype(f32)).astype(bf16)
        here_too = local(ref.at[mine], place.at[g])
        return here_too, push(ref.at[mine], place.at[g], seqk(2)), push(ref.at[mine], place.at[g], seqk(1))

    m_own, m_pair, m_s1 = far_sum(wM, m_far, mfar, o_m)
    n_z.step4()
    u_z.step5()
    b_z[1].step2()
    b_z[0].step2()
    b_z[2].step3()
    arrived(sm_dp)
    sent(sm_dp)
    gsm[...] = gsm[...] + sm1[0] + sm1[1] + sm1[2]
    sm_seq = [push(gsm, sm2.at[k - 1], seqk(k)) for k in range(1, 8)]
    q_own, q_pair, q_s1 = far_sum(wQ, q_far, qfar, o_q)
    b_z[1].step3()
    b_z[0].step3()
    b_z[2].step4()
    n_z.step5()
    b_z[1].step4()
    b_z[0].step4()
    arrived(sm_seq)
    val = gsm[...]
    for k in range(7):
        val = val + sm2[k]
    o_small[...] = val
    other = flip(g, 2, 2)
    arrived([m_pair])
    m_s2 = push(o_m.at[other], o_m.at[other], seqk(1))
    arrived([q_pair])
    q_s2 = push(o_q.at[other], o_q.at[other], seqk(1))
    for i in (2, 1, 0):
        b_z[i].step5()
    gin_recv([gin.at[0], gin.at[1]])
    gin_sent()
    cot_sent()
    m_own.wait()
    q_own.wait()
    arrived([m_s1, q_s1, m_s2, q_s2])
    for chain in (g_z, u_z, n_z, *b_z):
        arrived([chain.copy])
    for cp in list(flying):
        cp.wait_send()


def scratch():
    def vm(kind, *shape):
        return pltpu.VMEM(shape, kind)

    return dict(
        xrow=vm(bf16, 1024, 768),
        mrow=vm(bf16, 1024, 768),
        h1=vm(bf16, 1024, 768),
        wQ=vm(bf16, 768, 576),
        wM=vm(bf16, 768, 384),
        W3=vm(bf16, 3, 768, 768),
        wgu=vm(bf16, 768, 2048),
        wd=vm(bf16, 1024, 768),
        sm=vm(bf16, 4, 16, 768),
        sg=vm(bf16, 8, 16, 128),
        gains=vm(f32, 16, 768),
        lines=vm(f32, 16, 1024),
        hot=vm(bf16, 128, 1024),
        tbias=vm(f32, 3, 256, 768),
        qh=vm(bf16, 3, 1024, 128),
        kh=vm(bf16, 3, 1536, 128),
        vh=vm(bf16, 3, 1536, 128),
        mkv=vm(bf16, 3, 1024, 128),
        p_self=vm(bf16, 3, 4, 256, 768),
        p_cross=vm(bf16, 3, 4, 256, 1024),
        opack=vm(bf16, 4, 384, 128),
        arecv=vm(bf16, 4, 384, 128),
        attn=vm(bf16, 256, 768),
        qpack=vm(bf16, 4, 384, 128),
        qrecv=vm(bf16, 4, 384, 128),
        crecv=vm(bf16, 4, 384, 128),
        cattn=vm(bf16, 256, 768),
        after_self=vm(f32, 256, 768),
        after_cross=vm(f32, 256, 768),
        h2=vm(bf16, 256, 768),
        h3=vm(bf16, 2, 256, 768),
        prod=vm(bf16, 2, 256, 1024),
        dgu=vm(bf16, 2, 256, 2048),
        cotb=vm(bf16, 2, 256, 768),
        frecv=vm(bf16, 256, 768),
        hrecv=vm(bf16, 256, 768),
        outb=vm(bf16, 256, 768),
        grad=vm(f32, 256, 768),
        low=vm(bf16, 2, 256, 768),
        dcq=vm(bf16, 256, 768),
        acc=vm(f32, 3, 1536, 128),
        dqkv=vm(bf16, 1024, 576),
        rs1=vm(bf16, 2, 256, 768),
        rs2=vm(bf16, 256, 768),
        rt1=vm(bf16, 2, 256, 768),
        rt2=vm(bf16, 256, 768),
        gur=vm(bf16, 2, 6, 96, 1024),
        dnr=vm(bf16, 6, 128, 768),
        bsib=vm(bf16, 3, 4, 96, 768),
        bdp=vm(bf16, 3, 6, 48, 768),
        qdp=vm(bf16, 6, 96, 576),
        mdp=vm(bf16, 6, 96, 384),
        zg1=vm(bf16, 2, 192, 1024),
        zg2=vm(bf16, 2, 96, 1024),
        zd1=vm(bf16, 256, 768),
        zd2=vm(bf16, 128, 768),
        zb1=vm(bf16, 3, 96, 768),
        zb2=vm(bf16, 3, 48, 768),
        qfar=vm(bf16, 192, 576),
        mfar=vm(bf16, 192, 384),
        gsm=vm(f32, 16, 768),
        sm1=vm(f32, 3, 16, 768),
        sm2=vm(f32, 7, 16, 768),
        sgown=vm(bf16, 2, 16, 128),
        ssem=pltpu.SemaphoreType.DMA((N_SEM,)),
        rsem=pltpu.SemaphoreType.DMA((N_SEM,)),
        lsem=pltpu.SemaphoreType.DMA((N_LOCAL,)),
    )


def finish_kernel(
    out, gin, gmem, o_gu, o_dn, o_b, o_q, o_m, o_small,
    y_out, y_gin, y_gmem, y_g1, y_qkv, y_ao, y_rel, y_g2, y_cq, y_kv, y_co, y_g3, y_gu, y_dn, rel_t,
):
    d = lax.axis_index("dp")
    y_out[...] = out[...]
    y_gin[...] = gin[...]
    y_gmem[...] = gmem[...]
    for half in range(2):
        for q in range(4):
            for c in range(2):
                at = 2048 * half + 512 * q + 256 * c
                y_gu[:, at : at + 256] = o_gu[c, :, 512 * q + 256 * half : 512 * q + 256 * half + 256].astype(f32)
    y_dn[...] = o_dn[...].astype(f32)
    for i, y in enumerate((y_ao, y_cq, y_co)):
        y[...] = o_b[i, 0].astype(f32)
    for p in range(5):
        y, src, i = (y_qkv, o_q, p) if p < 3 else (y_kv, o_m, p - 3)
        for t in range(2):
            two = [src[2 * t + j, :, 192 * i : 192 * i + 192].astype(f32) for j in range(2)]
            y[:, 768 * i + 384 * t : 768 * i + 384 * t + 384] = jnp.concatenate(two, axis=1)
    for i, y in enumerate((y_g1, y_g2, y_g3)):
        line = o_small[12 + i : 13 + i, :]
        val = line[:, 0:192]
        for q in range(1, 4):
            val = jnp.where(d == q, line[:, 192 * q : 192 * q + 192], val)
        y[...] = val
    rel_t[...] = jnp.transpose(o_small[:, 0:128])
    y_rel[...] = rel_t[pl.ds(pl.multiple_of(8 * d, 8), 8), 0:12]


def per_device_kernel(
    inputs, memory, cotangent, segment_ids, row_live, buckets, gain_self, w_qkv, w_attn_out, rel_bias, gain_cross,
    c_query, c_keyval, c_out, gain_ff, w_gate_up, w_down,
):
    anywhere = pl.BlockSpec(memory_space=pl.ANY)
    vmem = pl.BlockSpec(memory_space=pltpu.VMEM)
    smem = pl.BlockSpec(memory_space=pltpu.SMEM)
    shapes = (
        ((2, 128, 768), bf16), ((2, 128, 768), bf16), ((2, 128, 768), bf16),
        ((2, 192, 2048), bf16), ((2, 256, 768), bf16), ((3, 2, 96, 768), bf16), ((4, 192, 576), bf16), ((4, 192, 384), bf16),
        ((16, 768), f32),
    )
    parts = pl.pallas_call(
        layer_kernel,
        out_shape=[jax.ShapeDtypeStruct(*sh) for sh in shapes],
        in_specs=[anywhere] * 3 + [vmem] * 6 + [smem] + [anywhere] * 7,
        out_specs=[anywhere] * 8 + [vmem],
        scratch_shapes=scratch(),
        compiler_params=pltpu.CompilerParams(collective_id=0, has_side_effects=True, vmem_limit_bytes=66500000),
        name="layer",
    )(
        inputs, memory, cotangent, segment_ids, gain_self, gain_cross, gain_ff, rel_bias,
        buckets.reshape(8, 128), row_live, w_qkv, c_keyval, w_attn_out, c_query, c_out, w_gate_up, w_down,
    )
    act = pl.BlockSpec((1, 64, 768), lambda i: (i // 2, i % 2, 0))
    whole = pl.BlockSpec((16, 768), lambda i: (0, 0))

    def rows(n, width):
        return pl.BlockSpec((n, width), lambda i: (i, 0)), jax.ShapeDtypeStruct((4 * n, width), f32)

    line = pl.BlockSpec((1, 192), lambda i: (0, 0)), jax.ShapeDtypeStruct((1, 192), f32)
    square = rows(48, 768)
    tokens = act, jax.ShapeDtypeStruct((2, 128, 768), bf16)
    down = (
        pl.BlockSpec((2, 64, 768), lambda i: (0, i, 0)),
        jax.ShapeDtypeStruct((2, 256, 768), f32),
    )
    table = pl.BlockSpec((8, 12), lambda i: (0, 0)), jax.ShapeDtypeStruct((8, 12), f32)
    outs = (
        tokens, tokens, tokens, line, rows(48, 2304), square, table, line, square, rows(48, 1536), square, line,
        rows(48, 4096), down,
    )
    res = pl.pallas_call(
        finish_kernel,
        grid=(4,),
        out_shape=[o for _, o in outs],
        in_specs=[
            act, act, act,
            pl.BlockSpec((2, 48, 2048), lambda i: (0, i, 0)),
            pl.BlockSpec((2, 64, 768), lambda i: (0, i, 0)),
            pl.BlockSpec((3, 1, 48, 768), lambda i: (0, i // 2, i % 2, 0)),
            pl.BlockSpec((4, 48, 576), lambda i: (0, i, 0)),
            pl.BlockSpec((4, 48, 384), lambda i: (0, i, 0)),
            whole,
        ],
        out_specs=[b for b, _ in outs],
        scratch_shapes=[pltpu.VMEM((128, 16), f32)],
        compiler_params=pltpu.CompilerParams(vmem_limit_bytes=66500000),
        name="finish",
    )(*parts)
    res = list(res)
    for i in (3, 7, 11):
        res[i] = res[i].reshape(192)
    res[13] = res[13].reshape(512, 768)
    return tuple(res)


def solution(mesh):
    in_specs = (
        P("dp", "seq", None),
        P("dp", "seq", None),
        P("dp", "seq", None),
        P("dp", "seq"),
        P("dp"),
        P(),
        P("dp"),
        P("dp", None),
        P("dp", None),
        P("dp", None),
        P("dp"),
        P("dp", None),
        P("dp", None),
        P("dp", None),
        P("dp"),
        P("dp", None),
        P("dp", None),
    )
    out_specs = (
        P("dp", "seq", None),
        P("dp", "seq", None),
        P("dp", "seq", None),
        P("dp"),
        P("dp", None),
        P("dp", None),
        P("dp", None),
        P("dp"),
        P("dp", None),
        P("dp", None),
        P("dp", None),
        P("dp"),
        P("dp", None),
        P("dp", None),
    )
    fits = dict(mesh.shape) == {"dp": 4, "seq": 8}
    return jax.shard_map(
        per_device_kernel if fits else per_device, mesh=mesh, in_specs=in_specs, out_specs=out_specs, check_vma=False
    )
```

```python
import jax
import jax.numpy as jnp
from jax import lax
from jax.experimental import pallas as pl
from jax.experimental.pallas import tpu as pltpu
from jax.sharding import PartitionSpec as P

D = 768
HEADS = 12
HEAD_DIM = 64
FF = 2048
BUCKETS = 32
LEN = 1024
MEM = 1024


epsilon = 1e-06
masked_score = -1000000000.0
highest = lax.Precision.HIGHEST


def rms_norm(values, gain):
    return values * lax.rsqrt(jnp.mean(values * values, axis=-1, keepdims=True) + epsilon) * gain


def matmul(left, right, form):
    return jnp.einsum(form, left, right, preferred_element_type=jnp.float32)


def softmax_parts(scores):
    top = jnp.max(scores, axis=-1, keepdims=True)
    expo = jnp.exp(scores - top)
    total = jnp.sum(expo, axis=-1, keepdims=True)
    return (expo / total, (top + jnp.log(total))[..., 0])


def score_grads(scores, lse_row, value_row, grad_row):
    probs = jnp.exp(scores - lse_row[..., None])
    grad_probs = matmul(grad_row, value_row, "qhd,khd->hqk")
    centre = jnp.sum(grad_probs * probs, axis=-1, keepdims=True)
    grad_scores = (probs * (grad_probs - centre)).astype(jnp.bfloat16)
    return (probs, grad_scores, centre[..., 0])


def one_hot_of(buckets):
    return (buckets[:, None] == jnp.arange(BUCKETS, dtype=jnp.int32)).astype(jnp.float32)


def skewed(by_dist, start, rows):
    table = jnp.concatenate([jnp.zeros((LEN - 1, HEADS), by_dist.dtype), by_dist], axis=0)
    window = lax.dynamic_slice_in_dim(table, start, rows + LEN - 1, axis=0)
    line = jnp.pad(window[::-1].T, ((0, 0), (0, 1)))
    width = rows + LEN
    flat = jnp.broadcast_to(line[:, None, :], (HEADS, rows, width)).reshape(HEADS, rows * width)
    return flat[:, : rows * (width - 1)].reshape(HEADS, rows, width - 1)[:, :, rows - 1 :]


def unskewed(block, start, rows):
    width = rows + LEN
    wide = jnp.pad(block, ((0, 0), (0, 0), (rows - 1, 0))).reshape(HEADS, rows * (width - 1))
    line = jnp.sum(jnp.pad(wide, ((0, 0), (0, rows))).reshape(HEADS, rows, width), axis=1)
    window = line[:, : width - 1][:, ::-1].T
    table = jnp.zeros((2 * LEN - 1, HEADS), block.dtype)
    return lax.dynamic_update_slice_in_dim(table, window, start, axis=0)[LEN - 1 :]


def per_device(
    inputs,
    memory,
    cotangent,
    segment_ids,
    row_live,
    buckets,
    gain_self,
    w_qkv,
    w_attn_out,
    rel_bias,
    gain_cross,
    c_query,
    c_keyval,
    c_out,
    gain_ff,
    w_gate_up,
    w_down,
):
    (
        g_self,
        qkv_full,
        out_full,
        bias_full,
        g_cross,
        cq_full,
        ckv_full,
        cout_full,
        g_ffn,
        gu_full,
        down_full,
    ) = (
        lax.all_gather(gain_self, "dp", axis=0, tiled=True),
        lax.all_gather(w_qkv, "dp", axis=0, tiled=True),
        lax.all_gather(w_attn_out, "dp", axis=0, tiled=True),
        lax.all_gather(rel_bias, "dp", axis=0, tiled=True),
        lax.all_gather(gain_cross, "dp", axis=0, tiled=True),
        lax.all_gather(c_query, "dp", axis=0, tiled=True),
        lax.all_gather(c_keyval, "dp", axis=0, tiled=True),
        lax.all_gather(c_out, "dp", axis=0, tiled=True),
        lax.all_gather(gain_ff, "dp", axis=0, tiled=True),
        lax.all_gather(w_gate_up, "dp", axis=0, tiled=True),
        lax.all_gather(w_down, "dp", axis=0, tiled=True),
    )
    num_rows, local_len, _ = inputs.shape
    seq_index = lax.axis_index("seq")
    scale = HEAD_DIM ** (-0.5)
    dense = inputs.astype(jnp.float32)
    live_rows = row_live.astype(jnp.float32)[:, None, None]
    normed_one = rms_norm(dense, g_self.astype(jnp.float32))
    hidden_one = normed_one.astype(jnp.bfloat16)
    qkv_local = matmul(hidden_one, qkv_full, "rcd,de->rce").astype(jnp.bfloat16)
    queries = qkv_local[..., :D]
    key_value = qkv_local[..., D:]
    seg_local = segment_ids.astype(jnp.bfloat16)
    key_all, seg_all = (
        lax.all_gather(key_value, "seq", axis=1, tiled=True),
        lax.all_gather(seg_local, "seq", axis=1, tiled=True),
    )
    positions = seq_index * local_len + jnp.arange(local_len, dtype=jnp.int32)
    offsets = positions[:, None] - jnp.arange(LEN, dtype=jnp.int32)[None, :]
    causal = offsets >= 0
    bucket_hot = one_hot_of(buckets)
    by_dist = jnp.einsum(
        "lb,bh->lh",
        bucket_hot,
        bias_full.astype(jnp.float32),
        precision=highest,
        preferred_element_type=jnp.float32,
    )
    bias_block = skewed(by_dist, seq_index * local_len, local_len)

    def self_scores(queries_h, key_row, seg_row, segk_row):
        raw = matmul(queries_h, key_row, "qhd,khd->hqk") * scale + bias_block
        allowed = causal & (seg_row[:, None] == segk_row[None, :])
        return jnp.where(allowed[None], raw, masked_score)

    def self_forward(items):
        query_row, kv_row, seg_row, segk_row = items
        key_row = kv_row[:, :D].reshape(LEN, HEADS, HEAD_DIM)
        value_row = kv_row[:, D:].reshape(LEN, HEADS, HEAD_DIM)
        scores = self_scores(
            query_row.reshape(local_len, HEADS, HEAD_DIM), key_row, seg_row, segk_row
        )
        probs, lse_row = softmax_parts(scores)
        mixed = matmul(probs.astype(jnp.bfloat16), value_row, "hqk,khd->qhd")
        return (mixed.reshape(local_len, D), lse_row)

    attn_self, lse_self = lax.map(self_forward, (queries, key_all, seg_local, seg_all))
    attn_low = attn_self.astype(jnp.bfloat16)
    branch_one = matmul(attn_low, out_full, "rcd,de->rce")
    after_self = dense + live_rows * branch_one
    normed_two = rms_norm(after_self, g_cross.astype(jnp.float32))
    hidden_two = normed_two.astype(jnp.bfloat16)
    cross_q = matmul(hidden_two, cq_full, "rcd,de->rce").astype(jnp.bfloat16)
    memory_kv = matmul(memory, ckv_full, "rmd,de->rme").astype(jnp.bfloat16)
    memory_all = lax.all_gather(memory_kv, "seq", axis=1, tiled=True)

    def cross_forward(items):
        query_row, kv_row = items
        key_row = kv_row[:, :D].reshape(MEM, HEADS, HEAD_DIM)
        value_row = kv_row[:, D:].reshape(MEM, HEADS, HEAD_DIM)
        scores = (
            matmul(query_row.reshape(local_len, HEADS, HEAD_DIM), key_row, "qhd,khd->hqk") * scale
        )
        probs, lse_row = softmax_parts(scores)
        mixed = matmul(probs.astype(jnp.bfloat16), value_row, "hqk,khd->qhd")
        return (mixed.reshape(local_len, D), lse_row)

    attn_cross, lse_cross = lax.map(cross_forward, (cross_q, memory_all))
    cross_low = attn_cross.astype(jnp.bfloat16)
    branch_two = matmul(cross_low, cout_full, "rcd,de->rce")
    after_cross = after_self + live_rows * branch_two
    normed_three = rms_norm(after_cross, g_ffn.astype(jnp.float32))
    hidden_three = normed_three.astype(jnp.bfloat16)
    gate_up = matmul(hidden_three, gu_full, "rcd,df->rcf")
    gate = gate_up[..., :FF]
    upward = gate_up[..., FF:]
    mixed_ff = (jax.nn.gelu(gate, approximate=True) * upward).astype(jnp.bfloat16)
    branch_three = matmul(mixed_ff, down_full, "rcf,fd->rcd")
    output = (after_cross + live_rows * branch_three).astype(jnp.bfloat16)
    (
        g_self,
        qkv_full,
        out_full,
        bias_full,
        g_cross,
        cq_full,
        ckv_full,
        cout_full,
        g_ffn,
        gu_full,
        down_full,
    ) = (
        lax.all_gather(gain_self, "dp", axis=0, tiled=True),
        lax.all_gather(w_qkv, "dp", axis=0, tiled=True),
        lax.all_gather(w_attn_out, "dp", axis=0, tiled=True),
        lax.all_gather(rel_bias, "dp", axis=0, tiled=True),
        lax.all_gather(gain_cross, "dp", axis=0, tiled=True),
        lax.all_gather(c_query, "dp", axis=0, tiled=True),
        lax.all_gather(c_keyval, "dp", axis=0, tiled=True),
        lax.all_gather(c_out, "dp", axis=0, tiled=True),
        lax.all_gather(gain_ff, "dp", axis=0, tiled=True),
        lax.all_gather(w_gate_up, "dp", axis=0, tiled=True),
        lax.all_gather(w_down, "dp", axis=0, tiled=True),
    )
    grad_out = cotangent.astype(jnp.float32)
    down_in = (live_rows * grad_out).astype(jnp.bfloat16)
    grad_down = matmul(mixed_ff, down_in, "rcf,rcd->fd")
    grad_mixed = matmul(down_in, down_full, "rcd,fd->rcf")
    _, gelu_pull = jax.vjp(
        lambda gate_in, up_in: jax.nn.gelu(gate_in, approximate=True) * up_in, gate, upward
    )
    grad_gate, grad_upward = gelu_pull(grad_mixed)
    grad_gu_low = jnp.concatenate([grad_gate, grad_upward], axis=-1).astype(jnp.bfloat16)
    grad_gate_up = matmul(hidden_three, grad_gu_low, "rcd,rcf->df")
    grad_normed_three = matmul(grad_gu_low, gu_full, "rcf,df->rcd")
    _, pull_three = jax.vjp(rms_norm, after_cross, g_ffn.astype(jnp.float32))
    part_three, grad_gain_ff = pull_three(grad_normed_three)
    grad_after_cross = grad_out + part_three
    cross_in = (live_rows * grad_after_cross).astype(jnp.bfloat16)
    grad_cout = matmul(cross_low, cross_in, "rcd,rce->de")
    grad_cross_attn = matmul(cross_in, cout_full, "rce,de->rcd").astype(jnp.bfloat16)

    def cross_backward(items):
        query_row, kv_row, lse_row, grad_row = items
        queries_h = query_row.reshape(local_len, HEADS, HEAD_DIM)
        grad_h = grad_row.reshape(local_len, HEADS, HEAD_DIM)
        key_row = kv_row[:, :D].reshape(MEM, HEADS, HEAD_DIM)
        value_row = kv_row[:, D:].reshape(MEM, HEADS, HEAD_DIM)
        scores = matmul(queries_h, key_row, "qhd,khd->hqk") * scale
        probs, grad_scores, centre = score_grads(scores, lse_row, value_row, grad_h)
        grad_query = matmul(grad_scores, key_row, "hqk,khd->qhd") * scale
        grad_key = matmul(grad_scores, queries_h, "hqk,qhd->khd") * scale
        grad_value = matmul(probs.astype(jnp.bfloat16), grad_h, "hqk,qhd->khd")
        kv_grads = jnp.concatenate([grad_key.reshape(MEM, D), grad_value.reshape(MEM, D)], axis=-1)
        return (grad_query.reshape(local_len, D), kv_grads, centre)

    grad_cq_rows, grad_memkv_full, _ = lax.map(
        cross_backward, (cross_q, memory_all, lse_cross, grad_cross_attn)
    )
    grad_memkv = lax.psum_scatter(
        grad_memkv_full.astype(jnp.bfloat16), "seq", scatter_dimension=1, tiled=True
    )
    grad_ckv = matmul(memory, grad_memkv, "rmd,rme->de")
    grad_memory = matmul(grad_memkv, ckv_full, "rme,de->rmd").astype(jnp.bfloat16)
    grad_cq_low = grad_cq_rows.astype(jnp.bfloat16)
    grad_cquery = matmul(hidden_two, grad_cq_low, "rcd,rce->de")
    grad_normed_two = matmul(grad_cq_low, cq_full, "rce,de->rcd")
    _, pull_two = jax.vjp(rms_norm, after_self, g_cross.astype(jnp.float32))
    part_two, grad_gain_cross = pull_two(grad_normed_two)
    grad_after_self = grad_after_cross + part_two
    self_in = (live_rows * grad_after_self).astype(jnp.bfloat16)
    grad_wout = matmul(attn_low, self_in, "rcd,rce->de")
    grad_self_attn = matmul(self_in, out_full, "rce,de->rcd").astype(jnp.bfloat16)

    def self_backward(carry, items):
        query_row, kv_row, seg_row, segk_row, lse_row, grad_row = items
        queries_h = query_row.reshape(local_len, HEADS, HEAD_DIM)
        grad_h = grad_row.reshape(local_len, HEADS, HEAD_DIM)
        key_row = kv_row[:, :D].reshape(LEN, HEADS, HEAD_DIM)
        value_row = kv_row[:, D:].reshape(LEN, HEADS, HEAD_DIM)
        scores = self_scores(queries_h, key_row, seg_row, segk_row)
        probs, grad_scores, centre = score_grads(scores, lse_row, value_row, grad_h)
        grad_query = matmul(grad_scores, key_row, "hqk,khd->qhd") * scale
        grad_key = matmul(grad_scores, queries_h, "hqk,qhd->khd") * scale
        grad_value = matmul(probs.astype(jnp.bfloat16), grad_h, "hqk,qhd->khd")
        kv_grads = jnp.concatenate([grad_key.reshape(LEN, D), grad_value.reshape(LEN, D)], axis=-1)
        return (
            carry + grad_scores.astype(jnp.float32),
            (grad_query.reshape(local_len, D), kv_grads, centre),
        )

    zero_block = jnp.zeros((HEADS, local_len, LEN), jnp.float32)
    score_total, (grad_q_rows, grad_kv_full, _) = lax.scan(
        self_backward, zero_block, (queries, key_all, seg_local, seg_all, lse_self, grad_self_attn)
    )
    grad_kv = lax.psum_scatter(
        grad_kv_full.astype(jnp.bfloat16), "seq", scatter_dimension=1, tiled=True
    )
    grad_bias = jnp.einsum(
        "lh,lb->bh",
        unskewed(score_total, seq_index * local_len, local_len),
        bucket_hot,
        precision=highest,
        preferred_element_type=jnp.float32,
    )
    grad_qkv_low = jnp.concatenate([grad_q_rows.astype(jnp.bfloat16), grad_kv], axis=-1)
    grad_wqkv = matmul(hidden_one, grad_qkv_low, "rcd,rce->de")
    grad_normed_one = matmul(grad_qkv_low, qkv_full, "rce,de->rcd")
    _, pull_one = jax.vjp(rms_norm, dense, g_self.astype(jnp.float32))
    part_one, grad_gain_self = pull_one(grad_normed_one)
    grad_inputs = (grad_after_self + part_one).astype(jnp.bfloat16)
    (
        own_gself,
        own_qkv,
        own_wout,
        own_bias,
        own_gcross,
        own_cquery,
        own_ckv,
        own_cout,
        own_gff,
        own_gateup,
        own_down,
    ) = (
        lax.psum_scatter(
            grad_gain_self.astype(jnp.bfloat16), "dp", scatter_dimension=0, tiled=True
        ).astype(jnp.float32),
        lax.psum_scatter(
            grad_wqkv.astype(jnp.bfloat16), "dp", scatter_dimension=0, tiled=True
        ).astype(jnp.float32),
        lax.psum_scatter(
            grad_wout.astype(jnp.bfloat16), "dp", scatter_dimension=0, tiled=True
        ).astype(jnp.float32),
        lax.psum_scatter(
            grad_bias.astype(jnp.bfloat16), "dp", scatter_dimension=0, tiled=True
        ).astype(jnp.float32),
        lax.psum_scatter(
            grad_gain_cross.astype(jnp.bfloat16), "dp", scatter_dimension=0, tiled=True
        ).astype(jnp.float32),
        lax.psum_scatter(
            grad_cquery.astype(jnp.bfloat16), "dp", scatter_dimension=0, tiled=True
        ).astype(jnp.float32),
        lax.psum_scatter(
            grad_ckv.astype(jnp.bfloat16), "dp", scatter_dimension=0, tiled=True
        ).astype(jnp.float32),
        lax.psum_scatter(
            grad_cout.astype(jnp.bfloat16), "dp", scatter_dimension=0, tiled=True
        ).astype(jnp.float32),
        lax.psum_scatter(
            grad_gain_ff.astype(jnp.bfloat16), "dp", scatter_dimension=0, tiled=True
        ).astype(jnp.float32),
        lax.psum_scatter(
            grad_gate_up.astype(jnp.bfloat16), "dp", scatter_dimension=0, tiled=True
        ).astype(jnp.float32),
        lax.psum_scatter(
            grad_down.astype(jnp.bfloat16), "dp", scatter_dimension=0, tiled=True
        ).astype(jnp.float32),
    )
    summed = (
        lax.psum(own_gself.astype(jnp.bfloat16), "seq").astype(jnp.float32),
        lax.psum(own_qkv.astype(jnp.bfloat16), "seq").astype(jnp.float32),
        lax.psum(own_wout.astype(jnp.bfloat16), "seq").astype(jnp.float32),
        lax.psum(own_bias.astype(jnp.bfloat16), "seq").astype(jnp.float32),
        lax.psum(own_gcross.astype(jnp.bfloat16), "seq").astype(jnp.float32),
        lax.psum(own_cquery.astype(jnp.bfloat16), "seq").astype(jnp.float32),
        lax.psum(own_ckv.astype(jnp.bfloat16), "seq").astype(jnp.float32),
        lax.psum(own_cout.astype(jnp.bfloat16), "seq").astype(jnp.float32),
        lax.psum(own_gff.astype(jnp.bfloat16), "seq").astype(jnp.float32),
        lax.psum(own_gateup.astype(jnp.bfloat16), "seq").astype(jnp.float32),
        lax.psum(own_down.astype(jnp.bfloat16), "seq").astype(jnp.float32),
    )
    return (
        output,
        grad_inputs,
        grad_memory,
        summed[0],
        summed[1],
        summed[2],
        summed[3],
        summed[4],
        summed[5],
        summed[6],
        summed[7],
        summed[8],
        summed[9],
        summed[10],
    )


f32, bf16 = jnp.float32, jnp.bfloat16
BIG = 1.0e9
SCALE = HEAD_DIM ** (-0.5)
MESH = pl.DeviceIdType.MESH
GELU_A, GELU_B = 0.7978845608028654, 0.044715
N_SEM, N_LOCAL = 232, 32


def flip(v, k, bits):
    for i in range(bits):
        if (k >> i) & 1:
            b = 1 << i
            v = v + b - 2 * b * lax.rem(lax.div(v, b), 2)
    return v


def dot(a, b):
    return lax.dot_general(a, b, (((1,), (0,)), ((), ())), preferred_element_type=f32)


def dot_nt(a, b):
    return lax.dot_general(a, b, (((1,), (1,)), ((), ())), preferred_element_type=f32)


def dot_tn(a, b):
    return lax.dot_general(a, b, (((0,), (0,)), ((), ())), preferred_element_type=f32)


def inv_rms(v):
    return lax.rsqrt(jnp.mean(v * v, axis=-1, keepdims=True) + epsilon)


def norm_back(v, gain, w):
    r = inv_rms(v)
    gw = gain * w
    mean = jnp.mean(gw * v, axis=-1, keepdims=True)
    return r * gw - v * (r * r * r * mean), jnp.sum(w * (v * r), axis=0, keepdims=True)


def gelu_parts(gate):
    sq = gate * gate
    th = jnp.tanh(GELU_A * gate * (1.0 + GELU_B * sq))
    half = 0.5 * (1.0 + th)
    slope = half + 0.5 * gate * (1.0 - th * th) * (GELU_A * (1.0 + 3.0 * GELU_B * sq))
    return gate * half, slope


def softmax(scores):
    e = jnp.exp(scores - jnp.max(scores, axis=-1, keepdims=True))
    return (e * (1.0 / jnp.sum(e, axis=-1, keepdims=True))).astype(bf16)


def pad64(v):
    return jnp.concatenate([v, jnp.zeros((v.shape[0], 64), v.dtype)], axis=1)


def above64(v):
    return jnp.concatenate([jnp.zeros((v.shape[0], 64), v.dtype), v], axis=1)


def pack(ref, slot, parts):
    ref[slot, 0:256, :] = jnp.concatenate([parts[0], parts[1]], axis=1)
    ref[slot, 256:384, :] = jnp.concatenate([parts[2][0:128], parts[2][128:256]], axis=1)


def unpack(ref, slot):
    two = ref[slot, 0:256, :]
    last = ref[slot, 256:384, :]
    return (two[:, :64], two[:, 64:], jnp.concatenate([last[:, :64], last[:, 64:]], axis=0))


def assemble(ref, dst):
    for t in range(2):
        a = unpack(ref, 2 * t) + unpack(ref, 2 * t + 1)
        for j in range(3):
            at = 384 * t + 128 * j
            dst[:, at : at + 128] = jnp.concatenate([a[2 * j], a[2 * j + 1]], axis=1)


def disperse(val, ref):
    for gg in range(4):
        pack(ref, gg, [val[:, 192 * gg + 64 * h : 192 * gg + 64 * h + 64] for h in range(3)])


def block(i):
    return pl.ds(pl.multiple_of(i * 256, 256), 256)


def layer_kernel(
    x, mem, cot, segs, gain1, gain2, gain3, rel, buck, live, w_in, w_kv, w_ao, w_cq, w_co, w_gu, w_dn,
    out, gin, gmem, o_gu, o_dn, o_b, o_q, o_m, o_small,
    *,
    xrow, mrow, h1, wQ, wM, W3, wgu, wd, sm, sg, gains, lines, hot, tbias, qh, kh, vh, mkv, p_self, p_cross,
    opack, arecv, attn, qpack, qrecv, crecv, cattn, after_self, after_cross, h2, h3, prod, dgu, cotb, frecv,
    hrecv, outb, grad, low, dcq, acc, dqkv, rs1, rs2, rt1, rt2, gur, dnr, bsib, bdp, qdp, mdp, zg1, zg2, zd1, zd2,
    zb1, zb2, qfar, mfar, gsm, sm1, sm2, sgown, ssem, rsem, lsem,
):
    drecv, dqrecv, srecv = arecv, crecv, qrecv
    fown, fpart, xown = tbias.at[2], outb, after_cross
    keep, hpart = p_cross.at[0], low.at[1]

    d, s = lax.axis_index("dp"), lax.axis_index("seq")
    c, z, g, r = lax.rem(s, 2), lax.div(s, 2), lax.rem(s, 4), lax.div(s, 4)
    used = {"remote": 0, "local": 0}
    flying = []

    def remote(src, dst, send_sem, recv_sem, dev):
        return pltpu.make_async_remote_copy(
            src_ref=src, dst_ref=dst, send_sem=ssem.at[send_sem], recv_sem=rsem.at[recv_sem],
            device_id=dev, device_id_type=MESH,
        )

    def fresh(n=1):
        used["remote"] += n
        assert used["remote"] <= N_SEM
        return used["remote"] - n

    def push(src, dst, dev):
        sem = fresh()
        copy = remote(src, dst, sem, sem, dev)
        copy.start()
        flying.append(copy)
        return copy

    def sent(copies):
        for copy in copies:
            copy.wait_send()
            flying[:] = [other for other in flying if other is not copy]

    def arrived(copies):
        for copy in copies:
            copy.wait_recv()

    def local(src, dst):
        copy = pltpu.make_async_copy(src, dst, lsem.at[used["local"]])
        used["local"] += 1
        copy.start()
        return copy

    def dpk(k):
        return (flip(d, k, 2), s)

    def seqk(k):
        return (d, flip(s, k, 3))

    class Gather:
        def __init__(self, whole, part):
            self.part = part
            own = whole(d)
            self.first = {k: push(own, own, dpk(k)) for k in (1, 2)}
            self.second = []

        def relay(self):
            for k, half in ((1, 0), (2, 1)):
                arrived([self.first[k]])
                src = self.part(flip(d, k, 2), half)
                self.second.append(push(src, src, dpk(3 - k)))

        def done(self):
            arrived(self.second)

        def gone(self):
            sent([*self.first.values(), *self.second])

    class Reduce:
        def __init__(self, part, got):
            self.part, self.got = part, got
            self.first = {}
            for k, half in ((1, 0), (2, 1)):
                for j, kk in ((0, k), (1, 3)):
                    copy = push(part(flip(d, kk, 2), half), got.at[3 * half + j], dpk(k))
                    self.first[half, j] = copy

        def middle(self):
            self.second = {}
            for k, half in ((1, 0), (2, 1)):
                arrived([self.first[half, 1]])
                ref = self.part(flip(d, 3 - k, 2), half)
                ref[...] = (ref[...].astype(f32) + self.got[3 * half + 1].astype(f32)).astype(bf16)
                self.second[half] = push(ref, self.got.at[3 * half + 2], dpk(3 - k))

        def end(self):
            for half in (0, 1):
                arrived([self.first[half, 0], self.second[half]])
                ref = self.part(d, half)
                total = ref[...].astype(f32) + self.got[3 * half].astype(f32) + self.got[3 * half + 2].astype(f32)
                ref[...] = total.astype(bf16)

    def moved(srcs, dsts, devs, slot):
        base = fresh(2)
        for i in range(2):
            away = remote(srcs[i], dsts[i], base + i, base + slot, (d, devs[i]))
            here = pltpu.make_async_copy(srcs[i], dsts[i], rsem.at[base + slot])

            @pl.when(devs[i] != s)
            def _():
                away.start()

            @pl.when(devs[i] == s)
            def _():
                here.start()

        def wait_recv(places):
            for i in range(2):
                pltpu.make_async_copy(places[i], places[i], rsem.at[base + i]).wait()

        def wait_send():
            for i in range(2):
                away = remote(srcs[i], dsts[i], base + i, base + slot, (d, devs[i]))

                @pl.when(devs[i] != s)
                def _():
                    away.wait_send()

        return wait_recv, wait_send

    mine, mine_d = pl.ds(pl.multiple_of(d * 192, 64), 192), block(d)
    here = pl.ds(s * 128, 128)
    own_x = local(x.at[r], xrow.at[here])
    stage = [p_self.at[0, i, 0:192] for i in range(4)] + [p_self.at[1, 0, 0:192]]
    own_in = [
        local(w.at[:, 768 * i : 768 * i + 768], stage[p])
        for p, (w, i) in enumerate(((w_in, 0), (w_in, 1), (w_in, 2), (w_kv, 0), (w_kv, 1)))
    ]
    own_W3 = [local(w, W3.at[i, mine]) for i, w in enumerate((w_ao, w_cq, w_co))]
    own_m = local(mem.at[r], mrow.at[here])
    own_gu = []
    for p in range(8):
        at = pl.multiple_of((p // 4) * FF + (p % 4) * 512 + c * 256, 256)
        own_gu.append(local(w_gu.at[:, pl.ds(at, 256)], wgu.at[mine, pl.ds(512 * (p % 4) + 256 * (p // 4), 256)]))
    own_dn = local(w_dn.at[block(c)], wd.at[mine_d])

    barrier = pltpu.get_barrier_semaphore()
    peers = [dpk(k) for k in (1, 2, 3)] + [seqk(k) for k in range(1, 8)]
    for p in peers:
        pl.semaphore_signal(barrier, inc=1, device_id=p, device_id_type=MESH)
    for i in range(2):
        sgown[i] = jnp.broadcast_to(segs[i : i + 1, :].astype(f32), (16, 128)).astype(bf16)
    sg[s] = sgown[r]
    at_bucket = lax.broadcasted_iota(jnp.int32, (8, 128), 1) == lax.broadcasted_iota(jnp.int32, (8, 128), 0) + 8 * d
    gains[...] = jnp.zeros((16, 768), f32)
    gains[0:12, 0:128] = dot_tn(rel[...].astype(f32), at_bucket.astype(f32))
    for q in range(4):

        @pl.when(d == q)
        def _():
            for i, gain in enumerate((gain1, gain2, gain3)):
                gains[12 + i : 13 + i, 192 * q : 192 * q + 192] = gain[...].astype(f32).reshape(1, 192)

    sm[d] = gains[...].astype(bf16)
    pl.semaphore_wait(barrier, len(peers))

    def row_of(k):
        return lax.div(flip(s, k, 3), 4)

    def spread(src, dst):
        return {m: push(src.at[row_of(2 * m)], dst.at[here], seqk(2 * m)) for m in (1, 2, 3)}

    def hand_on(dst, m):
        part = dst.at[pl.ds(flip(s, 2 * m, 3) * 128, 128)]
        return push(part, part, seqk(1))

    sm_in = [push(sm.at[d], sm.at[d], dpk(k)) for k in (1, 2, 3)]
    sg_in = [push(sgown.at[row_of(k)], sg.at[s], seqk(k)) for k in range(1, 8)]
    xd = spread(x, xrow)
    own_x.wait()
    xs = {0: hand_on(xrow, 0)}
    for cp in own_in:
        cp.wait()
    for q in range(4):

        @pl.when(g == q)
        def _():
            for p in range(5):
                dst, at = (wQ, 192 * p) if p < 3 else (wM, 192 * (p - 3))
                dst[mine, at : at + 192] = stage[p][:, 192 * q : 192 * q + 192]

    def part192(ref):
        return lambda dd, half: ref.at[pl.ds(pl.multiple_of(dd * 192 + 96 * half, 32), 96)]

    def whole192(ref):
        return lambda dd: ref.at[pl.ds(pl.multiple_of(dd * 192, 64), 192)]

    def part_dn(dd, half):
        return wd.at[pl.ds(pl.multiple_of(dd * 256 + 128 * half, 128), 128)]

    def part_b(i):
        return lambda dd, half: W3.at[i, pl.ds(pl.multiple_of(dd * 192 + c * 96 + 48 * half, 16), 48)]

    q_w = Gather(whole192(wQ), part192(wQ))

    def half_rows(dd, cc):
        return pl.ds(pl.multiple_of(dd * 192 + cc * 96, 32), 96)

    def send_W3(i):
        own_W3[i].wait()
        return Gather(lambda dd: W3.at[i, half_rows(dd, c)], part_b(i))

    def share_W3(i):
        W3_w[i].done()
        return [push(W3.at[i, rows], W3.at[i, rows], seqk(1)) for rows in (half_rows(flip(d, k, 2), c) for k in (1, 2, 3))]

    m_w = Gather(whole192(wM), part192(wM))
    W3_w = {0: send_W3(0)}
    W3_sib = {}

    arrived(sm_in)
    total = sm[0].astype(f32)
    for i in range(1, 4):
        total += sm[i].astype(f32)
    gains[...] = total
    near = jnp.concatenate([buck[i : i + 1, :] for i in range(4)], axis=1)
    by_dist = (lax.broadcasted_iota(jnp.int32, (128, 512), 0) == near).astype(bf16)
    turn = lax.broadcasted_iota(jnp.int32, (512, 1024), 0) + lax.broadcasted_iota(jnp.int32, (512, 1024), 1) == 768
    hot[...] = dot(by_dist, turn.astype(bf16)).astype(bf16)
    column = lax.broadcasted_iota(jnp.int32, (16, 1024), 1)
    line = dot(total[:, :128].astype(bf16), hot[...])
    lines[...] = jnp.where((column > 256) & (column < 769), line, masked_score)
    for h in range(3):
        row = jnp.broadcast_to(lines[pl.ds(3 * g + h, 1), :], (256, 1024))
        tbias[h] = pltpu.roll(row, 0, 1, stride=1, stride_axis=0)[:, 256:]

    def norm_block(m):
        rows = block(flip(z, m, 2))
        val = xrow[rows, :].astype(f32)
        h1[rows, :] = (val * inv_rms(val) * gains[12:13, :]).astype(bf16)

    arrived([xs[0]])
    norm_block(0)
    for m in (1, 2):
        arrived([xd[m]])
        xs[m] = hand_on(xrow, m)
    q_w.relay()
    arrived([xs[1]])
    norm_block(1)
    m_w.relay()
    W3_w[1] = send_W3(1)
    arrived([xd[3]])
    xs[3] = hand_on(xrow, 3)
    md = spread(mem, mrow)
    own_m.wait()
    ms = {0: hand_on(mrow, 0)}
    W3_w[0].relay()
    W3_w[2] = send_W3(2)
    arrived([xs[2]])
    norm_block(2)
    arrived([xs[3]])
    norm_block(3)

    arrived(sg_in)
    lane64 = lax.broadcasted_iota(jnp.int32, (128, 64), 1).astype(f32)
    inside = lane64 < 3.5
    for h in range(3):
        beyond = lax.broadcasted_iota(jnp.int32, (512, 128), 1) >= 64
        kh[h, 0:512, :] = jnp.where(beyond, -1.0, 0.0).astype(bf16)
        vh[h, 0:512, :] = jnp.zeros((512, 128), bf16)
    q_w.done()

    def project(i, carry):
        rows = block(i)
        res = dot(h1[rows, :], wQ[...]).astype(bf16)
        qa, ka = [], []
        for j in range(2):
            seg = sg[2 * i + j, 0:1, :].astype(f32)
            same = jnp.transpose(jnp.broadcast_to(seg, (128, 128)))[:, :64] == lane64
            qa.append(jnp.where(same, BIG, 0.0))
            ka.append(jnp.where(inside & jnp.logical_not(same), -1.0, 0.0))
        qa = jnp.concatenate(qa, axis=0).astype(bf16)
        ka = jnp.concatenate(ka, axis=0).astype(bf16)
        lower = pl.ds(pl.multiple_of(i * 256 + 512, 256), 256)
        for h in range(3):
            qv = (res[:, 64 * h : 64 * h + 64].astype(f32) * SCALE).astype(bf16)
            qh[h, rows, :] = jnp.concatenate([qv, qa], axis=1)
            kh[h, lower, :] = jnp.concatenate([res[:, 192 + 64 * h : 256 + 64 * h], ka], axis=1)
            vh[h, lower, :] = pad64(res[:, 384 + 64 * h : 448 + 64 * h])
        return carry

    lax.fori_loop(0, 4, project, 0)

    for cp in own_gu:
        cp.wait()
    gu_w = Gather(whole192(wgu), part192(wgu))

    def window(b):
        return pl.ds(pl.multiple_of(b * 256, 256), 768)

    a_in = []
    for k in (2, 3, 1, 0):
        b = flip(g, k, 2)
        parts = []
        for h in range(3):
            p = softmax(dot_nt(qh[h, block(b), :], kh[h, window(b), :]) + tbias[h])
            p_self[h, b] = p
            parts.append(dot(p, vh[h, window(b), :])[:, :64].astype(bf16))
        if k == 0:
            pack(arecv, g, parts)
        else:
            pack(opack, b, parts)
            a_in.append(push(opack.at[b], arecv.at[g], seqk(k)))
        if k == 2:
            W3_w[1].relay()
        if k == 1:
            W3_w[2].relay()

    own_dn.wait()
    dn_w = Gather(lambda dd: wd.at[block(dd)], part_dn)
    for m in (1, 2, 3):
        arrived([md[m]])
        ms[m] = hand_on(mrow, m)
    halves = [cotb.at[c, pl.ds(c * 128, 128)]] * 2
    dests = [4 * rr + z for rr in range(2)]
    cslot = lax.rem(z, 2)
    cot_recv, cot_sent = moved(
        [cot.at[0], cot.at[1]], [cotb.at[cslot, pl.ds(c * 128, 128)]] * 2, dests, c
    )
    W3_sib[0] = share_W3(0)
    m_w.done()
    arrived(ms.values())

    def project_memory(i, carry):
        rows = block(i)
        res = dot(mrow[rows, :], wM[...]).astype(bf16)
        for h in range(3):
            mkv[h, rows, :] = jnp.concatenate(
                [res[:, 64 * h : 64 * h + 64], res[:, 192 + 64 * h : 256 + 64 * h]], axis=1
            )
        return carry

    lax.fori_loop(0, 4, project_memory, 0)
    W3_sib[1] = share_W3(1)

    arrived(a_in)
    assemble(arecv, attn)
    arrived(W3_sib[0])
    alive = live[r].astype(f32)
    res = xrow[block(g), :].astype(f32) + alive * dot(attn[...], W3[0])
    after_self[...] = res
    h2[...] = (res * inv_rms(res) * gains[13:14, :]).astype(bf16)
    arrived(W3_sib[1])
    disperse((dot(h2[...], W3[1]).astype(bf16).astype(f32) * SCALE).astype(bf16), qpack)
    q_in = {k: push(qpack.at[flip(g, k, 2)], qrecv.at[g], seqk(k)) for k in (2, 3, 1)}
    qrecv[g] = qpack[g]
    gu_w.relay()
    cot_recv([cotb.at[c, pl.ds(0, 128)], cotb.at[c, pl.ds(128, 128)]])
    cot_sib = push(cotb.at[c], cotb.at[c], seqk(1))

    sent(a_in)
    c_in = []
    for k in (0, 1, 2, 3):
        b = flip(g, k, 2)
        if k:
            arrived([q_in[k]])
        qs = unpack(qrecv, b)
        parts = []
        for h in range(3):
            p = softmax(dot_nt(pad64(qs[h]), mkv[h]))
            p_cross[h, b] = p
            parts.append(dot(p, mkv[h])[:, 64:].astype(bf16))
        if k == 0:
            pack(crecv, g, parts)
        else:
            pack(opack, b, parts)
            c_in.append(push(opack.at[b], crecv.at[g], seqk(k)))
        if k == 0:
            W3_sib[2] = share_W3(2)
        if k == 1:
            dn_w.relay()
    arrived(W3_sib[2])
    arrived(c_in)
    assemble(crecv, cattn)
    res = after_self[...] + alive * dot(cattn[...], W3[2])
    after_cross[...] = res
    h3[c] = (res * inv_rms(res) * gains[14:15, :]).astype(bf16)
    h3_in = push(h3.at[c], h3.at[c], seqk(1))
    arrived([cot_sib])
    gu_w.done()
    dn_w.done()
    arrived([h3_in])

    gu_w.gone()
    dn_w.gone()
    tbias[0:2] = jnp.zeros((2, 256, 768), f32)

    def feed_forward(n, carry):
        cols = block(n)
        both = pl.ds(pl.multiple_of(n * 512, 512), 512)
        gates, ups = pl.ds(pl.multiple_of(n * 512, 512), 256), pl.ds(pl.multiple_of(n * 512 + 256, 256), 256)
        for t in range(2):
            gate, up = dot(h3[t], wgu[:, gates]), dot(h3[t], wgu[:, ups])
            act, slope = gelu_parts(gate)
            prod[t, :, cols] = (act * up).astype(bf16)
            gp = dot_nt((cotb[t].astype(f32) * alive).astype(bf16), wd[cols, :])
            dgu[t, :, gates] = (gp * up * slope).astype(bf16)
            dgu[t, :, ups] = (gp * act).astype(bf16)
            tbias[t] += dot_nt(dgu[t, :, both], wgu[:, both])
        for part in (gates, ups):
            wgu[:, part] = dot_tn(h3[...].reshape(512, 768), dgu[:, :, part].reshape(512, 256)).astype(bf16)
        return carry

    def grad_dn(n, carry):
        cols = block(n)
        down_in = (cotb[...].astype(f32) * alive).astype(bf16).reshape(512, 768)
        wd[cols, :] = dot_tn(prod[:, :, cols].reshape(512, 256), down_in).astype(bf16)
        return carry

    def part_gu(i):
        cols = pl.ds(1024 * i, 1024)
        return lambda dd, half: wgu.at[pl.ds(pl.multiple_of(dd * 192 + 96 * half, 32), 96), cols]

    far_side = lax.div(z, 2)
    outer = lax.rem(z, 2) == far_side
    inner = jnp.logical_not(outer)

    def push_if(src, dst, dev, sends, gets):
        copy = remote(src, dst, fresh(1), used["remote"] - 1, dev)

        class Copy:
            def wait_send(self):
                pl.when(sends)(copy.wait_send)

            def wait_recv(self):
                pl.when(gets)(copy.wait_recv)

        pl.when(sends)(copy.start)
        res = Copy()
        flying.append(res)
        return res

    class Around:
        def __init__(self, own, out, half, got):
            self.own, self.out, self.half, self.got = own, out, half, got

        def add(self, ref, got):
            @pl.when(inner)
            def _():
                ref[...] = (ref[...].astype(f32) + got[...].astype(f32)).astype(bf16)

        def step1(self):
            self.copy = push_if(self.own, self.got[0], seqk(2), outer, inner)

        def step2(self):
            arrived([self.copy])
            self.add(self.own, self.got[0])
            self.copy = push_if(self.half(self.own, 1 - far_side), self.got[1], seqk(6), inner, inner)

        def step3(self):
            arrived([self.copy])
            src, dst = self.half(self.own, far_side), self.half(self.out, far_side)
            self.add(src, self.got[1])
            self.copy = push_if(src, dst, seqk(6), inner, inner)
            self.back = [push_if(src, dst, seqk(2), inner, outer)]
            self.keep = pltpu.make_async_copy(src, dst, lsem.at[used["local"]])
            used["local"] += 1
            pl.when(inner)(self.keep.start)

        def step4(self):
            arrived([self.copy])
            pl.when(inner)(self.keep.wait)
            place = self.half(self.out, 1 - far_side)
            self.back.append(push_if(place, place, seqk(2), inner, outer))

        def step5(self):
            arrived(self.back)
            self.copy = push(self.out, self.out, seqk(1))

    def halves(n):
        return lambda ref, i: ref.at[pl.ds(pl.multiple_of(n * i, 16), n)]

    cols_gu = [pl.ds(1024 * i, 1024) for i in range(2)]
    g_z, u_z = [
        Around(wgu.at[mine, cols_gu[i]], o_gu.at[c, :, cols_gu[i]], halves(96), (zg1.at[i], zg2.at[i])) for i in range(2)
    ]
    n_z = Around(wd.at[mine_d], o_dn.at[c], halves(128), (zd1, zd2))
    b_z = [Around(W3.at[i, half_rows(d, c)], o_b.at[i, c], halves(48), (zb1.at[i], zb2.at[i])) for i in range(3)]

    lax.fori_loop(0, 2, feed_forward, 0)
    g_rs = Reduce(part_gu(0), gur.at[0])
    lax.fori_loop(2, 4, feed_forward, 0)
    u_rs = Reduce(part_gu(1), gur.at[1])
    hpart[...] = tbias[1 - c].astype(bf16)
    h_in = push(hpart, hrecv, seqk(1))
    fpart[...] = dot(prod[1 - c], wd[...]).astype(bf16)
    f_in = push(fpart, frecv, seqk(1))
    arrived([h_in])
    dv, dgain3 = norm_back(after_cross[...], gains[14:15, :], tbias[c] + hrecv[...].astype(f32))
    gsm[...] = jnp.zeros((32, 128), f32)

    def put_gain(i, val):
        for j in range(6):
            gsm[12 + 6 * i + j : 13 + 6 * i + j, :] = val[:, 128 * j : 128 * j + 128]

    put_gain(2, dgain3)
    grad[...] = cotb[c].astype(f32) + dv
    low[0] = (grad[...] * alive).astype(bf16)
    sent(c_in)
    sent(q_in.values())
    disperse(dot_nt(low[0], W3[2]).astype(bf16), opack)
    d_in = {k: push(opack.at[flip(g, k, 2)], drecv.at[g], seqk(k)) for k in (2, 3, 1)}
    drecv[g] = opack[g]
    g_rs.middle()
    fown[...] = dot(prod[c], wd[...])
    lax.fori_loop(0, 4, grad_dn, 0)

    arrived([f_in])
    sent([f_in])
    outb[...] = (after_cross[...] + alive * (fown[...] + frecv[...].astype(f32))).astype(bf16)
    back = [2 * g + j for j in range(2)]
    out_recv, out_sent = moved([outb.at[pl.ds(0, 128)], outb.at[pl.ds(128, 128)]], [out.at[r]] * 2, back, r)

    lefts = (attn, h2, cattn)
    rights = (low.at[1], dcq, low.at[0])
    b_sib = {}

    def grad_square(i):
        W3_w[i].gone()
        sent(W3_sib[i])
        W3[i] = dot_tn(lefts[i][...], rights[i][...]).astype(bf16)
        b_sib[i] = [push(W3.at[i, half_rows(q, 1 - c)], bsib.at[i, q], seqk(1)) for q in range(4)]

    def chip_square(i):
        arrived(b_sib[i])
        for q in range(4):
            rows = half_rows(q, c)
            W3[i, rows, :] = (W3[i, rows, :].astype(f32) + bsib[i, q].astype(f32)).astype(bf16)
        return Reduce(part_b(i), bdp.at[i])

    grad_square(2)

    for h in range(3):
        acc[h, 0:1024, :] = jnp.zeros((1024, 128), f32)
    dq_in = []

    def cross_back(k):
        b = flip(g, k, 2)
        if k:
            arrived([d_in[k]])
        dos, qs = unpack(drecv, b), unpack(qrecv, b)
        parts = []
        for h in range(3):
            p = p_cross[h, b]
            do = above64(dos[h])
            dp = dot_nt(do, mkv[h])
            pf = p.astype(f32)
            ds = (pf * (dp - jnp.sum(dp * pf, axis=-1, keepdims=True))).astype(bf16)
            parts.append((dot(ds, mkv[h])[:, :64] * SCALE).astype(bf16))
            acc[h, 0:1024, :] += dot_tn(ds, pad64(qs[h])) + dot_tn(p, do)
        if k == 0:
            pack(dqrecv, g, parts)
        else:
            pack(qpack, b, parts)
            dq_in.append(push(qpack.at[b], dqrecv.at[g], seqk(k)))

    cross_back(2)
    n_rs = Reduce(part_dn, dnr)
    cross_back(3)
    u_rs.middle()
    cross_back(1)
    g_rs.end()
    g_z.step1()
    cross_back(0)
    b_rs = {2: chip_square(2)}

    def keep_memory(i, carry):
        rows = block(i)
        vals = [acc[h, rows, :][:, :64] for h in range(3)] + [acc[h, rows, :][:, 64:] for h in range(3)]
        dqkv[rows, 0:384] = jnp.concatenate(vals, axis=1).astype(bf16)
        return carry

    lax.fori_loop(0, 4, keep_memory, 0)
    arrived(dq_in)
    assemble(dqrecv, dcq)
    dv, dgain2 = norm_back(after_self[...], gains[13:14, :], dot_nt(dcq[...], W3[1]))
    put_gain(1, dgain2)
    grad[...] += dv
    sent([h_in])
    low[1] = (grad[...] * alive).astype(bf16)
    sent(d_in.values())
    disperse(dot_nt(low[1], W3[0]).astype(bf16), opack)
    s_in = {k: push(opack.at[flip(g, k, 2)], srecv.at[g], seqk(k)) for k in (2, 3, 1)}
    srecv[g] = opack[g]

    u_rs.end()
    u_z.step1()
    n_rs.middle()
    grad_square(1)
    grad_square(0)

    class Rows:
        def __init__(self, compute, first, second):
            self.compute, self.first, self.second = compute, first, second
            self.in3 = push(compute(flip(g, 3, 2)), first.at[0], seqk(1))
            self.part2 = compute(flip(g, 2, 2))
            self.in1 = push(compute(flip(g, 1, 2)), first.at[1], seqk(1))

        def far(self):
            arrived([self.in3])
            self.part2[...] = (self.part2[...].astype(f32) + self.first[0].astype(f32)).astype(bf16)
            self.out = push(self.part2, self.second, seqk(2))
            self.part0 = self.compute(g)

        def total(self):
            arrived([self.in1, self.out])
            return self.part0[...].astype(f32) + self.first[1].astype(f32) + self.second[...].astype(f32)

    m_w.gone()
    sent(ms.values())
    for i in range(3):
        keep[i, :, 0:384] = dot_tn(mrow[:, 256 * i : 256 * i + 256], dqkv[:, 0:384]).astype(bf16)

    def memory_part(b):
        mrow[block(b), :] = dot_nt(dqkv[block(b), 0:384], wM[...]).astype(bf16)
        return mrow.at[block(b)]

    m_rows = Rows(memory_part, rt1, rt2)
    m_rows.far()
    for i in range(3):
        wM[256 * i : 256 * i + 256, :] = keep[i, :, 0:384]

    g_z.step2()
    m_rs = Reduce(part192(wM), mdp)

    for h in range(3):
        acc[h] = jnp.zeros((1536, 128), f32)
        tbias[h] = jnp.zeros((256, 768), f32)

    def self_back(k):
        b = flip(g, k, 2)
        if k:
            arrived([s_in[k]])
        dos = unpack(srecv, b)
        for h in range(3):
            p = p_self[h, b]
            do = pad64(dos[h])
            dp = dot_nt(do, vh[h, window(b), :])
            pf = p.astype(f32)
            ds = pf * (dp - jnp.sum(dp * pf, axis=-1, keepdims=True))
            tbias[h] += ds
            ds = ds.astype(bf16)
            dqkv[block(b), 64 * h : 64 * h + 64] = (dot(ds, kh[h, window(b), :])[:, :64] * SCALE).astype(bf16)
            acc[h, window(b), :] += dot_tn(ds, pad64(qh[h, block(b), :][:, :64])) + dot_tn(p, above64(dos[h]))

    self_back(0)
    b_rs[1] = chip_square(1)
    b_rs[0] = chip_square(0)
    n_rs.end()
    n_z.step1()
    g_z.step3()
    self_back(2)
    m_rs.middle()
    b_rs[2].middle()
    u_z.step2()
    self_back(3)
    g_z.step4()

    total = m_rows.total()
    out_recv([out.at[0], out.at[1]])
    out_sent()
    outb[...] = total.astype(bf16)
    mem_recv, mem_sent = moved([outb.at[pl.ds(0, 128)], outb.at[pl.ds(128, 128)]], [gmem.at[r]] * 2, back, r)

    self_back(1)
    u_z.step3()

    def keep_self(i, carry):
        rows, lower = block(i), pl.ds(pl.multiple_of(i * 256 + 512, 256), 256)
        for h in range(3):
            dqkv[rows, 192 + 64 * h : 256 + 64 * h] = acc[h, lower, :][:, :64].astype(bf16)
            dqkv[rows, 384 + 64 * h : 448 + 64 * h] = acc[h, lower, :][:, 64:].astype(bf16)
        return carry

    lax.fori_loop(0, 4, keep_self, 0)
    xown[...] = xrow[block(g), :].astype(f32)
    sent(xs.values())

    def self_part(b):
        xrow[block(b), :] = dot_nt(dqkv[block(b), :], wQ[...]).astype(bf16)
        return xrow.at[block(b)]

    x_rows = Rows(self_part, rs1, rs2)
    x_rows.far()
    m_rs.end()
    m_far = push(wM.at[mine], mfar, seqk(4))
    b_rs[1].middle()
    b_rs[0].middle()
    n_z.step2()
    q_w.gone()

    def grad_qkv(n, carry):
        cols = pl.ds(pl.multiple_of(n * 128, 128), 128)
        wQ[cols, :] = dot_tn(h1[:, cols], dqkv[...]).astype(bf16)
        return carry

    lax.fori_loop(0, 6, grad_qkv, 0)
    q_rs = Reduce(part192(wQ), qdp)

    b_rs[2].end()
    b_z[2].step1()

    for h in range(3):
        wide = jnp.concatenate([jnp.zeros((256, 256), f32), tbias[h]], axis=1)
        rows = lax.broadcasted_iota(jnp.int32, (256, 1024), 0)
        for i in range(8):
            bit = lax.rem(lax.div(rows, 1 << i), 2) == 1
            wide = jnp.where(bit, pltpu.roll(wide, 1024 - (1 << i), 1), wide)
        lines[h : h + 1, :] = jnp.sum(wide, axis=0, keepdims=True)
    val = lines[...]
    top = val.astype(bf16)
    rest = val - top.astype(f32)
    mid = rest.astype(bf16)
    last = (rest - mid.astype(f32)).astype(bf16)
    by_bucket = dot_nt(top, hot[...]) + dot_nt(mid, hot[...]) + dot_nt(last, hot[...])
    row32 = lax.broadcasted_iota(jnp.int32, (32, 128), 0)
    spot = jnp.zeros((32, 128), f32)
    for h in range(3):
        spot = jnp.where(row32 == 3 * g + h, jnp.broadcast_to(by_bucket[h : h + 1, :], (32, 128)), spot)
    gsm[...] += spot

    for i in (1, 0):
        b_rs[i].end()
        b_z[i].step1()
    u_z.step4()
    g_z.step5()
    n_z.step3()
    q_rs.middle()

    b_z[2].step2()
    q_rs.end()
    q_far = push(wQ.at[mine], qfar, seqk(4))

    dv, dgain1 = norm_back(xown[...], gains[12:13, :], x_rows.total())
    put_gain(0, dgain1)
    sm_dp = [push(gsm, sm1.at[k - 1], dpk(k)) for k in (1, 2, 3)]
    mem_recv([gmem.at[0], gmem.at[1]])
    mem_sent()
    outb[...] = (grad[...] + dv).astype(bf16)
    gin_recv, gin_sent = moved([outb.at[pl.ds(0, 128)], outb.at[pl.ds(128, 128)]], [gin.at[r]] * 2, back, r)

    def far_sum(ref, copy, got, place):
        arrived([copy])
        sent([copy])
        ref[mine, :] = (ref[mine, :].astype(f32) + got[...].astype(f32)).astype(bf16)
        here_too = local(ref.at[mine], place.at[g])
        return here_too, push(ref.at[mine], place.at[g], seqk(2)), push(ref.at[mine], place.at[g], seqk(1))

    m_own, m_pair, m_s1 = far_sum(wM, m_far, mfar, o_m)
    n_z.step4()
    u_z.step5()
    b_z[1].step2()
    b_z[0].step2()
    b_z[2].step3()
    arrived(sm_dp)
    sent(sm_dp)
    gsm[...] = gsm[...] + sm1[0] + sm1[1] + sm1[2]
    sm_seq = [push(gsm, sm2.at[k - 1], seqk(k)) for k in range(1, 8)]
    q_own, q_pair, q_s1 = far_sum(wQ, q_far, qfar, o_q)
    b_z[1].step3()
    b_z[0].step3()
    b_z[2].step4()
    n_z.step5()
    b_z[1].step4()
    b_z[0].step4()
    arrived(sm_seq)
    val = gsm[...]
    for k in range(7):
        val = val + sm2[k]
    o_small[...] = val
    other = flip(g, 2, 2)
    arrived([m_pair])
    m_s2 = push(o_m.at[other], o_m.at[other], seqk(1))
    arrived([q_pair])
    q_s2 = push(o_q.at[other], o_q.at[other], seqk(1))
    for i in (2, 1, 0):
        b_z[i].step5()
    gin_recv([gin.at[0], gin.at[1]])
    gin_sent()
    cot_sent()
    m_own.wait()
    q_own.wait()
    arrived([m_s1, q_s1, m_s2, q_s2])
    for chain in (g_z, u_z, n_z, *b_z):
        arrived([chain.copy])
    for cp in list(flying):
        cp.wait_send()


def scratch():
    def vm(kind, *shape):
        return pltpu.VMEM(shape, kind)

    return dict(
        xrow=vm(bf16, 1024, 768),
        mrow=vm(bf16, 1024, 768),
        h1=vm(bf16, 1024, 768),
        wQ=vm(bf16, 768, 576),
        wM=vm(bf16, 768, 384),
        W3=vm(bf16, 3, 768, 768),
        wgu=vm(bf16, 768, 2048),
        wd=vm(bf16, 1024, 768),
        sm=vm(bf16, 4, 16, 768),
        sg=vm(bf16, 8, 16, 128),
        gains=vm(f32, 16, 768),
        lines=vm(f32, 16, 1024),
        hot=vm(bf16, 128, 1024),
        tbias=vm(f32, 3, 256, 768),
        qh=vm(bf16, 3, 1024, 128),
        kh=vm(bf16, 3, 1536, 128),
        vh=vm(bf16, 3, 1536, 128),
        mkv=vm(bf16, 3, 1024, 128),
        p_self=vm(bf16, 3, 4, 256, 768),
        p_cross=vm(bf16, 3, 4, 256, 1024),
        opack=vm(bf16, 4, 384, 128),
        arecv=vm(bf16, 4, 384, 128),
        attn=vm(bf16, 256, 768),
        qpack=vm(bf16, 4, 384, 128),
        qrecv=vm(bf16, 4, 384, 128),
        crecv=vm(bf16, 4, 384, 128),
        cattn=vm(bf16, 256, 768),
        after_self=vm(f32, 256, 768),
        after_cross=vm(f32, 256, 768),
        h2=vm(bf16, 256, 768),
        h3=vm(bf16, 2, 256, 768),
        prod=vm(bf16, 2, 256, 1024),
        dgu=vm(bf16, 2, 256, 2048),
        cotb=vm(bf16, 2, 256, 768),
        frecv=vm(bf16, 256, 768),
        hrecv=vm(bf16, 256, 768),
        outb=vm(bf16, 256, 768),
        grad=vm(f32, 256, 768),
        low=vm(bf16, 2, 256, 768),
        dcq=vm(bf16, 256, 768),
        acc=vm(f32, 3, 1536, 128),
        dqkv=vm(bf16, 1024, 576),
        rs1=vm(bf16, 2, 256, 768),
        rs2=vm(bf16, 256, 768),
        rt1=vm(bf16, 2, 256, 768),
        rt2=vm(bf16, 256, 768),
        gur=vm(bf16, 2, 6, 96, 1024),
        dnr=vm(bf16, 6, 128, 768),
        bsib=vm(bf16, 3, 4, 96, 768),
        bdp=vm(bf16, 3, 6, 48, 768),
        qdp=vm(bf16, 6, 96, 576),
        mdp=vm(bf16, 6, 96, 384),
        zg1=vm(bf16, 2, 192, 1024),
        zg2=vm(bf16, 2, 96, 1024),
        zd1=vm(bf16, 256, 768),
        zd2=vm(bf16, 128, 768),
        zb1=vm(bf16, 3, 96, 768),
        zb2=vm(bf16, 3, 48, 768),
        qfar=vm(bf16, 192, 576),
        mfar=vm(bf16, 192, 384),
        gsm=vm(f32, 32, 128),
        sm1=vm(f32, 3, 32, 128),
        sm2=vm(f32, 7, 32, 128),
        sgown=vm(bf16, 2, 16, 128),
        ssem=pltpu.SemaphoreType.DMA((N_SEM,)),
        rsem=pltpu.SemaphoreType.DMA((N_SEM,)),
        lsem=pltpu.SemaphoreType.DMA((N_LOCAL,)),
    )


def finish_kernel(
    out, gin, gmem, o_gu, o_dn, o_b, o_q, o_m, o_small,
    y_out, y_gin, y_gmem, y_g1, y_qkv, y_ao, y_rel, y_g2, y_cq, y_kv, y_co, y_g3, y_gu, y_dn, rel_t,
):
    d = lax.axis_index("dp")
    y_out[...] = out[...]
    y_gin[...] = gin[...]
    y_gmem[...] = gmem[...]
    for half in range(2):
        for q in range(4):
            for c in range(2):
                at = 2048 * half + 512 * q + 256 * c
                y_gu[:, at : at + 256] = o_gu[c, :, 512 * q + 256 * half : 512 * q + 256 * half + 256].astype(f32)
    y_dn[...] = o_dn[...].astype(f32)
    for i, y in enumerate((y_ao, y_cq, y_co)):
        y[...] = o_b[i, 0].astype(f32)
    for p in range(5):
        y, src, i = (y_qkv, o_q, p) if p < 3 else (y_kv, o_m, p - 3)
        for t in range(2):
            two = [src[2 * t + j, :, 192 * i : 192 * i + 192].astype(f32) for j in range(2)]
            y[:, 768 * i + 384 * t : 768 * i + 384 * t + 384] = jnp.concatenate(two, axis=1)
    for i, y in enumerate((y_g1, y_g2, y_g3)):
        line = jnp.concatenate([o_small[12 + 6 * i + j : 13 + 6 * i + j, :] for j in range(6)], axis=1)
        val = line[:, 0:192]
        for q in range(1, 4):
            val = jnp.where(d == q, line[:, 192 * q : 192 * q + 192], val)
        y[...] = val
    rel_t[...] = jnp.transpose(o_small[...])
    y_rel[...] = rel_t[pl.ds(pl.multiple_of(8 * d, 8), 8), 0:12]


def per_device_kernel(
    inputs, memory, cotangent, segment_ids, row_live, buckets, gain_self, w_qkv, w_attn_out, rel_bias, gain_cross,
    c_query, c_keyval, c_out, gain_ff, w_gate_up, w_down,
):
    anywhere = pl.BlockSpec(memory_space=pl.ANY)
    vmem = pl.BlockSpec(memory_space=pltpu.VMEM)
    smem = pl.BlockSpec(memory_space=pltpu.SMEM)
    shapes = (
        ((2, 128, 768), bf16), ((2, 128, 768), bf16), ((2, 128, 768), bf16),
        ((2, 192, 2048), bf16), ((2, 256, 768), bf16), ((3, 2, 96, 768), bf16), ((4, 192, 576), bf16), ((4, 192, 384), bf16),
        ((32, 128), f32),
    )
    parts = pl.pallas_call(
        layer_kernel,
        out_shape=[jax.ShapeDtypeStruct(*sh) for sh in shapes],
        in_specs=[anywhere] * 3 + [vmem] * 6 + [smem] + [anywhere] * 7,
        out_specs=[anywhere] * 8 + [vmem],
        scratch_shapes=scratch(),
        compiler_params=pltpu.CompilerParams(collective_id=0, has_side_effects=True, vmem_limit_bytes=66500000),
        name="layer",
    )(
        inputs, memory, cotangent, segment_ids, gain_self, gain_cross, gain_ff, rel_bias,
        buckets.reshape(8, 128), row_live, w_qkv, c_keyval, w_attn_out, c_query, c_out, w_gate_up, w_down,
    )
    act = pl.BlockSpec((1, 64, 768), lambda i: (i // 2, i % 2, 0))
    whole = pl.BlockSpec((32, 128), lambda i: (0, 0))

    def rows(n, width):
        return pl.BlockSpec((n, width), lambda i: (i, 0)), jax.ShapeDtypeStruct((4 * n, width), f32)

    line = pl.BlockSpec((1, 192), lambda i: (0, 0)), jax.ShapeDtypeStruct((1, 192), f32)
    square = rows(48, 768)
    tokens = act, jax.ShapeDtypeStruct((2, 128, 768), bf16)
    down = (
        pl.BlockSpec((2, 64, 768), lambda i: (0, i, 0)),
        jax.ShapeDtypeStruct((2, 256, 768), f32),
    )
    table = pl.BlockSpec((8, 12), lambda i: (0, 0)), jax.ShapeDtypeStruct((8, 12), f32)
    outs = (
        tokens, tokens, tokens, line, rows(48, 2304), square, table, line, square, rows(48, 1536), square, line,
        rows(48, 4096), down,
    )
    res = pl.pallas_call(
        finish_kernel,
        grid=(4,),
        out_shape=[o for _, o in outs],
        in_specs=[
            act, act, act,
            pl.BlockSpec((2, 48, 2048), lambda i: (0, i, 0)),
            pl.BlockSpec((2, 64, 768), lambda i: (0, i, 0)),
            pl.BlockSpec((3, 1, 48, 768), lambda i: (0, i // 2, i % 2, 0)),
            pl.BlockSpec((4, 48, 576), lambda i: (0, i, 0)),
            pl.BlockSpec((4, 48, 384), lambda i: (0, i, 0)),
            whole,
        ],
        out_specs=[b for b, _ in outs],
        scratch_shapes=[pltpu.VMEM((128, 32), f32)],
        compiler_params=pltpu.CompilerParams(vmem_limit_bytes=66500000),
        name="finish",
    )(*parts)
    res = list(res)
    for i in (3, 7, 11):
        res[i] = res[i].reshape(192)
    res[13] = res[13].reshape(512, 768)
    return tuple(res)


def solution(mesh):
    in_specs = (
        P("dp", "seq", None),
        P("dp", "seq", None),
        P("dp", "seq", None),
        P("dp", "seq"),
        P("dp"),
        P(),
        P("dp"),
        P("dp", None),
        P("dp", None),
        P("dp", None),
        P("dp"),
        P("dp", None),
        P("dp", None),
        P("dp", None),
        P("dp"),
        P("dp", None),
        P("dp", None),
    )
    out_specs = (
        P("dp", "seq", None),
        P("dp", "seq", None),
        P("dp", "seq", None),
        P("dp"),
        P("dp", None),
        P("dp", None),
        P("dp", None),
        P("dp"),
        P("dp", None),
        P("dp", None),
        P("dp", None),
        P("dp"),
        P("dp", None),
        P("dp", None),
    )
    fits = dict(mesh.shape) == {"dp": 4, "seq": 8}
    return jax.shard_map(
        per_device_kernel if fits else per_device, mesh=mesh, in_specs=in_specs, out_specs=out_specs, check_vma=False
    )
```

```python
import jax
import jax.numpy as jnp
from jax import lax
from jax.experimental import pallas as pl
from jax.experimental.pallas import tpu as pltpu
from jax.sharding import PartitionSpec as P

D = 768
HEADS = 12
HEAD_DIM = 64
FF = 2048
BUCKETS = 32
LEN = 1024
MEM = 1024


epsilon = 1e-06
masked_score = -1000000000.0
highest = lax.Precision.HIGHEST


def rms_norm(values, gain):
    return values * lax.rsqrt(jnp.mean(values * values, axis=-1, keepdims=True) + epsilon) * gain


def matmul(left, right, form):
    return jnp.einsum(form, left, right, preferred_element_type=jnp.float32)


def softmax_parts(scores):
    top = jnp.max(scores, axis=-1, keepdims=True)
    expo = jnp.exp(scores - top)
    total = jnp.sum(expo, axis=-1, keepdims=True)
    return (expo / total, (top + jnp.log(total))[..., 0])


def score_grads(scores, lse_row, value_row, grad_row):
    probs = jnp.exp(scores - lse_row[..., None])
    grad_probs = matmul(grad_row, value_row, "qhd,khd->hqk")
    centre = jnp.sum(grad_probs * probs, axis=-1, keepdims=True)
    grad_scores = (probs * (grad_probs - centre)).astype(jnp.bfloat16)
    return (probs, grad_scores, centre[..., 0])


def one_hot_of(buckets):
    return (buckets[:, None] == jnp.arange(BUCKETS, dtype=jnp.int32)).astype(jnp.float32)


def skewed(by_dist, start, rows):
    table = jnp.concatenate([jnp.zeros((LEN - 1, HEADS), by_dist.dtype), by_dist], axis=0)
    window = lax.dynamic_slice_in_dim(table, start, rows + LEN - 1, axis=0)
    line = jnp.pad(window[::-1].T, ((0, 0), (0, 1)))
    width = rows + LEN
    flat = jnp.broadcast_to(line[:, None, :], (HEADS, rows, width)).reshape(HEADS, rows * width)
    return flat[:, : rows * (width - 1)].reshape(HEADS, rows, width - 1)[:, :, rows - 1 :]


def unskewed(block, start, rows):
    width = rows + LEN
    wide = jnp.pad(block, ((0, 0), (0, 0), (rows - 1, 0))).reshape(HEADS, rows * (width - 1))
    line = jnp.sum(jnp.pad(wide, ((0, 0), (0, rows))).reshape(HEADS, rows, width), axis=1)
    window = line[:, : width - 1][:, ::-1].T
    table = jnp.zeros((2 * LEN - 1, HEADS), block.dtype)
    return lax.dynamic_update_slice_in_dim(table, window, start, axis=0)[LEN - 1 :]


def per_device(
    inputs,
    memory,
    cotangent,
    segment_ids,
    row_live,
    buckets,
    gain_self,
    w_qkv,
    w_attn_out,
    rel_bias,
    gain_cross,
    c_query,
    c_keyval,
    c_out,
    gain_ff,
    w_gate_up,
    w_down,
):
    (
        g_self,
        qkv_full,
        out_full,
        bias_full,
        g_cross,
        cq_full,
        ckv_full,
        cout_full,
        g_ffn,
        gu_full,
        down_full,
    ) = (
        lax.all_gather(gain_self, "dp", axis=0, tiled=True),
        lax.all_gather(w_qkv, "dp", axis=0, tiled=True),
        lax.all_gather(w_attn_out, "dp", axis=0, tiled=True),
        lax.all_gather(rel_bias, "dp", axis=0, tiled=True),
        lax.all_gather(gain_cross, "dp", axis=0, tiled=True),
        lax.all_gather(c_query, "dp", axis=0, tiled=True),
        lax.all_gather(c_keyval, "dp", axis=0, tiled=True),
        lax.all_gather(c_out, "dp", axis=0, tiled=True),
        lax.all_gather(gain_ff, "dp", axis=0, tiled=True),
        lax.all_gather(w_gate_up, "dp", axis=0, tiled=True),
        lax.all_gather(w_down, "dp", axis=0, tiled=True),
    )
    num_rows, local_len, _ = inputs.shape
    seq_index = lax.axis_index("seq")
    scale = HEAD_DIM ** (-0.5)
    dense = inputs.astype(jnp.float32)
    live_rows = row_live.astype(jnp.float32)[:, None, None]
    normed_one = rms_norm(dense, g_self.astype(jnp.float32))
    hidden_one = normed_one.astype(jnp.bfloat16)
    qkv_local = matmul(hidden_one, qkv_full, "rcd,de->rce").astype(jnp.bfloat16)
    queries = qkv_local[..., :D]
    key_value = qkv_local[..., D:]
    seg_local = segment_ids.astype(jnp.bfloat16)
    key_all, seg_all = (
        lax.all_gather(key_value, "seq", axis=1, tiled=True),
        lax.all_gather(seg_local, "seq", axis=1, tiled=True),
    )
    positions = seq_index * local_len + jnp.arange(local_len, dtype=jnp.int32)
    offsets = positions[:, None] - jnp.arange(LEN, dtype=jnp.int32)[None, :]
    causal = offsets >= 0
    bucket_hot = one_hot_of(buckets)
    by_dist = jnp.einsum(
        "lb,bh->lh",
        bucket_hot,
        bias_full.astype(jnp.float32),
        precision=highest,
        preferred_element_type=jnp.float32,
    )
    bias_block = skewed(by_dist, seq_index * local_len, local_len)

    def self_scores(queries_h, key_row, seg_row, segk_row):
        raw = matmul(queries_h, key_row, "qhd,khd->hqk") * scale + bias_block
        allowed = causal & (seg_row[:, None] == segk_row[None, :])
        return jnp.where(allowed[None], raw, masked_score)

    def self_forward(items):
        query_row, kv_row, seg_row, segk_row = items
        key_row = kv_row[:, :D].reshape(LEN, HEADS, HEAD_DIM)
        value_row = kv_row[:, D:].reshape(LEN, HEADS, HEAD_DIM)
        scores = self_scores(
            query_row.reshape(local_len, HEADS, HEAD_DIM), key_row, seg_row, segk_row
        )
        probs, lse_row = softmax_parts(scores)
        mixed = matmul(probs.astype(jnp.bfloat16), value_row, "hqk,khd->qhd")
        return (mixed.reshape(local_len, D), lse_row)

    attn_self, lse_self = lax.map(self_forward, (queries, key_all, seg_local, seg_all))
    attn_low = attn_self.astype(jnp.bfloat16)
    branch_one = matmul(attn_low, out_full, "rcd,de->rce")
    after_self = dense + live_rows * branch_one
    normed_two = rms_norm(after_self, g_cross.astype(jnp.float32))
    hidden_two = normed_two.astype(jnp.bfloat16)
    cross_q = matmul(hidden_two, cq_full, "rcd,de->rce").astype(jnp.bfloat16)
    memory_kv = matmul(memory, ckv_full, "rmd,de->rme").astype(jnp.bfloat16)
    memory_all = lax.all_gather(memory_kv, "seq", axis=1, tiled=True)

    def cross_forward(items):
        query_row, kv_row = items
        key_row = kv_row[:, :D].reshape(MEM, HEADS, HEAD_DIM)
        value_row = kv_row[:, D:].reshape(MEM, HEADS, HEAD_DIM)
        scores = (
            matmul(query_row.reshape(local_len, HEADS, HEAD_DIM), key_row, "qhd,khd->hqk") * scale
        )
        probs, lse_row = softmax_parts(scores)
        mixed = matmul(probs.astype(jnp.bfloat16), value_row, "hqk,khd->qhd")
        return (mixed.reshape(local_len, D), lse_row)

    attn_cross, lse_cross = lax.map(cross_forward, (cross_q, memory_all))
    cross_low = attn_cross.astype(jnp.bfloat16)
    branch_two = matmul(cross_low, cout_full, "rcd,de->rce")
    after_cross = after_self + live_rows * branch_two
    normed_three = rms_norm(after_cross, g_ffn.astype(jnp.float32))
    hidden_three = normed_three.astype(jnp.bfloat16)
    gate_up = matmul(hidden_three, gu_full, "rcd,df->rcf")
    gate = gate_up[..., :FF]
    upward = gate_up[..., FF:]
    mixed_ff = (jax.nn.gelu(gate, approximate=True) * upward).astype(jnp.bfloat16)
    branch_three = matmul(mixed_ff, down_full, "rcf,fd->rcd")
    output = (after_cross + live_rows * branch_three).astype(jnp.bfloat16)
    (
        g_self,
        qkv_full,
        out_full,
        bias_full,
        g_cross,
        cq_full,
        ckv_full,
        cout_full,
        g_ffn,
        gu_full,
        down_full,
    ) = (
        lax.all_gather(gain_self, "dp", axis=0, tiled=True),
        lax.all_gather(w_qkv, "dp", axis=0, tiled=True),
        lax.all_gather(w_attn_out, "dp", axis=0, tiled=True),
        lax.all_gather(rel_bias, "dp", axis=0, tiled=True),
        lax.all_gather(gain_cross, "dp", axis=0, tiled=True),
        lax.all_gather(c_query, "dp", axis=0, tiled=True),
        lax.all_gather(c_keyval, "dp", axis=0, tiled=True),
        lax.all_gather(c_out, "dp", axis=0, tiled=True),
        lax.all_gather(gain_ff, "dp", axis=0, tiled=True),
        lax.all_gather(w_gate_up, "dp", axis=0, tiled=True),
        lax.all_gather(w_down, "dp", axis=0, tiled=True),
    )
    grad_out = cotangent.astype(jnp.float32)
    down_in = (live_rows * grad_out).astype(jnp.bfloat16)
    grad_down = matmul(mixed_ff, down_in, "rcf,rcd->fd")
    grad_mixed = matmul(down_in, down_full, "rcd,fd->rcf")
    _, gelu_pull = jax.vjp(
        lambda gate_in, up_in: jax.nn.gelu(gate_in, approximate=True) * up_in, gate, upward
    )
    grad_gate, grad_upward = gelu_pull(grad_mixed)
    grad_gu_low = jnp.concatenate([grad_gate, grad_upward], axis=-1).astype(jnp.bfloat16)
    grad_gate_up = matmul(hidden_three, grad_gu_low, "rcd,rcf->df")
    grad_normed_three = matmul(grad_gu_low, gu_full, "rcf,df->rcd")
    _, pull_three = jax.vjp(rms_norm, after_cross, g_ffn.astype(jnp.float32))
    part_three, grad_gain_ff = pull_three(grad_normed_three)
    grad_after_cross = grad_out + part_three
    cross_in = (live_rows * grad_after_cross).astype(jnp.bfloat16)
    grad_cout = matmul(cross_low, cross_in, "rcd,rce->de")
    grad_cross_attn = matmul(cross_in, cout_full, "rce,de->rcd").astype(jnp.bfloat16)

    def cross_backward(items):
        query_row, kv_row, lse_row, grad_row = items
        queries_h = query_row.reshape(local_len, HEADS, HEAD_DIM)
        grad_h = grad_row.reshape(local_len, HEADS, HEAD_DIM)
        key_row = kv_row[:, :D].reshape(MEM, HEADS, HEAD_DIM)
        value_row = kv_row[:, D:].reshape(MEM, HEADS, HEAD_DIM)
        scores = matmul(queries_h, key_row, "qhd,khd->hqk") * scale
        probs, grad_scores, centre = score_grads(scores, lse_row, value_row, grad_h)
        grad_query = matmul(grad_scores, key_row, "hqk,khd->qhd") * scale
        grad_key = matmul(grad_scores, queries_h, "hqk,qhd->khd") * scale
        grad_value = matmul(probs.astype(jnp.bfloat16), grad_h, "hqk,qhd->khd")
        kv_grads = jnp.concatenate([grad_key.reshape(MEM, D), grad_value.reshape(MEM, D)], axis=-1)
        return (grad_query.reshape(local_len, D), kv_grads, centre)

    grad_cq_rows, grad_memkv_full, _ = lax.map(
        cross_backward, (cross_q, memory_all, lse_cross, grad_cross_attn)
    )
    grad_memkv = lax.psum_scatter(
        grad_memkv_full.astype(jnp.bfloat16), "seq", scatter_dimension=1, tiled=True
    )
    grad_ckv = matmul(memory, grad_memkv, "rmd,rme->de")
    grad_memory = matmul(grad_memkv, ckv_full, "rme,de->rmd").astype(jnp.bfloat16)
    grad_cq_low = grad_cq_rows.astype(jnp.bfloat16)
    grad_cquery = matmul(hidden_two, grad_cq_low, "rcd,rce->de")
    grad_normed_two = matmul(grad_cq_low, cq_full, "rce,de->rcd")
    _, pull_two = jax.vjp(rms_norm, after_self, g_cross.astype(jnp.float32))
    part_two, grad_gain_cross = pull_two(grad_normed_two)
    grad_after_self = grad_after_cross + part_two
    self_in = (live_rows * grad_after_self).astype(jnp.bfloat16)
    grad_wout = matmul(attn_low, self_in, "rcd,rce->de")
    grad_self_attn = matmul(self_in, out_full, "rce,de->rcd").astype(jnp.bfloat16)

    def self_backward(carry, items):
        query_row, kv_row, seg_row, segk_row, lse_row, grad_row = items
        queries_h = query_row.reshape(local_len, HEADS, HEAD_DIM)
        grad_h = grad_row.reshape(local_len, HEADS, HEAD_DIM)
        key_row = kv_row[:, :D].reshape(LEN, HEADS, HEAD_DIM)
        value_row = kv_row[:, D:].reshape(LEN, HEADS, HEAD_DIM)
        scores = self_scores(queries_h, key_row, seg_row, segk_row)
        probs, grad_scores, centre = score_grads(scores, lse_row, value_row, grad_h)
        grad_query = matmul(grad_scores, key_row, "hqk,khd->qhd") * scale
        grad_key = matmul(grad_scores, queries_h, "hqk,qhd->khd") * scale
        grad_value = matmul(probs.astype(jnp.bfloat16), grad_h, "hqk,qhd->khd")
        kv_grads = jnp.concatenate([grad_key.reshape(LEN, D), grad_value.reshape(LEN, D)], axis=-1)
        return (
            carry + grad_scores.astype(jnp.float32),
            (grad_query.reshape(local_len, D), kv_grads, centre),
        )

    zero_block = jnp.zeros((HEADS, local_len, LEN), jnp.float32)
    score_total, (grad_q_rows, grad_kv_full, _) = lax.scan(
        self_backward, zero_block, (queries, key_all, seg_local, seg_all, lse_self, grad_self_attn)
    )
    grad_kv = lax.psum_scatter(
        grad_kv_full.astype(jnp.bfloat16), "seq", scatter_dimension=1, tiled=True
    )
    grad_bias = jnp.einsum(
        "lh,lb->bh",
        unskewed(score_total, seq_index * local_len, local_len),
        bucket_hot,
        precision=highest,
        preferred_element_type=jnp.float32,
    )
    grad_qkv_low = jnp.concatenate([grad_q_rows.astype(jnp.bfloat16), grad_kv], axis=-1)
    grad_wqkv = matmul(hidden_one, grad_qkv_low, "rcd,rce->de")
    grad_normed_one = matmul(grad_qkv_low, qkv_full, "rce,de->rcd")
    _, pull_one = jax.vjp(rms_norm, dense, g_self.astype(jnp.float32))
    part_one, grad_gain_self = pull_one(grad_normed_one)
    grad_inputs = (grad_after_self + part_one).astype(jnp.bfloat16)
    (
        own_gself,
        own_qkv,
        own_wout,
        own_bias,
        own_gcross,
        own_cquery,
        own_ckv,
        own_cout,
        own_gff,
        own_gateup,
        own_down,
    ) = (
        lax.psum_scatter(
            grad_gain_self.astype(jnp.bfloat16), "dp", scatter_dimension=0, tiled=True
        ).astype(jnp.float32),
        lax.psum_scatter(
            grad_wqkv.astype(jnp.bfloat16), "dp", scatter_dimension=0, tiled=True
        ).astype(jnp.float32),
        lax.psum_scatter(
            grad_wout.astype(jnp.bfloat16), "dp", scatter_dimension=0, tiled=True
        ).astype(jnp.float32),
        lax.psum_scatter(
            grad_bias.astype(jnp.bfloat16), "dp", scatter_dimension=0, tiled=True
        ).astype(jnp.float32),
        lax.psum_scatter(
            grad_gain_cross.astype(jnp.bfloat16), "dp", scatter_dimension=0, tiled=True
        ).astype(jnp.float32),
        lax.psum_scatter(
            grad_cquery.astype(jnp.bfloat16), "dp", scatter_dimension=0, tiled=True
        ).astype(jnp.float32),
        lax.psum_scatter(
            grad_ckv.astype(jnp.bfloat16), "dp", scatter_dimension=0, tiled=True
        ).astype(jnp.float32),
        lax.psum_scatter(
            grad_cout.astype(jnp.bfloat16), "dp", scatter_dimension=0, tiled=True
        ).astype(jnp.float32),
        lax.psum_scatter(
            grad_gain_ff.astype(jnp.bfloat16), "dp", scatter_dimension=0, tiled=True
        ).astype(jnp.float32),
        lax.psum_scatter(
            grad_gate_up.astype(jnp.bfloat16), "dp", scatter_dimension=0, tiled=True
        ).astype(jnp.float32),
        lax.psum_scatter(
            grad_down.astype(jnp.bfloat16), "dp", scatter_dimension=0, tiled=True
        ).astype(jnp.float32),
    )
    summed = (
        lax.psum(own_gself.astype(jnp.bfloat16), "seq").astype(jnp.float32),
        lax.psum(own_qkv.astype(jnp.bfloat16), "seq").astype(jnp.float32),
        lax.psum(own_wout.astype(jnp.bfloat16), "seq").astype(jnp.float32),
        lax.psum(own_bias.astype(jnp.bfloat16), "seq").astype(jnp.float32),
        lax.psum(own_gcross.astype(jnp.bfloat16), "seq").astype(jnp.float32),
        lax.psum(own_cquery.astype(jnp.bfloat16), "seq").astype(jnp.float32),
        lax.psum(own_ckv.astype(jnp.bfloat16), "seq").astype(jnp.float32),
        lax.psum(own_cout.astype(jnp.bfloat16), "seq").astype(jnp.float32),
        lax.psum(own_gff.astype(jnp.bfloat16), "seq").astype(jnp.float32),
        lax.psum(own_gateup.astype(jnp.bfloat16), "seq").astype(jnp.float32),
        lax.psum(own_down.astype(jnp.bfloat16), "seq").astype(jnp.float32),
    )
    return (
        output,
        grad_inputs,
        grad_memory,
        summed[0],
        summed[1],
        summed[2],
        summed[3],
        summed[4],
        summed[5],
        summed[6],
        summed[7],
        summed[8],
        summed[9],
        summed[10],
    )


f32, bf16 = jnp.float32, jnp.bfloat16
BIG = 1.0e9
SCALE = HEAD_DIM ** (-0.5)
MESH = pl.DeviceIdType.MESH
GELU_A, GELU_B = 0.7978845608028654, 0.044715
N_SEM, N_LOCAL = 232, 32


def flip(v, k, bits):
    for i in range(bits):
        if (k >> i) & 1:
            b = 1 << i
            v = v + b - 2 * b * lax.rem(lax.div(v, b), 2)
    return v


def dot(a, b):
    return lax.dot_general(a, b, (((1,), (0,)), ((), ())), preferred_element_type=f32)


def dot_nt(a, b):
    return lax.dot_general(a, b, (((1,), (1,)), ((), ())), preferred_element_type=f32)


def dot_tn(a, b):
    return lax.dot_general(a, b, (((0,), (0,)), ((), ())), preferred_element_type=f32)


def inv_rms(v):
    return lax.rsqrt(jnp.mean(v * v, axis=-1, keepdims=True) + epsilon)


def norm_back(v, gain, w):
    r = inv_rms(v)
    gw = gain * w
    mean = jnp.mean(gw * v, axis=-1, keepdims=True)
    return r * gw - v * (r * r * r * mean), jnp.sum(w * (v * r), axis=0, keepdims=True)


def gelu_parts(gate):
    sq = gate * gate
    th = jnp.tanh(GELU_A * gate * (1.0 + GELU_B * sq))
    half = 0.5 * (1.0 + th)
    slope = half + 0.5 * gate * (1.0 - th * th) * (GELU_A * (1.0 + 3.0 * GELU_B * sq))
    return gate * half, slope


def softmax(scores):
    e = jnp.exp(scores - jnp.max(scores, axis=-1, keepdims=True))
    return (e * (1.0 / jnp.sum(e, axis=-1, keepdims=True))).astype(bf16)


def pad64(v):
    return jnp.concatenate([v, jnp.zeros((v.shape[0], 64), v.dtype)], axis=1)


def above64(v):
    return jnp.concatenate([jnp.zeros((v.shape[0], 64), v.dtype), v], axis=1)


def pack(ref, slot, parts):
    ref[slot, 0:256, :] = jnp.concatenate([parts[0], parts[1]], axis=1)
    ref[slot, 256:384, :] = jnp.concatenate([parts[2][0:128], parts[2][128:256]], axis=1)


def unpack(ref, slot):
    two = ref[slot, 0:256, :]
    last = ref[slot, 256:384, :]
    return (two[:, :64], two[:, 64:], jnp.concatenate([last[:, :64], last[:, 64:]], axis=0))


def assemble(ref, dst):
    for t in range(2):
        a = unpack(ref, 2 * t) + unpack(ref, 2 * t + 1)
        for j in range(3):
            at = 384 * t + 128 * j
            dst[:, at : at + 128] = jnp.concatenate([a[2 * j], a[2 * j + 1]], axis=1)


def disperse(val, ref):
    for gg in range(4):
        pack(ref, gg, [val[:, 192 * gg + 64 * h : 192 * gg + 64 * h + 64] for h in range(3)])


def block(i):
    return pl.ds(pl.multiple_of(i * 256, 256), 256)


def layer_kernel(
    x, mem, cot, segs, gain1, gain2, gain3, rel, buck, live, w_in, w_kv, w_ao, w_cq, w_co, w_gu, w_dn,
    out, gin, gmem, o_gu, o_dn, o_b, o_q, o_m, o_small,
    *,
    xrow, mrow, h1, wQ, wM, W3, wgu, wd, sm, sg, gains, lines, hot, tbias, qh, kh, vh, mkv, p_self, p_cross,
    opack, arecv, attn, qpack, qrecv, crecv, cattn, after_self, after_cross, h2, h3, prod, dgu, cotb, frecv,
    hrecv, outb, grad, low, dcq, acc, dqkv, rs1, rs2, rt1, rt2, gur, dnr, bsib, bdp, qdp, mdp, zg1, zg2, zd1, zd2,
    zb1, zb2, qfar, mfar, gsm, sm1, sm2, sgown, ssem, rsem, lsem,
):
    drecv, dqrecv, srecv = arecv, crecv, qrecv
    fown, fpart, xown = tbias.at[2], outb, after_cross
    keep, hpart = p_cross.at[0], low.at[1]

    d, s = lax.axis_index("dp"), lax.axis_index("seq")
    c, z, g, r = lax.rem(s, 2), lax.div(s, 2), lax.rem(s, 4), lax.div(s, 4)
    used = {"remote": 0, "local": 0}
    flying = []

    def remote(src, dst, send_sem, recv_sem, dev):
        return pltpu.make_async_remote_copy(
            src_ref=src, dst_ref=dst, send_sem=ssem.at[send_sem], recv_sem=rsem.at[recv_sem],
            device_id=dev, device_id_type=MESH,
        )

    def fresh(n=1):
        used["remote"] += n
        assert used["remote"] <= N_SEM
        return used["remote"] - n

    def push(src, dst, dev):
        sem = fresh()
        copy = remote(src, dst, sem, sem, dev)
        copy.start()
        flying.append(copy)
        return copy

    def sent(copies):
        for copy in copies:
            copy.wait_send()
            flying[:] = [other for other in flying if other is not copy]

    def arrived(copies):
        for copy in copies:
            copy.wait_recv()

    def local(src, dst):
        copy = pltpu.make_async_copy(src, dst, lsem.at[used["local"]])
        used["local"] += 1
        copy.start()
        return copy

    def dpk(k):
        return (flip(d, k, 2), s)

    def seqk(k):
        return (d, flip(s, k, 3))

    class Gather:
        def __init__(self, whole, part):
            self.part = part
            own = whole(d)
            self.first = {k: push(own, own, dpk(k)) for k in (1, 2)}
            self.second = []

        def relay(self):
            for k, half in ((1, 0), (2, 1)):
                arrived([self.first[k]])
                src = self.part(flip(d, k, 2), half)
                self.second.append(push(src, src, dpk(3 - k)))

        def done(self):
            arrived(self.second)

        def gone(self):
            sent([*self.first.values(), *self.second])

    class Reduce:
        def __init__(self, part, got):
            self.part, self.got = part, got
            self.first = {}
            for k, half in ((1, 0), (2, 1)):
                for j, kk in ((0, k), (1, 3)):
                    copy = push(part(flip(d, kk, 2), half), got.at[3 * half + j], dpk(k))
                    self.first[half, j] = copy

        def middle(self):
            self.second = {}
            for k, half in ((1, 0), (2, 1)):
                arrived([self.first[half, 1]])
                ref = self.part(flip(d, 3 - k, 2), half)
                ref[...] = (ref[...].astype(f32) + self.got[3 * half + 1].astype(f32)).astype(bf16)
                self.second[half] = push(ref, self.got.at[3 * half + 2], dpk(3 - k))

        def end(self):
            for half in (0, 1):
                arrived([self.first[half, 0], self.second[half]])
                ref = self.part(d, half)
                total = ref[...].astype(f32) + self.got[3 * half].astype(f32) + self.got[3 * half + 2].astype(f32)
                ref[...] = total.astype(bf16)

    def moved(srcs, dsts, devs, slot):
        base = fresh(2)
        for i in range(2):
            away = remote(srcs[i], dsts[i], base + i, base + slot, (d, devs[i]))
            here = pltpu.make_async_copy(srcs[i], dsts[i], rsem.at[base + slot])

            @pl.when(devs[i] != s)
            def _():
                away.start()

            @pl.when(devs[i] == s)
            def _():
                here.start()

        def wait_recv(places):
            for i in range(2):
                pltpu.make_async_copy(places[i], places[i], rsem.at[base + i]).wait()

        def wait_send():
            for i in range(2):
                away = remote(srcs[i], dsts[i], base + i, base + slot, (d, devs[i]))

                @pl.when(devs[i] != s)
                def _():
                    away.wait_send()

        return wait_recv, wait_send

    mine, mine_d = pl.ds(pl.multiple_of(d * 192, 64), 192), block(d)
    here = pl.ds(s * 128, 128)
    own_x = local(x.at[r], xrow.at[here])
    stage = [p_self.at[0, i, 0:192] for i in range(4)] + [p_self.at[1, 0, 0:192]]
    own_in = [
        local(w.at[:, 768 * i : 768 * i + 768], stage[p])
        for p, (w, i) in enumerate(((w_in, 0), (w_in, 1), (w_in, 2), (w_kv, 0), (w_kv, 1)))
    ]
    own_W3 = [local(w, W3.at[i, mine]) for i, w in enumerate((w_ao, w_cq, w_co))]
    own_m = local(mem.at[r], mrow.at[here])
    own_gu = []
    for p in range(8):
        at = pl.multiple_of((p // 4) * FF + (p % 4) * 512 + c * 256, 256)
        own_gu.append(local(w_gu.at[:, pl.ds(at, 256)], wgu.at[mine, pl.ds(512 * (p % 4) + 256 * (p // 4), 256)]))
    own_dn = local(w_dn.at[block(c)], wd.at[mine_d])

    barrier = pltpu.get_barrier_semaphore()
    peers = [dpk(k) for k in (1, 2, 3)] + [seqk(k) for k in range(1, 8)]
    for p in peers:
        pl.semaphore_signal(barrier, inc=1, device_id=p, device_id_type=MESH)
    for i in range(2):
        sgown[i] = jnp.broadcast_to(segs[i : i + 1, :].astype(f32), (16, 128)).astype(bf16)
    sg[s] = sgown[r]
    at_bucket = lax.broadcasted_iota(jnp.int32, (8, 128), 1) == lax.broadcasted_iota(jnp.int32, (8, 128), 0) + 8 * d
    gains[...] = jnp.zeros((16, 768), f32)
    gains[0:12, 0:128] = dot_tn(rel[...].astype(f32), at_bucket.astype(f32))
    for q in range(4):

        @pl.when(d == q)
        def _():
            for i, gain in enumerate((gain1, gain2, gain3)):
                gains[12 + i : 13 + i, 192 * q : 192 * q + 192] = gain[...].astype(f32).reshape(1, 192)

    sm[d] = gains[...].astype(bf16)
    pl.semaphore_wait(barrier, len(peers))

    def row_of(k):
        return lax.div(flip(s, k, 3), 4)

    def spread(src, dst):
        return {m: push(src.at[row_of(2 * m)], dst.at[here], seqk(2 * m)) for m in (1, 2, 3)}

    def hand_on(dst, m):
        part = dst.at[pl.ds(flip(s, 2 * m, 3) * 128, 128)]
        return push(part, part, seqk(1))

    sm_in = [push(sm.at[d], sm.at[d], dpk(k)) for k in (1, 2, 3)]
    sg_in = [push(sgown.at[row_of(k)], sg.at[s], seqk(k)) for k in range(1, 8)]
    xd = spread(x, xrow)
    own_x.wait()
    xs = {0: hand_on(xrow, 0)}
    for cp in own_in:
        cp.wait()
    for q in range(4):

        @pl.when(g == q)
        def _():
            for p in range(5):
                dst, at = (wQ, 192 * p) if p < 3 else (wM, 192 * (p - 3))
                dst[mine, at : at + 192] = stage[p][:, 192 * q : 192 * q + 192]

    def part192(ref):
        return lambda dd, half: ref.at[pl.ds(pl.multiple_of(dd * 192 + 96 * half, 32), 96)]

    def whole192(ref):
        return lambda dd: ref.at[pl.ds(pl.multiple_of(dd * 192, 64), 192)]

    def part_dn(dd, half):
        return wd.at[pl.ds(pl.multiple_of(dd * 256 + 128 * half, 128), 128)]

    def part_b(i):
        return lambda dd, half: W3.at[i, pl.ds(pl.multiple_of(dd * 192 + c * 96 + 48 * half, 16), 48)]

    q_w = Gather(whole192(wQ), part192(wQ))

    def half_rows(dd, cc):
        return pl.ds(pl.multiple_of(dd * 192 + cc * 96, 32), 96)

    def send_W3(i):
        own_W3[i].wait()
        return Gather(lambda dd: W3.at[i, half_rows(dd, c)], part_b(i))

    def share_W3(i):
        W3_w[i].done()
        return [push(W3.at[i, rows], W3.at[i, rows], seqk(1)) for rows in (half_rows(flip(d, k, 2), c) for k in (1, 2, 3))]

    m_w = Gather(whole192(wM), part192(wM))
    W3_w = {0: send_W3(0)}
    W3_sib = {}

    arrived(sm_in)
    total = sm[0].astype(f32)
    for i in range(1, 4):
        total += sm[i].astype(f32)
    gains[...] = total
    near = jnp.concatenate([buck[i : i + 1, :] for i in range(4)], axis=1)
    by_dist = (lax.broadcasted_iota(jnp.int32, (128, 512), 0) == near).astype(bf16)
    turn = lax.broadcasted_iota(jnp.int32, (512, 1024), 0) + lax.broadcasted_iota(jnp.int32, (512, 1024), 1) == 768
    hot[...] = dot(by_dist, turn.astype(bf16)).astype(bf16)
    column = lax.broadcasted_iota(jnp.int32, (16, 1024), 1)
    line = dot(total[:, :128].astype(bf16), hot[...])
    lines[...] = jnp.where((column > 256) & (column < 769), line, masked_score)
    for h in range(3):
        row = jnp.broadcast_to(lines[pl.ds(3 * g + h, 1), :], (256, 1024))
        tbias[h] = pltpu.roll(row, 0, 1, stride=1, stride_axis=0)[:, 256:]

    def norm_block(m):
        rows = block(flip(z, m, 2))
        val = xrow[rows, :].astype(f32)
        h1[rows, :] = (val * inv_rms(val) * gains[12:13, :]).astype(bf16)

    arrived([xs[0]])
    norm_block(0)
    for m in (1, 2):
        arrived([xd[m]])
        xs[m] = hand_on(xrow, m)
        if m == 1:
            q_w.relay()
    arrived([xs[1]])
    norm_block(1)
    m_w.relay()
    W3_w[1] = send_W3(1)
    arrived([xd[3]])
    xs[3] = hand_on(xrow, 3)
    md = spread(mem, mrow)
    own_m.wait()
    ms = {0: hand_on(mrow, 0)}
    W3_w[0].relay()
    W3_w[2] = send_W3(2)
    arrived([xs[2]])
    norm_block(2)
    arrived([xs[3]])
    norm_block(3)

    arrived(sg_in)
    lane64 = lax.broadcasted_iota(jnp.int32, (128, 64), 1).astype(f32)
    inside = lane64 < 3.5
    for h in range(3):
        beyond = lax.broadcasted_iota(jnp.int32, (512, 128), 1) >= 64
        kh[h, 0:512, :] = jnp.where(beyond, -1.0, 0.0).astype(bf16)
        vh[h, 0:512, :] = jnp.zeros((512, 128), bf16)
    q_w.done()

    def project(i, carry):
        rows = block(i)
        res = dot(h1[rows, :], wQ[...]).astype(bf16)
        qa, ka = [], []
        for j in range(2):
            seg = sg[2 * i + j, 0:1, :].astype(f32)
            same = jnp.transpose(jnp.broadcast_to(seg, (128, 128)))[:, :64] == lane64
            qa.append(jnp.where(same, BIG, 0.0))
            ka.append(jnp.where(inside & jnp.logical_not(same), -1.0, 0.0))
        qa = jnp.concatenate(qa, axis=0).astype(bf16)
        ka = jnp.concatenate(ka, axis=0).astype(bf16)
        lower = pl.ds(pl.multiple_of(i * 256 + 512, 256), 256)
        for h in range(3):
            qv = (res[:, 64 * h : 64 * h + 64].astype(f32) * SCALE).astype(bf16)
            qh[h, rows, :] = jnp.concatenate([qv, qa], axis=1)
            kh[h, lower, :] = jnp.concatenate([res[:, 192 + 64 * h : 256 + 64 * h], ka], axis=1)
            vh[h, lower, :] = pad64(res[:, 384 + 64 * h : 448 + 64 * h])
        return carry

    lax.fori_loop(0, 4, project, 0)

    for cp in own_gu:
        cp.wait()
    gu_w = Gather(whole192(wgu), part192(wgu))

    def window(b):
        return pl.ds(pl.multiple_of(b * 256, 256), 768)

    a_in = []
    for k in (2, 3, 1, 0):
        b = flip(g, k, 2)
        parts = []
        for h in range(3):
            p = softmax(dot_nt(qh[h, block(b), :], kh[h, window(b), :]) + tbias[h])
            p_self[h, b] = p
            parts.append(dot(p, vh[h, window(b), :])[:, :64].astype(bf16))
        if k == 0:
            pack(arecv, g, parts)
        else:
            pack(opack, b, parts)
            a_in.append(push(opack.at[b], arecv.at[g], seqk(k)))
        if k == 2:
            W3_w[1].relay()
        if k == 1:
            W3_w[2].relay()

    own_dn.wait()
    dn_w = Gather(lambda dd: wd.at[block(dd)], part_dn)
    halves = [cotb.at[c, pl.ds(c * 128, 128)]] * 2
    dests = [4 * rr + z for rr in range(2)]
    cslot = lax.rem(z, 2)
    cot_recv, cot_sent = moved(
        [cot.at[0], cot.at[1]], [cotb.at[cslot, pl.ds(c * 128, 128)]] * 2, dests, c
    )
    W3_sib[0] = share_W3(0)
    W3_sib[1] = share_W3(1)

    arrived(a_in)
    assemble(arecv, attn)
    arrived(W3_sib[0])
    alive = live[r].astype(f32)
    res = xrow[block(g), :].astype(f32) + alive * dot(attn[...], W3[0])
    after_self[...] = res
    h2[...] = (res * inv_rms(res) * gains[13:14, :]).astype(bf16)
    arrived(W3_sib[1])
    disperse((dot(h2[...], W3[1]).astype(bf16).astype(f32) * SCALE).astype(bf16), qpack)
    q_in = {k: push(qpack.at[flip(g, k, 2)], qrecv.at[g], seqk(k)) for k in (2, 3, 1)}
    qrecv[g] = qpack[g]
    for m in (1, 2, 3):
        arrived([md[m]])
        ms[m] = hand_on(mrow, m)
    m_w.done()
    arrived(ms.values())

    def project_memory(i, carry):
        rows = block(i)
        res = dot(mrow[rows, :], wM[...]).astype(bf16)
        for h in range(3):
            mkv[h, rows, :] = jnp.concatenate(
                [res[:, 64 * h : 64 * h + 64], res[:, 192 + 64 * h : 256 + 64 * h]], axis=1
            )
        return carry

    lax.fori_loop(0, 4, project_memory, 0)
    gu_w.relay()
    cot_recv([cotb.at[c, pl.ds(0, 128)], cotb.at[c, pl.ds(128, 128)]])
    cot_sib = push(cotb.at[c], cotb.at[c], seqk(1))

    sent(a_in)
    c_in = []
    for k in (0, 1, 2, 3):
        b = flip(g, k, 2)
        if k:
            arrived([q_in[k]])
        qs = unpack(qrecv, b)
        parts = []
        for h in range(3):
            p = softmax(dot_nt(pad64(qs[h]), mkv[h]))
            p_cross[h, b] = p
            parts.append(dot(p, mkv[h])[:, 64:].astype(bf16))
        if k == 0:
            pack(crecv, g, parts)
        else:
            pack(opack, b, parts)
            c_in.append(push(opack.at[b], crecv.at[g], seqk(k)))
        if k == 0:
            W3_sib[2] = share_W3(2)
        if k == 1:
            dn_w.relay()
    arrived(W3_sib[2])
    arrived(c_in)
    assemble(crecv, cattn)
    res = after_self[...] + alive * dot(cattn[...], W3[2])
    after_cross[...] = res
    h3[c] = (res * inv_rms(res) * gains[14:15, :]).astype(bf16)
    h3_in = push(h3.at[c], h3.at[c], seqk(1))
    arrived([cot_sib])
    gu_w.done()
    dn_w.done()
    arrived([h3_in])

    gu_w.gone()
    dn_w.gone()
    tbias[0:2] = jnp.zeros((2, 256, 768), f32)

    def feed_forward(n, carry):
        cols = block(n)
        both = pl.ds(pl.multiple_of(n * 512, 512), 512)
        gates, ups = pl.ds(pl.multiple_of(n * 512, 512), 256), pl.ds(pl.multiple_of(n * 512 + 256, 256), 256)
        for t in range(2):
            gate, up = dot(h3[t], wgu[:, gates]), dot(h3[t], wgu[:, ups])
            act, slope = gelu_parts(gate)
            prod[t, :, cols] = (act * up).astype(bf16)
            gp = dot_nt((cotb[t].astype(f32) * alive).astype(bf16), wd[cols, :])
            dgu[t, :, gates] = (gp * up * slope).astype(bf16)
            dgu[t, :, ups] = (gp * act).astype(bf16)
            tbias[t] += dot_nt(dgu[t, :, both], wgu[:, both])
        for part in (gates, ups):
            wgu[:, part] = dot_tn(h3[...].reshape(512, 768), dgu[:, :, part].reshape(512, 256)).astype(bf16)
        return carry

    def grad_dn(n, carry):
        cols = block(n)
        down_in = (cotb[...].astype(f32) * alive).astype(bf16).reshape(512, 768)
        wd[cols, :] = dot_tn(prod[:, :, cols].reshape(512, 256), down_in).astype(bf16)
        return carry

    def part_gu(i):
        cols = pl.ds(1024 * i, 1024)
        return lambda dd, half: wgu.at[pl.ds(pl.multiple_of(dd * 192 + 96 * half, 32), 96), cols]

    far_side = lax.div(z, 2)
    outer = lax.rem(z, 2) == far_side
    inner = jnp.logical_not(outer)

    def push_if(src, dst, dev, sends, gets):
        copy = remote(src, dst, fresh(1), used["remote"] - 1, dev)

        class Copy:
            def wait_send(self):
                pl.when(sends)(copy.wait_send)

            def wait_recv(self):
                pl.when(gets)(copy.wait_recv)

        pl.when(sends)(copy.start)
        res = Copy()
        flying.append(res)
        return res

    class Around:
        def __init__(self, own, out, half, got):
            self.own, self.out, self.half, self.got = own, out, half, got

        def add(self, ref, got):
            @pl.when(inner)
            def _():
                ref[...] = (ref[...].astype(f32) + got[...].astype(f32)).astype(bf16)

        def step1(self):
            self.copy = push_if(self.own, self.got[0], seqk(2), outer, inner)

        def step2(self):
            arrived([self.copy])
            self.add(self.own, self.got[0])
            self.copy = push_if(self.half(self.own, 1 - far_side), self.got[1], seqk(6), inner, inner)

        def step3(self):
            arrived([self.copy])
            src, dst = self.half(self.own, far_side), self.half(self.out, far_side)
            self.add(src, self.got[1])
            self.copy = push_if(src, dst, seqk(6), inner, inner)
            self.back = [push_if(src, dst, seqk(2), inner, outer)]
            self.keep = pltpu.make_async_copy(src, dst, lsem.at[used["local"]])
            used["local"] += 1
            pl.when(inner)(self.keep.start)

        def step4(self):
            arrived([self.copy])
            pl.when(inner)(self.keep.wait)
            place = self.half(self.out, 1 - far_side)
            self.back.append(push_if(place, place, seqk(2), inner, outer))

        def step5(self):
            arrived(self.back)
            self.copy = push(self.out, self.out, seqk(1))

    def halves(n):
        return lambda ref, i: ref.at[pl.ds(pl.multiple_of(n * i, 16), n)]

    cols_gu = [pl.ds(1024 * i, 1024) for i in range(2)]
    g_z, u_z = [
        Around(wgu.at[mine, cols_gu[i]], o_gu.at[c, :, cols_gu[i]], halves(96), (zg1.at[i], zg2.at[i])) for i in range(2)
    ]
    n_z = Around(wd.at[mine_d], o_dn.at[c], halves(128), (zd1, zd2))
    b_z = [Around(W3.at[i, half_rows(d, c)], o_b.at[i, c], halves(48), (zb1.at[i], zb2.at[i])) for i in range(3)]

    lax.fori_loop(0, 2, feed_forward, 0)
    g_rs = Reduce(part_gu(0), gur.at[0])
    lax.fori_loop(2, 4, feed_forward, 0)
    u_rs = Reduce(part_gu(1), gur.at[1])
    hpart[...] = tbias[1 - c].astype(bf16)
    h_in = push(hpart, hrecv, seqk(1))
    fpart[...] = dot(prod[1 - c], wd[...]).astype(bf16)
    f_in = push(fpart, frecv, seqk(1))
    arrived([h_in])
    dv, dgain3 = norm_back(after_cross[...], gains[14:15, :], tbias[c] + hrecv[...].astype(f32))
    gsm[...] = jnp.zeros((32, 128), f32)

    def put_gain(i, val):
        for j in range(6):
            gsm[12 + 6 * i + j : 13 + 6 * i + j, :] = val[:, 128 * j : 128 * j + 128]

    put_gain(2, dgain3)
    grad[...] = cotb[c].astype(f32) + dv
    low[0] = (grad[...] * alive).astype(bf16)
    sent(c_in)
    sent(q_in.values())
    disperse(dot_nt(low[0], W3[2]).astype(bf16), opack)
    d_in = {k: push(opack.at[flip(g, k, 2)], drecv.at[g], seqk(k)) for k in (2, 3, 1)}
    drecv[g] = opack[g]
    fown[...] = dot(prod[c], wd[...])
    lax.fori_loop(0, 4, grad_dn, 0)
    g_rs.middle()

    arrived([f_in])
    sent([f_in])
    outb[...] = (after_cross[...] + alive * (fown[...] + frecv[...].astype(f32))).astype(bf16)
    back = [2 * g + j for j in range(2)]
    out_recv, out_sent = moved([outb.at[pl.ds(0, 128)], outb.at[pl.ds(128, 128)]], [out.at[r]] * 2, back, r)

    lefts = (attn, h2, cattn)
    rights = (low.at[1], dcq, low.at[0])
    b_sib = {}

    def grad_square(i):
        W3_w[i].gone()
        sent(W3_sib[i])
        W3[i] = dot_tn(lefts[i][...], rights[i][...]).astype(bf16)
        b_sib[i] = [push(W3.at[i, half_rows(q, 1 - c)], bsib.at[i, q], seqk(1)) for q in range(4)]

    def chip_square(i):
        arrived(b_sib[i])
        for q in range(4):
            rows = half_rows(q, c)
            W3[i, rows, :] = (W3[i, rows, :].astype(f32) + bsib[i, q].astype(f32)).astype(bf16)
        return Reduce(part_b(i), bdp.at[i])

    grad_square(2)

    for h in range(3):
        acc[h, 0:1024, :] = jnp.zeros((1024, 128), f32)
    dq_in = []

    def cross_back(k):
        b = flip(g, k, 2)
        if k:
            arrived([d_in[k]])
        dos, qs = unpack(drecv, b), unpack(qrecv, b)
        parts = []
        for h in range(3):
            p = p_cross[h, b]
            do = above64(dos[h])
            dp = dot_nt(do, mkv[h])
            pf = p.astype(f32)
            ds = (pf * (dp - jnp.sum(dp * pf, axis=-1, keepdims=True))).astype(bf16)
            parts.append((dot(ds, mkv[h])[:, :64] * SCALE).astype(bf16))
            acc[h, 0:1024, :] += dot_tn(ds, pad64(qs[h])) + dot_tn(p, do)
        if k == 0:
            pack(dqrecv, g, parts)
        else:
            pack(qpack, b, parts)
            dq_in.append(push(qpack.at[b], dqrecv.at[g], seqk(k)))

    cross_back(2)
    n_rs = Reduce(part_dn, dnr)
    cross_back(3)
    u_rs.middle()
    cross_back(1)
    g_rs.end()
    g_z.step1()
    cross_back(0)
    b_rs = {2: chip_square(2)}

    def keep_memory(i, carry):
        rows = block(i)
        vals = [acc[h, rows, :][:, :64] for h in range(3)] + [acc[h, rows, :][:, 64:] for h in range(3)]
        dqkv[rows, 0:384] = jnp.concatenate(vals, axis=1).astype(bf16)
        return carry

    lax.fori_loop(0, 4, keep_memory, 0)
    arrived(dq_in)
    assemble(dqrecv, dcq)
    dv, dgain2 = norm_back(after_self[...], gains[13:14, :], dot_nt(dcq[...], W3[1]))
    put_gain(1, dgain2)
    grad[...] += dv
    sent([h_in])
    low[1] = (grad[...] * alive).astype(bf16)
    sent(d_in.values())
    disperse(dot_nt(low[1], W3[0]).astype(bf16), opack)
    s_in = {k: push(opack.at[flip(g, k, 2)], srecv.at[g], seqk(k)) for k in (2, 3, 1)}
    srecv[g] = opack[g]

    grad_square(1)
    grad_square(0)

    class Rows:
        def __init__(self, compute, first, second):
            self.compute, self.first, self.second = compute, first, second
            self.in3 = push(compute(flip(g, 3, 2)), first.at[0], seqk(1))
            self.part2 = compute(flip(g, 2, 2))
            self.in1 = push(compute(flip(g, 1, 2)), first.at[1], seqk(1))

        def far(self):
            arrived([self.in3])
            self.part2[...] = (self.part2[...].astype(f32) + self.first[0].astype(f32)).astype(bf16)
            self.out = push(self.part2, self.second, seqk(2))
            self.part0 = self.compute(g)

        def total(self):
            arrived([self.in1, self.out])
            return self.part0[...].astype(f32) + self.first[1].astype(f32) + self.second[...].astype(f32)

    m_w.gone()
    sent(ms.values())
    for i in range(3):
        keep[i, :, 0:384] = dot_tn(mrow[:, 256 * i : 256 * i + 256], dqkv[:, 0:384]).astype(bf16)

    def memory_part(b):
        mrow[block(b), :] = dot_nt(dqkv[block(b), 0:384], wM[...]).astype(bf16)
        return mrow.at[block(b)]

    m_rows = Rows(memory_part, rt1, rt2)
    m_rows.far()
    for i in range(3):
        wM[256 * i : 256 * i + 256, :] = keep[i, :, 0:384]

    u_rs.end()
    u_z.step1()
    n_rs.middle()
    g_z.step2()
    m_rs = Reduce(part192(wM), mdp)

    for h in range(3):
        acc[h] = jnp.zeros((1536, 128), f32)
        tbias[h] = jnp.zeros((256, 768), f32)

    def self_back(k):
        b = flip(g, k, 2)
        if k:
            arrived([s_in[k]])
        dos = unpack(srecv, b)
        for h in range(3):
            p = p_self[h, b]
            do = pad64(dos[h])
            dp = dot_nt(do, vh[h, window(b), :])
            pf = p.astype(f32)
            ds = pf * (dp - jnp.sum(dp * pf, axis=-1, keepdims=True))
            tbias[h] += ds
            ds = ds.astype(bf16)
            dqkv[block(b), 64 * h : 64 * h + 64] = (dot(ds, kh[h, window(b), :])[:, :64] * SCALE).astype(bf16)
            acc[h, window(b), :] += dot_tn(ds, pad64(qh[h, block(b), :][:, :64])) + dot_tn(p, above64(dos[h]))

    self_back(0)
    b_rs[1] = chip_square(1)
    b_rs[0] = chip_square(0)
    n_rs.end()
    n_z.step1()
    g_z.step3()
    self_back(2)
    m_rs.middle()
    b_rs[2].middle()
    u_z.step2()
    self_back(3)
    g_z.step4()

    self_back(1)
    u_z.step3()

    total = m_rows.total()
    out_recv([out.at[0], out.at[1]])
    out_sent()
    outb[...] = total.astype(bf16)
    mem_recv, mem_sent = moved([outb.at[pl.ds(0, 128)], outb.at[pl.ds(128, 128)]], [gmem.at[r]] * 2, back, r)

    def keep_self(i, carry):
        rows, lower = block(i), pl.ds(pl.multiple_of(i * 256 + 512, 256), 256)
        for h in range(3):
            dqkv[rows, 192 + 64 * h : 256 + 64 * h] = acc[h, lower, :][:, :64].astype(bf16)
            dqkv[rows, 384 + 64 * h : 448 + 64 * h] = acc[h, lower, :][:, 64:].astype(bf16)
        return carry

    lax.fori_loop(0, 4, keep_self, 0)
    xown[...] = xrow[block(g), :].astype(f32)
    sent(xs.values())

    def self_part(b):
        xrow[block(b), :] = dot_nt(dqkv[block(b), :], wQ[...]).astype(bf16)
        return xrow.at[block(b)]

    x_rows = Rows(self_part, rs1, rs2)
    x_rows.far()
    m_rs.end()
    m_far = push(wM.at[mine], mfar, seqk(4))
    b_rs[1].middle()
    b_rs[0].middle()
    n_z.step2()
    q_w.gone()

    def grad_qkv(n, carry):
        cols = pl.ds(pl.multiple_of(n * 128, 128), 128)
        wQ[cols, :] = dot_tn(h1[:, cols], dqkv[...]).astype(bf16)
        return carry

    lax.fori_loop(0, 6, grad_qkv, 0)
    q_rs = Reduce(part192(wQ), qdp)

    b_rs[2].end()
    b_z[2].step1()

    for h in range(3):
        wide = jnp.concatenate([jnp.zeros((256, 256), f32), tbias[h]], axis=1)
        rows = lax.broadcasted_iota(jnp.int32, (256, 1024), 0)
        for i in range(8):
            bit = lax.rem(lax.div(rows, 1 << i), 2) == 1
            wide = jnp.where(bit, pltpu.roll(wide, 1024 - (1 << i), 1), wide)
        lines[h : h + 1, :] = jnp.sum(wide, axis=0, keepdims=True)
    val = lines[...]
    top = val.astype(bf16)
    rest = val - top.astype(f32)
    mid = rest.astype(bf16)
    last = (rest - mid.astype(f32)).astype(bf16)
    by_bucket = dot_nt(top, hot[...]) + dot_nt(mid, hot[...]) + dot_nt(last, hot[...])
    row32 = lax.broadcasted_iota(jnp.int32, (32, 128), 0)
    spot = jnp.zeros((32, 128), f32)
    for h in range(3):
        spot = jnp.where(row32 == 3 * g + h, jnp.broadcast_to(by_bucket[h : h + 1, :], (32, 128)), spot)
    gsm[...] += spot

    for i in (1, 0):
        b_rs[i].end()
        b_z[i].step1()
    u_z.step4()
    g_z.step5()
    n_z.step3()
    q_rs.middle()

    b_z[2].step2()
    q_rs.end()
    q_far = push(wQ.at[mine], qfar, seqk(4))

    dv, dgain1 = norm_back(xown[...], gains[12:13, :], x_rows.total())
    put_gain(0, dgain1)
    sm_dp = [push(gsm, sm1.at[k - 1], dpk(k)) for k in (1, 2, 3)]
    mem_recv([gmem.at[0], gmem.at[1]])
    mem_sent()
    outb[...] = (grad[...] + dv).astype(bf16)
    gin_recv, gin_sent = moved([outb.at[pl.ds(0, 128)], outb.at[pl.ds(128, 128)]], [gin.at[r]] * 2, back, r)

    def far_sum(ref, copy, got, place):
        arrived([copy])
        sent([copy])
        ref[mine, :] = (ref[mine, :].astype(f32) + got[...].astype(f32)).astype(bf16)
        here_too = local(ref.at[mine], place.at[g])
        return here_too, push(ref.at[mine], place.at[g], seqk(2)), push(ref.at[mine], place.at[g], seqk(1))

    m_own, m_pair, m_s1 = far_sum(wM, m_far, mfar, o_m)
    n_z.step4()
    u_z.step5()
    b_z[1].step2()
    b_z[0].step2()
    b_z[2].step3()
    arrived(sm_dp)
    sent(sm_dp)
    gsm[...] = gsm[...] + sm1[0] + sm1[1] + sm1[2]
    sm_seq = [push(gsm, sm2.at[k - 1], seqk(k)) for k in range(1, 8)]
    q_own, q_pair, q_s1 = far_sum(wQ, q_far, qfar, o_q)
    b_z[1].step3()
    b_z[0].step3()
    b_z[2].step4()
    n_z.step5()
    b_z[1].step4()
    b_z[0].step4()
    arrived(sm_seq)
    val = gsm[...]
    for k in range(7):
        val = val + sm2[k]
    o_small[...] = val
    other = flip(g, 2, 2)
    arrived([m_pair])
    m_s2 = push(o_m.at[other], o_m.at[other], seqk(1))
    arrived([q_pair])
    q_s2 = push(o_q.at[other], o_q.at[other], seqk(1))
    for i in (2, 1, 0):
        b_z[i].step5()
    gin_recv([gin.at[0], gin.at[1]])
    gin_sent()
    cot_sent()
    m_own.wait()
    q_own.wait()
    arrived([m_s1, q_s1, m_s2, q_s2])
    for chain in (g_z, u_z, n_z, *b_z):
        arrived([chain.copy])
    for cp in list(flying):
        cp.wait_send()


def scratch():
    def vm(kind, *shape):
        return pltpu.VMEM(shape, kind)

    return dict(
        xrow=vm(bf16, 1024, 768),
        mrow=vm(bf16, 1024, 768),
        h1=vm(bf16, 1024, 768),
        wQ=vm(bf16, 768, 576),
        wM=vm(bf16, 768, 384),
        W3=vm(bf16, 3, 768, 768),
        wgu=vm(bf16, 768, 2048),
        wd=vm(bf16, 1024, 768),
        sm=vm(bf16, 4, 16, 768),
        sg=vm(bf16, 8, 16, 128),
        gains=vm(f32, 16, 768),
        lines=vm(f32, 16, 1024),
        hot=vm(bf16, 128, 1024),
        tbias=vm(f32, 3, 256, 768),
        qh=vm(bf16, 3, 1024, 128),
        kh=vm(bf16, 3, 1536, 128),
        vh=vm(bf16, 3, 1536, 128),
        mkv=vm(bf16, 3, 1024, 128),
        p_self=vm(bf16, 3, 4, 256, 768),
        p_cross=vm(bf16, 3, 4, 256, 1024),
        opack=vm(bf16, 4, 384, 128),
        arecv=vm(bf16, 4, 384, 128),
        attn=vm(bf16, 256, 768),
        qpack=vm(bf16, 4, 384, 128),
        qrecv=vm(bf16, 4, 384, 128),
        crecv=vm(bf16, 4, 384, 128),
        cattn=vm(bf16, 256, 768),
        after_self=vm(f32, 256, 768),
        after_cross=vm(f32, 256, 768),
        h2=vm(bf16, 256, 768),
        h3=vm(bf16, 2, 256, 768),
        prod=vm(bf16, 2, 256, 1024),
        dgu=vm(bf16, 2, 256, 2048),
        cotb=vm(bf16, 2, 256, 768),
        frecv=vm(bf16, 256, 768),
        hrecv=vm(bf16, 256, 768),
        outb=vm(bf16, 256, 768),
        grad=vm(f32, 256, 768),
        low=vm(bf16, 2, 256, 768),
        dcq=vm(bf16, 256, 768),
        acc=vm(f32, 3, 1536, 128),
        dqkv=vm(bf16, 1024, 576),
        rs1=vm(bf16, 2, 256, 768),
        rs2=vm(bf16, 256, 768),
        rt1=vm(bf16, 2, 256, 768),
        rt2=vm(bf16, 256, 768),
        gur=vm(bf16, 2, 6, 96, 1024),
        dnr=vm(bf16, 6, 128, 768),
        bsib=vm(bf16, 3, 4, 96, 768),
        bdp=vm(bf16, 3, 6, 48, 768),
        qdp=vm(bf16, 6, 96, 576),
        mdp=vm(bf16, 6, 96, 384),
        zg1=vm(bf16, 2, 192, 1024),
        zg2=vm(bf16, 2, 96, 1024),
        zd1=vm(bf16, 256, 768),
        zd2=vm(bf16, 128, 768),
        zb1=vm(bf16, 3, 96, 768),
        zb2=vm(bf16, 3, 48, 768),
        qfar=vm(bf16, 192, 576),
        mfar=vm(bf16, 192, 384),
        gsm=vm(f32, 32, 128),
        sm1=vm(f32, 3, 32, 128),
        sm2=vm(f32, 7, 32, 128),
        sgown=vm(bf16, 2, 16, 128),
        ssem=pltpu.SemaphoreType.DMA((N_SEM,)),
        rsem=pltpu.SemaphoreType.DMA((N_SEM,)),
        lsem=pltpu.SemaphoreType.DMA((N_LOCAL,)),
    )


def finish_kernel(
    out, gin, gmem, o_gu, o_dn, o_b, o_q, o_m, o_small,
    y_out, y_gin, y_gmem, y_g1, y_qkv, y_ao, y_rel, y_g2, y_cq, y_kv, y_co, y_g3, y_gu, y_dn, rel_t,
):
    d = lax.axis_index("dp")
    y_out[...] = out[...]
    y_gin[...] = gin[...]
    y_gmem[...] = gmem[...]
    for half in range(2):
        for q in range(4):
            for c in range(2):
                at = 2048 * half + 512 * q + 256 * c
                y_gu[:, at : at + 256] = o_gu[c, :, 512 * q + 256 * half : 512 * q + 256 * half + 256].astype(f32)
    y_dn[...] = o_dn[...].astype(f32)
    for i, y in enumerate((y_ao, y_cq, y_co)):
        y[...] = o_b[i, 0].astype(f32)
    for p in range(5):
        y, src, i = (y_qkv, o_q, p) if p < 3 else (y_kv, o_m, p - 3)
        for t in range(2):
            two = [src[2 * t + j, :, 192 * i : 192 * i + 192].astype(f32) for j in range(2)]
            y[:, 768 * i + 384 * t : 768 * i + 384 * t + 384] = jnp.concatenate(two, axis=1)
    for i, y in enumerate((y_g1, y_g2, y_g3)):
        line = jnp.concatenate([o_small[12 + 6 * i + j : 13 + 6 * i + j, :] for j in range(6)], axis=1)
        val = line[:, 0:192]
        for q in range(1, 4):
            val = jnp.where(d == q, line[:, 192 * q : 192 * q + 192], val)
        y[...] = val
    rel_t[...] = jnp.transpose(o_small[...])
    y_rel[...] = rel_t[pl.ds(pl.multiple_of(8 * d, 8), 8), 0:12]


def per_device_kernel(
    inputs, memory, cotangent, segment_ids, row_live, buckets, gain_self, w_qkv, w_attn_out, rel_bias, gain_cross,
    c_query, c_keyval, c_out, gain_ff, w_gate_up, w_down,
):
    anywhere = pl.BlockSpec(memory_space=pl.ANY)
    vmem = pl.BlockSpec(memory_space=pltpu.VMEM)
    smem = pl.BlockSpec(memory_space=pltpu.SMEM)
    shapes = (
        ((2, 128, 768), bf16), ((2, 128, 768), bf16), ((2, 128, 768), bf16),
        ((2, 192, 2048), bf16), ((2, 256, 768), bf16), ((3, 2, 96, 768), bf16), ((4, 192, 576), bf16), ((4, 192, 384), bf16),
        ((32, 128), f32),
    )
    parts = pl.pallas_call(
        layer_kernel,
        out_shape=[jax.ShapeDtypeStruct(*sh) for sh in shapes],
        in_specs=[anywhere] * 3 + [vmem] * 6 + [smem] + [anywhere] * 7,
        out_specs=[anywhere] * 8 + [vmem],
        scratch_shapes=scratch(),
        compiler_params=pltpu.CompilerParams(collective_id=0, has_side_effects=True, vmem_limit_bytes=66500000),
        name="layer",
    )(
        inputs, memory, cotangent, segment_ids, gain_self, gain_cross, gain_ff, rel_bias,
        buckets.reshape(8, 128), row_live, w_qkv, c_keyval, w_attn_out, c_query, c_out, w_gate_up, w_down,
    )
    act = pl.BlockSpec((1, 64, 768), lambda i: (i // 2, i % 2, 0))
    whole = pl.BlockSpec((32, 128), lambda i: (0, 0))

    def rows(n, width):
        return pl.BlockSpec((n, width), lambda i: (i, 0)), jax.ShapeDtypeStruct((4 * n, width), f32)

    line = pl.BlockSpec((1, 192), lambda i: (0, 0)), jax.ShapeDtypeStruct((1, 192), f32)
    square = rows(48, 768)
    tokens = act, jax.ShapeDtypeStruct((2, 128, 768), bf16)
    down = (
        pl.BlockSpec((2, 64, 768), lambda i: (0, i, 0)),
        jax.ShapeDtypeStruct((2, 256, 768), f32),
    )
    table = pl.BlockSpec((8, 12), lambda i: (0, 0)), jax.ShapeDtypeStruct((8, 12), f32)
    outs = (
        tokens, tokens, tokens, line, rows(48, 2304), square, table, line, square, rows(48, 1536), square, line,
        rows(48, 4096), down,
    )
    res = pl.pallas_call(
        finish_kernel,
        grid=(4,),
        out_shape=[o for _, o in outs],
        in_specs=[
            act, act, act,
            pl.BlockSpec((2, 48, 2048), lambda i: (0, i, 0)),
            pl.BlockSpec((2, 64, 768), lambda i: (0, i, 0)),
            pl.BlockSpec((3, 1, 48, 768), lambda i: (0, i // 2, i % 2, 0)),
            pl.BlockSpec((4, 48, 576), lambda i: (0, i, 0)),
            pl.BlockSpec((4, 48, 384), lambda i: (0, i, 0)),
            whole,
        ],
        out_specs=[b for b, _ in outs],
        scratch_shapes=[pltpu.VMEM((128, 32), f32)],
        compiler_params=pltpu.CompilerParams(vmem_limit_bytes=66500000),
        name="finish",
    )(*parts)
    res = list(res)
    for i in (3, 7, 11):
        res[i] = res[i].reshape(192)
    res[13] = res[13].reshape(512, 768)
    return tuple(res)


def solution(mesh):
    in_specs = (
        P("dp", "seq", None),
        P("dp", "seq", None),
        P("dp", "seq", None),
        P("dp", "seq"),
        P("dp"),
        P(),
        P("dp"),
        P("dp", None),
        P("dp", None),
        P("dp", None),
        P("dp"),
        P("dp", None),
        P("dp", None),
        P("dp", None),
        P("dp"),
        P("dp", None),
        P("dp", None),
    )
    out_specs = (
        P("dp", "seq", None),
        P("dp", "seq", None),
        P("dp", "seq", None),
        P("dp"),
        P("dp", None),
        P("dp", None),
        P("dp", None),
        P("dp"),
        P("dp", None),
        P("dp", None),
        P("dp", None),
        P("dp"),
        P("dp", None),
        P("dp", None),
    )
    fits = dict(mesh.shape) == {"dp": 4, "seq": 8}
    return jax.shard_map(
        per_device_kernel if fits else per_device, mesh=mesh, in_specs=in_specs, out_specs=out_specs, check_vma=False
    )
```
